32 devices in a mesh: dp: 8 (over y, x, core), blk: 4 (over z).
Axes of the slice: x: 2, y: 2, z: 4, core: 2. Of those that a mesh axis runs over, the one named last changes fastest.
Arguments:
- patches: bfloat16 [3, 8, 2048, 768], P(None, 'dp', 'blk'), may hold values from -6 to 6
- keep_index: int32 [3, 8, 1024], P(None, 'dp', 'blk'), may hold values from 0 to 511, as said below
- shard_counts: int32 [3, 8, 4], P(None, 'dp'), may hold values from 192 to 256, as said below
- cotangent: bfloat16 [3, 8, 1024, 768], P(None, 'dp', 'blk'), may hold values from -6 to 6
- norm_gain: bfloat16 [768], P(('dp', 'blk')), may hold values from 0.25 to 1.75
- norm_shift: bfloat16 [768], P(('dp', 'blk')), may hold values from -1.75 to 1.75
- qkv_weight: bfloat16 [768, 2304], P(('dp', 'blk')), may hold values from -0.3125 to 0.3125
- query_bias: bfloat16 [768], P(('dp', 'blk')), may hold values from -1.75 to 1.75
- value_bias: bfloat16 [768], P(('dp', 'blk')), may hold values from -1.75 to 1.75
- out_weight: bfloat16 [768, 768], P(('dp', 'blk')), may hold values from -0.875 to 0.875
- out_bias: bfloat16 [768], P(('dp', 'blk')), may hold values from -1.75 to 1.75
- mlp_gain: bfloat16 [768], P(('dp', 'blk')), may hold values from 0.25 to 1.75
- mlp_shift: bfloat16 [768], P(('dp', 'blk')), may hold values from -1.75 to 1.75
- up_weight: bfloat16 [768, 3072], P(('dp', 'blk')), may hold values from -0.21875 to 0.21875
- up_bias: bfloat16 [3072], P(('dp', 'blk')), may hold values from -1.75 to 1.75
- down_weight: bfloat16 [3072, 768], P(('dp', 'blk')), may hold values from -0.109375 to 0.109375
- down_bias: bfloat16 [768], P(('dp', 'blk')), may hold values from -1.75 to 1.75
Outputs:
- activations: bfloat16 [3, 8, 1024, 768], P(None, 'dp', 'blk')
- patch_grad: float32 [3, 8, 2048, 768], P(None, 'dp', 'blk')
- ngain_grad: float32 [768], P(('dp', 'blk'))
- nshift_grad: float32 [768], P(('dp', 'blk'))
- qkv_grad: float32 [768, 2304], P(('dp', 'blk'))
- qbias_grad: float32 [768], P(('dp', 'blk'))
- vbias_grad: float32 [768], P(('dp', 'blk'))
- outw_grad: float32 [768, 768], P(('dp', 'blk'))
- obias_grad: float32 [768], P(('dp', 'blk'))
- mgain_grad: float32 [768], P(('dp', 'blk'))
- mshift_grad: float32 [768], P(('dp', 'blk'))
- upw_grad: float32 [768, 3072], P(('dp', 'blk'))
- ubias_grad: float32 [3072], P(('dp', 'blk'))
- downw_grad: float32 [3072, 768], P(('dp', 'blk'))
- dbias_grad: float32 [768], P(('dp', 'blk'))
The draws below stay inside these ranges and needn't reach their ends.
Inputs may be any that keep to these rules, and one draw needn't show every extreme that they name: `keep_index`: within each block of 256 entries (one image on one index of blk): distinct rows of that block's 512 patch rows, in ascending order; the first entry of the first block of every image is 0, the class token. `shard_counts`: every image has a block with exactly 256 live slots.
All inputs are finite; a program needn't handle non-finite values.
Results may differ from the reference program's by a relative error of at most 0.014.
The reference program's roundings to bfloat16 on the way count: a program that leaves them out, or rounds other values in their place, can miss the bound.
Values may be sent and summed in bfloat16 or wider, within the bound.
A program may use at most 256 MiB of HBM per device.

```python
import jax
import jax.numpy as jnp
from jax import lax

D = 768
HEADS = 12
HEAD = 64
FF = 3072
CAP = 256
MB = 3
PATCH = 512
IMAGES = 8
N_BLK = 4


def draw_keep_index(key, part):
    key = jax.random.fold_in(key, 7)
    noise = jax.random.randint(key, (MB, IMAGES, N_BLK, PATCH), 0, 4096)
    shard = jnp.arange(N_BLK, dtype=jnp.int32)[:, None]
    patch = jnp.arange(PATCH, dtype=jnp.int32)[None, :]
    ranked = noise * PATCH + patch
    forced = (shard == 0) & (patch == 0) | (shard == N_BLK - 1) & (patch == PATCH - 1)
    ranked = jnp.where(forced, -1 - patch, ranked)
    chosen = jnp.argsort(ranked, axis=-1)[..., :CAP]
    chosen = jnp.sort(chosen, axis=-1)
    return chosen.reshape(MB, IMAGES, N_BLK * CAP).astype(jnp.int32)


def draw_shard_counts(key, part):
    key = jax.random.fold_in(key, 13)
    first, second = jax.random.split(key)
    values = jax.random.randint(first, (MB, IMAGES, N_BLK), 3 * CAP // 4, CAP + 1)
    fullest = jax.random.randint(second, (MB, IMAGES, 1), 0, N_BLK)
    return jnp.where(jnp.arange(N_BLK) == fullest, CAP, values).astype(jnp.int32)


def shard_levels(key, shape, cuts, low, high):
    factor_of, own = 1.0, jax.random.fold_in(key, 6)
    for dim, parts in cuts:
        draws = jnp.exp(jax.random.uniform(jax.random.fold_in(own, dim), (parts,), jnp.float32, low / len(cuts), high / len(cuts)))
        factor_of = factor_of * jnp.repeat(draws, shape[dim] // parts).reshape([-1 if axis == dim else 1 for axis in range(len(shape))])
    return factor_of


def normal_values(key, dims, width, limit, cuts=(), kind=jnp.bfloat16):
    level = shard_levels(key, dims, cuts, -0.22, 0.18) if cuts else 1.0
    drawn = jax.random.normal(key, dims, jnp.float32) * width * level
    return jnp.minimum(jnp.maximum(drawn, -limit), limit).astype(kind)


def setup_inputs(seed: int = 0) -> dict:
    arg_keys = jax.random.split(jax.random.key(seed), 18)
    return {
        "patches": normal_values(arg_keys[0], (MB, IMAGES, N_BLK * PATCH, D), 1.0, 6.0, ((1, 8), (2, 4))),
        "keep_index": draw_keep_index(jax.random.fold_in(arg_keys[17], 71), 0),
        "shard_counts": draw_shard_counts(jax.random.fold_in(arg_keys[17], 71), 0),
        "cotangent": normal_values(arg_keys[3], (MB, IMAGES, N_BLK * CAP, D), 1.0, 6.0, ((1, 8), (2, 4))),
        "norm_gain": jnp.clip(1.0 + 0.15 * jax.random.normal(arg_keys[4], (D,), jnp.float32), 0.25, 1.75).astype(jnp.bfloat16),
        "norm_shift": normal_values(arg_keys[5], (D,), 0.3, 1.75, ((0, 32),)),
        "qkv_weight": normal_values(arg_keys[6], (D, 3 * D), (D // 2) ** -0.5, 0.3125, ((0, 32),)),
        "query_bias": normal_values(arg_keys[7], (D,), 0.3, 1.75, ((0, 32),)),
        "value_bias": normal_values(arg_keys[8], (D,), 0.3, 1.75, ((0, 32),)),
        "out_weight": normal_values(arg_keys[9], (D, D), (D // 16) ** -0.5, 0.875, ((0, 32),)),
        "out_bias": normal_values(arg_keys[10], (D,), 0.3, 1.75, ((0, 32),)),
        "mlp_gain": jnp.clip(1.0 + 0.15 * jax.random.normal(arg_keys[11], (D,), jnp.float32), 0.25, 1.75).astype(jnp.bfloat16),
        "mlp_shift": normal_values(arg_keys[12], (D,), 0.3, 1.75, ((0, 32),)),
        "up_weight": normal_values(arg_keys[13], (D, FF), D ** -0.5, 0.21875, ((0, 32),)),
        "up_bias": normal_values(arg_keys[14], (FF,), 0.3, 1.75, ((0, 32),)),
        "down_weight": normal_values(arg_keys[15], (FF, D), FF ** -0.5, 0.109375, ((0, 32),)),
        "down_bias": normal_values(arg_keys[16], (D,), 0.3, 1.75, ((0, 32),)),
    }


HIGHEST = lax.Precision.HIGHEST
SCALE = 0.125
EPSILON = 1e-06

@jax.custom_vjp
def low(v):
    return lax.optimization_barrier(v.astype(jnp.bfloat16)).astype(jnp.float32)

@jax.custom_vjp
def low_back(v):
    return v

def low_keep(v):
    return (low(v), None)

def low_pass(kept, grad):
    return (grad,)

def back_keep(v):
    return (v, None)

def back_low(kept, grad):
    return (low(grad),)
low.defvjp(low_keep, low_pass)
low_back.defvjp(back_keep, back_low)

def layer_norm(rows, gain, shift):
    center = lax.optimization_barrier(jnp.mean(rows, axis=-1, keepdims=True))
    centred = rows - center
    spread = lax.optimization_barrier(jnp.mean(centred * centred, axis=-1, keepdims=True))
    return centred * lax.rsqrt(spread + EPSILON) * gain + shift

def encoder_layer(params, rows, live):
    gain_one, shift_one, mix_weight, bias_query, bias_value, proj_weight, bias_proj, gain_two, shift_two, expand_weight, bias_expand, shrink_weight, bias_shrink = params
    length = rows.shape[0]
    normed = low(layer_norm(rows, gain_one, shift_one))
    mixed = jnp.dot(normed, mix_weight, precision=HIGHEST)
    query = low_back(low(mixed[:, :D] + bias_query)).reshape(length, HEADS, HEAD)
    keys = low_back(low(mixed[:, D:2 * D])).reshape(length, HEADS, HEAD)
    values = low_back(low(mixed[:, 2 * D:] + bias_value)).reshape(length, HEADS, HEAD)
    scores = low_back(jnp.einsum('qhd,khd->hqk', query, keys, precision=HIGHEST) * SCALE)
    scores = jnp.where(live[None, None, :], scores, -1e+30)
    attention = low(jax.nn.softmax(scores, axis=-1))
    attended = jnp.einsum('hqk,khd->qhd', attention, values, precision=HIGHEST).reshape(length, D)
    attended = low_back(low(attended))
    middle = rows + low_back(jnp.dot(attended, proj_weight, precision=HIGHEST) + bias_proj)
    normed_two = low(layer_norm(middle, gain_two, shift_two))
    hidden = low_back(jnp.dot(normed_two, expand_weight, precision=HIGHEST) + bias_expand)
    active = low(jax.nn.gelu(hidden, approximate=False))
    result = low_back(jnp.dot(active, shrink_weight, precision=HIGHEST) + bias_shrink)
    return (middle + result) * live.astype(jnp.float32)[:, None]

def reference(patches, keep_index, shard_counts, cotangent, norm_gain, norm_shift, qkv_weight, query_bias, value_bias, out_weight, out_bias, mlp_gain, mlp_shift, up_weight, up_bias, down_weight, down_bias):
    params = tuple((piece.astype(jnp.float32) for piece in (norm_gain, norm_shift, qkv_weight, query_bias, value_bias, out_weight, out_bias, mlp_gain, mlp_shift, up_weight, up_bias, down_weight, down_bias)))
    places = jnp.arange(N_BLK * CAP, dtype=jnp.int32)
    owner = places // CAP
    slots = places % CAP

    def one_image(totals, item):
        image_patches, keep, counts, outer = item
        where_rows = (keep + owner * PATCH).astype(jnp.int32)
        live = slots < counts[owner]

        def forward(layer_params, patch_rows):
            rows = jnp.take(patch_rows, where_rows, axis=0)
            return encoder_layer(layer_params, rows, live)
        output, pullback = jax.vjp(forward, params, image_patches.astype(jnp.float32))
        grad_params, grad_patches = pullback(outer.astype(jnp.float32))
        totals = jax.tree.map(jnp.add, totals, grad_params)
        return (totals, (output.astype(jnp.bfloat16), grad_patches))
    items = (patches.reshape(MB * IMAGES, N_BLK * PATCH, D), keep_index.reshape(MB * IMAGES, N_BLK * CAP), shard_counts.reshape(MB * IMAGES, N_BLK), cotangent.reshape(MB * IMAGES, N_BLK * CAP, D))
    zeros = tuple((jnp.zeros_like(piece) for piece in params))
    totals, (outputs, grad_patches) = lax.scan(one_image, zeros, items)
    activations = outputs.reshape(MB, IMAGES, N_BLK * CAP, D)
    patch_grad = grad_patches.reshape(MB, IMAGES, N_BLK * PATCH, D)
    return (activations, patch_grad, totals[0], totals[1], totals[2], totals[3], totals[4], totals[5], totals[6], totals[7], totals[8], totals[9], totals[10], totals[11], totals[12])
```

```python
import functools

import jax
import jax.numpy as jnp
from jax import lax
from jax.experimental import pallas as pl
from jax.experimental.pallas import tpu as pltpu
from jax.sharding import PartitionSpec as P

MESH = pl.DeviceIdType.MESH
ANY = pl.BlockSpec(memory_space=pl.ANY)
VMEM = pl.BlockSpec(memory_space=pltpu.VMEM)
SMEM = pl.BlockSpec(memory_space=pltpu.SMEM)
f32, bf16, i32 = jnp.float32, jnp.bfloat16, jnp.int32

EPSILON = 1e-06
LOG2E = 1.4426950408889634
NEG = -1e30


def nn(a, b):
    return lax.dot_general(a, b, (((1,), (0,)), ((), ())), preferred_element_type=f32)


def nt(a, b):
    return lax.dot_general(a, b, (((1,), (1,)), ((), ())), preferred_element_type=f32)


def tn(a, b):
    return lax.dot_general(a, b, (((0,), (0,)), ((), ())), preferred_element_type=f32)


def mult(x, k):
    return x if isinstance(x, int) else pl.multiple_of(x, k)


def normalise(v):
    centred = v - jnp.mean(v, axis=1, keepdims=True)
    inv = lax.rsqrt(jnp.mean(centred * centred, axis=1, keepdims=True) + EPSILON)
    return centred * inv, inv


def norm_back(e, n, inv, gain):
    f = e * gain
    return inv * (f - jnp.mean(f, axis=1, keepdims=True) - n * jnp.mean(f * n, axis=1, keepdims=True))


def col_sum(v):
    return jnp.sum(v, axis=0, keepdims=True)


V_NG, V_NS, V_QB, V_VB, V_OB, V_MG, V_MS, V_DB, V_UB = range(9)


def layer_kernel(cfg, names_in, names_out, names_scratch, *refs):
    R = dict(zip(names_in + names_out + names_scratch, refs, strict=True))
    aligned, dps = cfg["aligned"], cfg["dps"]
    T, W, F = cfg["tokens"], cfg["width"], cfg["ff"]
    KR = W // dps
    FR = F // dps
    HALF = W // 2
    dp, z = lax.axis_index("dp"), lax.axis_index("blk")
    c = lax.rem(dp, 2)
    base = dp - c
    h, e = lax.div(z, 2), lax.rem(z, 2)
    g = 2 * e + c
    other = base + 1 - c
    ss, rs = R["ss"], R["rs"]
    count = [0]

    def take(n=1):
        count[0] += n
        return count[0] - n

    def rcopy(src, dst, s, r, dev):
        return pltpu.make_async_remote_copy(
            src_ref=src, dst_ref=dst, send_sem=ss.at[s], recv_sem=rs.at[r], device_id=dev, device_id_type=MESH
        )

    def recv(dst, r, dev=None):
        rcopy(dst, dst, 0, r, (other, z) if dev is None else dev).wait_recv()

    bar = pltpu.get_barrier_semaphore()
    peers = []
    for k in range(1, 8):
        j = lax.rem(c * 4 + z + k, 8)
        peers.append((base + lax.div(j, 4), lax.rem(j, 4)))
    if aligned:
        dx = 2 - 4 * lax.rem(lax.div(dp, 2), 2)
        dy = 4 - 8 * lax.div(dp, 4)
        p1, p2, p3 = dp + (1 - c) * dx + c * dy, dp + c * dx + (1 - c) * dy, dp + dx + dy
        peers += [(p1, z), (p2, z)]
    for dev in peers:
        pl.semaphore_signal(bar, inc=1, device_id=dev, device_id_type=MESH)

    def owner(m):
        if m < 2:
            return lax.div(z, 2), 2 * c + m, lax.rem(z, 2)
        return lax.rem(z, 2), 2 * c + lax.div(z, 2), 2

    def home(s):
        if s < 2:
            return h, 2 * c + s
        return h, 2 * e + c

    def move_out(m, src, dst, sid, rid):
        tc, tz, slot = owner(m)
        own = jnp.logical_and(tc == c, tz == z)

        @pl.when(own)
        def _():
            pltpu.make_async_copy(src, dst.at[slot], rs.at[rid + slot]).start()

        @pl.when(jnp.logical_not(own))
        def _():
            rcopy(src, dst.at[slot], sid + m, rid + slot, (base + tc, tz)).start()

    def move_out_done(m, src, dst, sid, rid):
        tc, tz, slot = owner(m)
        own = jnp.logical_and(tc == c, tz == z)

        @pl.when(jnp.logical_not(own))
        def _():
            rcopy(src, dst.at[slot], sid + m, rid + slot, (base + tc, tz)).wait_send()

    def move_home(s, src, dst, sid, rid):
        tc, tz = home(s)
        m = e if s < 2 else 2
        own = jnp.logical_and(tc == c, tz == z)

        @pl.when(own)
        def _():
            pltpu.make_async_copy(src, dst.at[m], ss.at[sid + s]).start()

        @pl.when(jnp.logical_not(own))
        def _():
            rcopy(src, dst.at[m], sid + s, rid + m, (base + tc, tz)).start()

    def move_home_done(s, src, dst, sid, rid):
        tc, tz = home(s)
        m = e if s < 2 else 2
        own = jnp.logical_and(tc == c, tz == z)

        @pl.when(own)
        def _():
            pltpu.make_async_copy(src, dst.at[m], ss.at[sid + s]).wait()

        @pl.when(jnp.logical_not(own))
        def _():
            rcopy(src, dst.at[m], sid + s, rid + m, (base + tc, tz)).wait_send()

    def arrived_home(m, dst, rid):
        tc, tz, _ = owner(m)

        @pl.when(jnp.logical_not(jnp.logical_and(tc == c, tz == z)))
        def _():
            recv(dst.at[m], rid + m)

    arrays = [R["wq"], R["wo"], R["wu"], R["wd"]]
    Q_, O_, U_, D_ = 0, 1, 2, 3
    if aligned:
        zbuf, zrr, zrl = R["zbuf"], R["zrr"], R["zrl"]
        flat = cfg["flat"]
        CH = {"Q": (0, flat[1]), "O": (flat[1], flat[2]), "U": (flat[2], flat[3]), "D": (flat[3], flat[4]), "V": (flat[4], flat[5])}
        ZR = {k: take(3) - 1 for k in CH}
        ZL = {k: take(3) - 1 for k in CH}
        YR = {k: take(3) - 1 for k in "QOUD"}
        YL = {k: take(3) - 1 for k in "QOUD"}
        gathered = arrays + [R["vw"]]
        XY = [take(3) for _ in range(5)]
        CR = [take(4) for _ in range(5)]
        R1 = [take(4) for _ in range(4)]
        R2 = [take(3) for _ in range(4)]

        def z_send(key, k, done=False):
            r0, r1 = CH[key]
            rows = pl.ds(r0, r1 - r0)
            right = jnp.logical_and(z < 3, z - (k - 1) >= 0)
            left = jnp.logical_and(z > 0, z + (k - 1) <= 3)

            @pl.when(right)
            def _():
                ref = zbuf.at[z - (k - 1), rows]
                d = rcopy(ref, ref, ZR[key] + k, ZR[key] + k, (dp, z + 1))
                d.wait_send() if done else d.start()

            @pl.when(left)
            def _():
                ref = zbuf.at[z + (k - 1), rows]
                d = rcopy(ref, ref, ZL[key] + k, ZL[key] + k, (dp, z - 1))
                d.wait_send() if done else d.start()

        def z_wait(key, k):
            r0, r1 = CH[key]
            rows = pl.ds(r0, r1 - r0)

            @pl.when(z - k >= 0)
            def _():
                recv(zbuf.at[z - k, rows], ZR[key] + k)

            @pl.when(z + k <= 3)
            def _():
                recv(zbuf.at[z + k, rows], ZL[key] + k)

        def flatten(a, ref, slot, block=None):
            if a == D_:
                n, rows = W // 128, FR // 4
            elif a == 4:
                n, rows = 1, 16
            else:
                n, rows = ref.shape[-1] // 128, KR // 4
            for t in range(n):
                cols = slice(t * 128, (t + 1) * 128)
                piece = ref[:, cols] if block is None else ref[block, slot * rows : (slot + 1) * rows, cols]
                zbuf[slot, flat[a] + t * rows : flat[a] + (t + 1) * rows, :] = piece

        def unflatten(a, block):
            dst = gathered[a]
            if a == D_:
                n, rows = W // 128, FR // 4
            elif a == 4:
                n, rows = 1, 16
            else:
                n, rows = dst.shape[-1] // 128, KR // 4
            for s in range(4):
                for t in range(n):
                    dst[block, s * rows : (s + 1) * rows, t * 128 : (t + 1) * 128] = zbuf[s, flat[a] + t * rows : flat[a] + (t + 1) * rows, :]

        def ag_copies(a):
            ref = gathered[a]

            def core(i):
                block = (dp, p1, p2, p3)[i]
                return rcopy(ref.at[block], ref.at[block], CR[a] + i, CR[a] + i, (other, z))

            return {
                "p1": lambda: rcopy(ref.at[dp], ref.at[dp], XY[a], XY[a], (p1, z)),
                "p2": lambda: rcopy(ref.at[dp], ref.at[dp], XY[a] + 1, XY[a] + 1, (p2, z)),
                "fw": lambda: rcopy(ref.at[p1], ref.at[p1], XY[a] + 2, XY[a] + 2, (p2, z)),
                "c0": lambda: core(0),
                "c1": lambda: core(1),
                "c2": lambda: core(2),
                "c3": lambda: core(3),
            }

        def ag1(a):
            d = ag_copies(a)
            d["p1"]().start()
            d["p2"]().start()
            d["c0"]().start()

        def ag2(a):
            d = ag_copies(a)
            ref = gathered[a]
            recv(ref.at[p1], XY[a])
            d["fw"]().start()
            d["c1"]().start()
            recv(ref.at[p2], XY[a] + 1)
            d["c2"]().start()

        def ag3(a):
            d = ag_copies(a)
            recv(gathered[a].at[p3], XY[a] + 2)
            d["c3"]().start()

        def ag4(a):
            d = ag_copies(a)
            for i, block in enumerate((dp, p2, p1, p3)):
                recv(gathered[a].at[block + other - dp], CR[a] + i)
            for k in d.values():
                k().wait_send()

        def blk_of(i):
            return 2 * i + c

        bufs1 = [R["rb1" + n] for n in "qoud"]
        bufs2 = [R["rb2" + n] for n in "qoud"]

        def view(buf, a, i):
            r, w = arrays[a].shape[1:]
            return buf.at[i, pl.ds(0, r), pl.ds(0, w)]

        def rs_core(a, i):
            return rcopy(arrays[a].at[2 * i + 1 - c], view(bufs1[a], a, i), R1[a] + i, R1[a] + i, (other, z))

        def rs1(a):
            for i in range(4):
                rs_core(a, i).start()

        def addto(ref, block, parts):
            rows, width = ref.shape[1:]
            step = 96

            @pl.loop(0, rows // step)
            def _(q):
                r = pl.ds(mult(q * step, step), step)
                total = ref[block, r, :].astype(f32)
                for p, i in parts:
                    total = total + p[i, r, pl.ds(0, width)].astype(f32)
                ref[block, r, :] = total.astype(bf16)

        def rs_xy(a):
            ref = arrays[a]
            return {
                "diag": lambda: rcopy(ref.at[p3], view(bufs2[a], a, 0), R2[a], R2[a], (p2, z)),
                "p2": lambda: rcopy(ref.at[p2], view(bufs2[a], a, 1), R2[a] + 1, R2[a] + 1, (p2, z)),
                "p1": lambda: rcopy(ref.at[p1], view(bufs2[a], a, 2), R2[a] + 2, R2[a] + 2, (p1, z)),
            }

        def rs2(a):
            for i in range(4):
                recv(view(bufs1[a], a, i), R1[a] + i)
                addto(arrays[a], blk_of(i), [(bufs1[a], i)])
            d = rs_xy(a)
            d["diag"]().start()
            d["p2"]().start()

        def rs3(a):
            recv(view(bufs2[a], a, 0), R2[a])
            addto(arrays[a], p1, [(bufs2[a], 0)])
            rs_xy(a)["p1"]().start()

        def rs4(a):
            recv(view(bufs2[a], a, 1), R2[a] + 1)
            recv(view(bufs2[a], a, 2), R2[a] + 2)
            addto(arrays[a], dp, [(bufs2[a], 1), (bufs2[a], 2)])
            for s in range(4):
                flatten(a, arrays[a], s, dp)
            y_send("QOUD"[a], 1)

        def y_send(key, k, done=False):
            r0, r1 = CH[key]
            rows = pl.ds(r0, r1 - r0)
            to_right = z + 4 - k
            to_left = z - 4 + k

            @pl.when(jnp.logical_and(z < 3, to_right <= 3))
            def _():
                if k > 1 and not done:

                    @pl.when(z >= 1)
                    def _():
                        recv(zrr.at[k - 2, rows], YR[key] + k - 1)
                        zbuf[to_right, rows, :] = (zbuf[to_right, rows, :].astype(f32) + zrr[k - 2, rows, :].astype(f32)).astype(bf16)

                d = rcopy(zbuf.at[to_right, rows], zrr.at[k - 1, rows], YR[key] + k, YR[key] + k, (dp, z + 1))
                d.wait_send() if done else d.start()

            @pl.when(jnp.logical_and(z > 0, to_left >= 0))
            def _():
                if k > 1 and not done:

                    @pl.when(z <= 2)
                    def _():
                        recv(zrl.at[k - 2, rows], YL[key] + k - 1)
                        zbuf[to_left, rows, :] = (zbuf[to_left, rows, :].astype(f32) + zrl[k - 2, rows, :].astype(f32)).astype(bf16)

                d = rcopy(zbuf.at[to_left, rows], zrl.at[k - 1, rows], YL[key] + k, YL[key] + k, (dp, z - 1))
                d.wait_send() if done else d.start()

        def y_final(a, out):
            key = "QOUD"[a]
            r0, r1 = CH[key]
            rows = pl.ds(r0, r1 - r0)

            @pl.when(z >= 1)
            def _():
                recv(zrr.at[2, rows], YR[key] + 3)

            @pl.when(z <= 2)
            def _():
                recv(zrl.at[2, rows], YL[key] + 3)

            if a == D_:
                n, step = W // 128, FR // 4
            else:
                n, step = out.shape[-1] // 128, KR // 4
            for t in range(n):
                piece = slice(r0 + t * step, r0 + (t + 1) * step)
                total = zbuf[z, piece, :].astype(f32)
                total = total + jnp.where(z >= 1, zrr[2, piece, :].astype(f32), 0.0)
                total = total + jnp.where(z <= 2, zrl[2, piece, :].astype(f32), 0.0)
                out[:, t * 128 : (t + 1) * 128] = total
            for k in (1, 2, 3):
                y_send(key, k, done=True)
            for i in range(4):
                rs_core(a, i).wait_send()
            for d in rs_xy(a).values():
                d().wait_send()

        outs = [R["gq"], R["go"], R["gu"], R["gd"]]

    I_ROWS, I_CNT, I_COT, I_ACT, I_GR = (take(3) for _ in range(5))
    S_ROWS, S_CNT, S_COT, S_ACT, S_GR = (take(3) for _ in range(5))
    EX = {}
    for k in ("qkv", "att", "do", "dqkv"):
        EX[k] = (take(1), take(4), take(4))
    L0 = take(12)

    rows, cot, cnt, nbuf = R["rows"], R["cot"], R["cnt"], R["nbuf"]
    qkv, qkva, qkvb = R["qkv"], R["qkva"], R["qkvb"]
    atta, attb, att, fromb = R["atta"], R["attb"], R["att"], R["fromb"]
    doa, dob, mid, vt, vg = R["doa"], R["dob"], R["mid"], R["vt"], R["vg"]
    lse, grh, keep, act = R["lse"], R["grh"], R["keep"], R["act"]
    lane = lax.broadcasted_iota(i32, (1, 128), 1)

    if aligned:
        for a, name in enumerate(("sq", "so", "su", "sd", "sv")):
            flatten(a, R[name], z)
    for m in range(3):
        for b in range(4):
            R["cnth"][m, b : b + 1, :] = jnp.full((1, 128), R["counts"][m, b], i32).astype(f32).astype(bf16)
        R["cnth"][m, 4:, :] = jnp.zeros((12, 128), bf16)

    pl.semaphore_wait(bar, len(peers))
    if aligned:
        z_send("Q", 1)
        z_send("V", 1)

    def pick_rows(pbuf, psem):
        copies = [pltpu.make_async_copy(R["patches"].at[m], pbuf.at[m], psem.at[m]) for m in range(3)]
        for d in copies:
            d.start()
        for m in range(3):
            copies[m].wait()
            spread = (lax.broadcasted_iota(i32, (cfg["patch"], T), 0) == keep[m]).astype(f32).astype(bf16)
            att[0, m * T : (m + 1) * T, :] = tn(spread, pbuf[m]).astype(bf16)
            move_out(m, att.at[0, pl.ds(m * T, T)], rows, S_ROWS, I_ROWS)
            move_out(m, R["cnth"].at[m], cnt, S_CNT, I_CNT)

    pl.run_scoped(pick_rows, pltpu.VMEM((3, cfg["patch"], W), bf16), pltpu.SemaphoreType.DMA((3,)))
    if aligned:
        for k in (1, 2):
            for key in "QV":
                z_wait(key, k)
                z_send(key, k + 1)
        for key in "OUD":
            z_send(key, 1)
        for key in "QV":
            z_wait(key, 3)
        unflatten(Q_, dp)
        ag1(Q_)
        unflatten(4, dp)
        ag1(4)
    else:
        full = [pltpu.make_async_copy(R[n], arrays[i], rs.at[L0 + 8 + i]) for i, n in enumerate(("sq", "so", "su", "sd"))]
        for d in full:
            d.start()
    for m in range(3):
        move_out(m, R["cotangent"].at[m], cot, S_COT, I_COT)
    if aligned:
        ag2(Q_)
        ag2(4)
        for key in "OUD":
            z_wait(key, 1)
            z_send(key, 2)
        ag3(Q_)
        ag3(4)
        ag4(4)
        v = R["vw"][...].reshape(32 * 16, 128)
        to = lax.broadcasted_iota(i32, (128, W), 1)
        frm = lax.broadcasted_iota(i32, (128, W), 0)
        dev = lax.broadcasted_iota(i32, (512, W), 0) // 16
        col = lax.broadcasted_iota(i32, (512, W), 1)
        n1, n2 = W // 32, F // 32
        x1 = nn(v, (lax.rem(to, n1) == frm).astype(f32).astype(bf16))
        x1 = jnp.where(dev == col // n1, x1, 0.0)
        vt[0:16, :] = jnp.sum(x1.reshape(32, 16, W), axis=0)
        x2 = nn(v, (lax.rem(to, n2) == frm).astype(f32).astype(bf16))
        x2 = jnp.where(lax.rem(dev, W // n2) == col // n2, x2, 0.0)
        x2 = jnp.sum(x2.reshape(4, 8, 16, W), axis=1)
        for q in range(4):
            vt[V_UB + q : V_UB + q + 1, :] = x2[q, V_UB : V_UB + 1, :]
    else:
        vt[...] = R["sv"][...]

    def vec(i):
        return vt[i : i + 1, :]

    def normed_rows(s):
        n, _ = normalise(rows[s].astype(f32))
        nbuf[s] = (n * vec(V_NG) + vec(V_NS)).astype(bf16)

    for s in range(3):
        recv(rows.at[s], I_ROWS + s)
        recv(cnt.at[s], I_CNT + s)
        normed_rows(s)
    if aligned:
        ag4(Q_)
        for key in "OUD":
            z_wait(key, 2)
            z_send(key, 3)
    else:
        for d in full:
            d.wait()

    def wblock(ref, cols=None):
        v = ref[...] if cols is None else ref[:, :, cols]
        return v.reshape(-1, v.shape[-1])

    def project(s):
        for j in range(3):
            v = nn(nbuf[s], wblock(R["wq"], slice(j * W, (j + 1) * W)))
            if j == 0:
                v = v + vec(V_QB)
            if j == 2:
                v = v + vec(V_VB)
            qkv[j, pl.ds(mult(s * T, T), T), :] = v.astype(bf16)

    def dev_of(i):
        return (base + lax.rem(i, 2), 2 * h + lax.div(i, 2))

    def ds128(x, n):
        return pl.ds(mult(x, 128), n)

    def to_heads_a(kind, src, dst):
        i0 = EX[kind][0]
        full_ = [slice(None)] * (len(src.shape) - 2)
        sref = src.at[(*full_, pl.ds(0, 2 * T), ds128(HALF * (1 - c), HALF))]
        dref = dst.at[(*full_, ds128(2 * T * c, 2 * T))]
        return rcopy(sref, dref, i0, i0, (other, z))

    def to_heads_a_own(kind, src, dst, lid):
        full_ = [slice(None)] * (len(src.shape) - 2)
        sref = src.at[(*full_, pl.ds(0, 2 * T), ds128(HALF * c, HALF))]
        dref = dst.at[(*full_, ds128(2 * T * c, 2 * T))]
        return pltpu.make_async_copy(sref, dref, rs.at[lid])

    def to_heads_b(kind, src, dst, k):
        _, rid, sid = EX[kind]
        full_ = [slice(None)] * (len(src.shape) - 2)
        t = lax.rem(g + k, 4)
        sref = src.at[(*full_, pl.ds(2 * T, T), ds128(HALF * lax.div(t, 2) + 128 * lax.rem(t, 2), 256))]
        dref = dst.at[(*full_, ds128(T * g, T))]
        return rcopy(sref, dref, sid + k, rid + k, dev_of(t))

    def to_heads_b_own(kind, src, dst, lid):
        full_ = [slice(None)] * (len(src.shape) - 2)
        sref = src.at[(*full_, pl.ds(2 * T, T), ds128(HALF * e + 128 * c, 256))]
        dref = dst.at[(*full_, ds128(T * g, T))]
        return pltpu.make_async_copy(sref, dref, rs.at[lid])

    def from_heads_a(kind, src, dst):
        i0 = EX[kind][0]
        full_ = [slice(None)] * (len(src.shape) - 2)
        sref = src.at[(*full_, ds128(2 * T * (1 - c), 2 * T))]
        dref = dst.at[(*full_, pl.ds(0, 2 * T), ds128(HALF * c, HALF))]
        return rcopy(sref, dref, i0, i0, (other, z))

    def from_heads_a_own(kind, src, dst, lid):
        full_ = [slice(None)] * (len(src.shape) - 2)
        sref = src.at[(*full_, ds128(2 * T * c, 2 * T))]
        dref = dst.at[(*full_, pl.ds(0, 2 * T), ds128(HALF * c, HALF))]
        return pltpu.make_async_copy(sref, dref, rs.at[lid])

    def from_heads_b(kind, src, j0, k):
        _, rid, sid = EX[kind]
        t = lax.rem(g + k, 4)
        n = src.shape[0]
        sref = src.at[:, ds128(T * t, T)]
        dref = fromb.at[g, pl.ds(0, n)]
        return rcopy(sref, dref, sid + k, rid + k, dev_of(t))

    def from_heads_b_own(src, lid):
        n = src.shape[0]
        return pltpu.make_async_copy(src.at[:, ds128(T * g, T)], fromb.at[g, pl.ds(0, n)], rs.at[lid])

    def wait_a(kind, dst, heads):
        full_ = [slice(None)] * (len(dst.shape) - 2)
        if heads:
            dref = dst.at[(*full_, ds128(2 * T * (1 - c), 2 * T))]
        else:
            dref = dst.at[(*full_, pl.ds(0, 2 * T), ds128(HALF * (1 - c), HALF))]
        recv(dref, EX[kind][0])

    def wait_b_heads(kind, dst):
        full_ = [slice(None)] * (len(dst.shape) - 2)
        for k in (1, 2, 3):
            recv(dst.at[(*full_, ds128(T * lax.rem(g + 4 - k, 4), T))], EX[kind][1] + k)

    def wait_b_tokens(kind, n):
        for k in (1, 2, 3):
            recv(fromb.at[lax.rem(g + 4 - k, 4), pl.ds(0, n)], EX[kind][1] + k)

    def merge_b(dst, j, n_from):
        for q in range(2):
            lo, hi = fromb[2 * q, n_from], fromb[2 * q + 1, n_from]
            at = q * HALF
            dst[j, 2 * T : 3 * T, at : at + 128] = lo[:, 0:128]
            dst[j, 2 * T : 3 * T, at + 128 : at + 256] = jnp.where(lane < 64, lo[:, 128:256], hi[:, 0:128])
            dst[j, 2 * T : 3 * T, at + 256 : at + 384] = hi[:, 128:256]

    @pl.loop(0, 2)
    def _(s):
        project(s)

    for m in range(3):
        move_out_done(m, att.at[0, pl.ds(m * T, T)], rows, S_ROWS, I_ROWS)
    xa = to_heads_a("qkv", qkv, qkva)
    xa.start()
    la = to_heads_a_own("qkv", qkv, qkva, L0)
    la.start()
    project(2)
    xb = [to_heads_b("qkv", qkv, qkvb, k) for k in (1, 2, 3)]
    for d in xb:
        d.start()
    lb = to_heads_b_own("qkv", qkv, qkvb, L0 + 1)
    lb.start()

    def weights_ready(step):
        if not aligned:
            return
        if step == 0:
            for key in "OUD":
                z_wait(key, 3)
            for a in (O_, U_, D_):
                unflatten(a, dp)
                ag1(a)
        elif step == 1:
            for a in (O_, U_, D_):
                ag2(a)
        elif step == 2:
            for a in (O_, U_, D_):
                ag3(a)
        elif step == 3:
            for a in (O_, U_, D_):
                ag4(a)
            for key in CH:
                for k in (1, 2, 3):
                    z_send(key, k, done=True)

    def key_bias(slot):
        parts = []
        at = lax.broadcasted_iota(i32, (T, 128), 0).astype(f32)
        for b in range(4):
            limit = cnt[slot, b : b + 1, :].astype(f32)
            parts.append(jnp.where(at < limit, 0.0, NEG))
        return jnp.concatenate(parts, axis=0).astype(bf16)

    bias = R["bias"]
    bias[0] = key_bias(0)
    bias[1] = key_bias(2)
    QT = 256
    N = 4 * T

    def half(i, x):
        return jnp.where(lane // 64 == i, x, jnp.zeros_like(x))

    def key_side(k2, b, i):
        spot = 64 * (1 - i)
        return jnp.where(lane // 64 == i, k2, jnp.where(lane == spot, b, jnp.zeros_like(b)))

    def query_side(q2, i):
        spot = 64 * (1 - i)
        return jnp.where(lane // 64 == i, q2, jnp.where(lane == spot, 1.0, 0.0).astype(bf16))

    SC = 0.125 * LOG2E

    def attend(src, dst, col, bi, sel, lrow):
        cols = ds128(col, 128)
        k2 = src[1, :, cols]
        b = bias[bi]
        keys = [key_side(k2, b, i) for i in sel]

        @pl.loop(0, N // QT)
        def _(q):
            r = ds128(q * QT, QT)
            q2 = src[0, r, cols]
            v2 = src[2, :, cols]
            outs = []
            for n, i in enumerate(sel):
                s = nt(query_side(q2, i), keys[n])
                top = jnp.max(s, axis=1, keepdims=True) * SC
                p = jnp.exp2(s * SC - top)
                total = jnp.sum(p, axis=1, keepdims=True)
                outs.append(nn(p.astype(bf16), v2) / total)
                full_total = jnp.broadcast_to(top + jnp.log2(total), (QT, 128)).T
                lse[pl.ds(lrow + n, 1), r] = full_total[0:1, :]
            if len(sel) == 2:
                o = jnp.where(lane < 64, outs[0], outs[1])
            else:
                o = jnp.where(lane // 64 == sel[0], outs[0], 0.0)
            dst[0, r, cols] = o.astype(bf16)

    la.wait()
    wait_a("qkv", qkva, True)

    @pl.loop(0, 2)
    def _(t):
        attend(qkva, atta, t * 128, 0, (0, 1), 2 * t)

    weights_ready(0)
    attend(qkva, atta, 256, 0, (0, 1), 4)
    xatt = from_heads_a("att", atta, att)
    xatt.start()
    latt = from_heads_a_own("att", atta, att, L0 + 2)
    latt.start()
    lb.wait()
    wait_b_heads("qkv", qkvb)
    weights_ready(1)
    attend(qkvb, attb, c * 128, 1, (0, 1), 6)
    weights_ready(2)
    attend(qkvb, attb, (1 - c) * 128, 1, (c,), 8)
    xattb = [from_heads_b("att", attb, 0, k) for k in (1, 2, 3)]
    for d in xattb:
        d.start()
    lattb = from_heads_b_own(attb, L0 + 3)
    lattb.start()
    weights_ready(3)
    xa.wait_send()
    for d in xb:
        d.wait_send()
    latt.wait()
    wait_a("att", att, False)
    lattb.wait()
    wait_b_tokens("att", 1)
    merge_b(att, 0, 0)

    def slot_rows(s):
        return pl.ds(mult(s * T, T), T)

    for s in range(3):
        recv(cot.at[s], I_COT + s)

    def live_of(s):
        b = 2 * c + s if s < 2 else g
        at = lax.broadcasted_iota(i32, (T, 128), 0).astype(f32)
        pick = jnp.zeros((1, 128), f32)
        for i in range(4):
            pick = pick + jnp.where(b == i, cnt[s, i : i + 1, :].astype(f32), 0.0)
        return jnp.where(at < pick, 1.0, 0.0)[:, 0:1]

    for s in range(3):
        r = pl.ds(s * T, T)
        v = nn(att[0, r, :], wblock(R["wo"])) + vec(V_OB) + rows[s].astype(f32)
        mid[r, :] = v
        n, _ = normalise(v)
        nbuf[s] = (n * vec(V_MG) + vec(V_MS)).astype(bf16)
        o = live_of(s) * cot[s].astype(f32)
        cot[s] = o.astype(bf16)
        part = col_sum(o)
        if s == 0:
            vg[V_DB : V_DB + 1, :] = part
        else:
            vg[V_DB : V_DB + 1, :] += part

    FT = FR

    def feed(res, gn2, n2t, tile):
        act_s, gh_s = tile.at[0], tile.at[1]
        for s in range(3):
            n2t[:, s * T : (s + 1) * T] = nbuf[s].T
        res[...] = jnp.zeros_like(res)
        gn2[...] = jnp.zeros_like(gn2)
        outer = branch = cot
        ub = R["ub"]

        @pl.loop(0, dps)
        def _(j):
            cols = ds128(j * FT, FT)
            up = wblock(R["wu"], cols)
            down = R["wd"][j]
            ub_j = ub[pl.ds(j, 1), :]

            @pl.loop(0, 3, init_carry=jnp.zeros((1, FT), f32))
            def bias_part(s, carry):
                r = slot_rows(s)
                hid = nn(nbuf[s], up) + ub_j
                phi_c = 0.5 * (1.0 + lax.erf(hid * 0.7071067811865476))
                act_low = (hid * phi_c).astype(bf16)
                act_s[r, :] = act_low
                res[r, :] += nn(act_low, down)
                slope = phi_c + hid * jnp.exp2(hid * hid * (-0.5 * LOG2E)) * 0.3989422804014327
                gh = (nt(outer[s], down) * slope).astype(bf16)
                gh_s[r, :] = gh
                gn2[r, :] += nt(gh, up)
                return carry + col_sum(gh.astype(f32))

            ub[pl.ds(j, 1), :] = bias_part
            R["wd"][j] = tn(act_s[...], outer[...].reshape(3 * T, W)).astype(bf16)
            R["wu"][:, :, cols] = nn(n2t[...], gh_s[...]).astype(bf16).reshape(dps, KR, FT)

        for s in range(3):
            r = pl.ds(s * T, T)
            v = mid[r, :]
            y = live_of(s) * (v + res[r, :] + vec(V_DB))
            n2t[r, :] = y.astype(bf16)
            move_home(s, n2t.at[r], act, S_ACT, I_ACT)
            n, inv = normalise(v)
            e_ = gn2[r, :]
            gm = outer[s].astype(f32) + norm_back(e_, n, inv, vec(V_MG))
            mid[r, :] = gm
            low = gm.astype(bf16)
            branch[s] = low
            for i, part in ((V_MG, col_sum(e_ * n)), (V_MS, col_sum(e_)), (V_OB, col_sum(low.astype(f32)))):
                if s == 0:
                    vg[i : i + 1, :] = part
                else:
                    vg[i : i + 1, :] += part
        if aligned:
            rs1(D_)
            rs1(U_)
        for s in range(3):
            r = pl.ds(s * T, T)
            nbuf[s] = nt(branch[s], wblock(R["wo"])).astype(bf16)
        send_do()
        for q in range(2):
            piece = tn(att[0, :, q * HALF : (q + 1) * HALF], branch[...].reshape(3 * T, W)).astype(bf16)
            R["wo"][q * (dps // 2) : (q + 1) * (dps // 2)] = piece.reshape(dps // 2, KR, W)
        for s in range(3):
            move_home_done(s, n2t.at[pl.ds(s * T, T)], act, S_ACT, I_ACT)

    do3 = R["nbuf"]

    def send_do(done=False):
        for j in range(2):
            i0 = EX["do"][0] if j == 0 else L0 + 4
            sref = do3.at[j, :, ds128(HALF * (1 - c), HALF)]
            dref = doa.at[ds128(2 * T * c + j * T, T)]
            d = rcopy(sref, dref, i0, i0, (other, z))
            d.wait_send() if done else d.start()
        for k in (1, 2, 3):
            t = lax.rem(g + k, 4)
            d = rcopy(
                do3.at[2, :, ds128(HALF * lax.div(t, 2) + 128 * lax.rem(t, 2), 256)],
                dob.at[ds128(T * g, T)],
                EX["do"][2] + k,
                EX["do"][1] + k,
                dev_of(t),
            )
            d.wait_send() if done else d.start()

    per = W // FT
    for q in range(dps):
        R["ub"][q : q + 1, :] = vt[V_UB + q // per : V_UB + q // per + 1, (q % per) * FT : (q % per + 1) * FT]
    pl.run_scoped(
        feed,
        pltpu.VMEM((3 * T, W), f32),
        pltpu.VMEM((3 * T, W), f32),
        pltpu.VMEM((W, 3 * T), bf16),
        pltpu.VMEM((2, 3 * T, FT), bf16),
    )
    for q in range(dps):
        vg[V_UB + q // per : V_UB + q // per + 1, (q % per) * FT : (q % per + 1) * FT] = R["ub"][q : q + 1, :]

    def grads_move(step):
        if not aligned:
            return
        if step == 0:
            rs1(O_)
            for a in (D_, U_, O_):
                rs2(a)
        elif step == 1:
            for a in (D_, U_, O_):
                rs3(a)
        elif step == 2:
            for a in (D_, U_, O_):
                rs4(a)
        elif step == 3:
            for a in (D_, U_, O_):
                y_send("QOUD"[a], 2)
        elif step == 4:
            for a in (D_, U_, O_):
                y_send("QOUD"[a], 3)
        elif step == 5:
            for a in (D_, U_, O_):
                y_final(a, outs[a])

    for j in range(2):
        doa[ds128(2 * T * c + j * T, T), :] = do3[j, :, ds128(HALF * c, HALF)]
    dob[ds128(T * g, T), :] = do3[2, :, ds128(HALF * e + 128 * c, 256)]
    recv(doa.at[ds128(2 * T * (1 - c), T)], EX["do"][0])
    recv(doa.at[ds128(2 * T * (1 - c) + T, T)], L0 + 4)
    grads_move(0)

    def attend_back(src, o_ref, d_ref, col, bi, sel, lrow, dk, dv, delta):
        cols = ds128(col, 128)
        k2 = src[1, :, cols]
        v2 = src[2, :, cols]
        kt = k2.T
        b = bias[bi]
        keys = [key_side(k2, b, i) for i in sel]
        dk[...] = jnp.zeros_like(dk)
        dv[...] = jnp.zeros_like(dv)
        prod = o_ref[0, :, cols].astype(f32) * d_ref[:, cols].astype(f32)
        hi = prod.astype(bf16)
        lo = (prod - hi.astype(f32)).astype(bf16)
        row = lax.broadcasted_iota(i32, (8, 128), 0)
        if len(sel) == 2:
            pickm = (row == lax.broadcasted_iota(i32, (8, 128), 1) // 64).astype(f32).astype(bf16)
        else:
            pickm = jnp.where(jnp.logical_and(row == 0, lane // 64 == sel[0]), 1.0, 0.0).astype(bf16)
        delta[...] = nt(pickm, hi) + nt(pickm, lo)

        @pl.loop(0, N // QT)
        def _(q):
            r = ds128(q * QT, QT)
            q2 = src[0, r, cols]
            d2 = d_ref[r, cols]
            dks, dvs, dqs = [], [], []
            for n, i in enumerate(sel):
                qm, dm = half(i, q2), half(i, d2)
                s = nt(keys[n], query_side(q2, i))
                p = jnp.exp2(s * SC - lse[pl.ds(lrow + n, 1), r])
                dp_ = nt(v2, dm)
                ds_ = (p * (dp_ - delta[pl.ds(n, 1), r])).astype(bf16)
                dvs.append(nn(p.astype(bf16), dm))
                dks.append(nn(ds_, qm))
                dqs.append(nn(kt, ds_).T if len(sel) == 1 else nn(kt[64 * i : 64 * i + 64], ds_))
            if len(sel) == 2:
                dk[...] += dks[0] + dks[1]
                dv[...] += dvs[0] + dvs[1]
                dq = jnp.concatenate(dqs, axis=0).T
            else:
                dk[...] += dks[0]
                dv[...] += dvs[0]
                dq = half(sel[0], dqs[0])
            src[0, r, cols] = (dq * 0.125).astype(bf16)

        src[1, :, cols] = (dk[...] * 0.125).astype(bf16)
        src[2, :, cols] = dv[...].astype(bf16)

    def back(dk, dv, delta):
        @pl.loop(0, 3)
        def _(t):
            attend_back(qkva, atta, doa, t * 128, 0, (0, 1), 2 * t, dk, dv, delta)

        from_heads_a("dqkv", qkva, qkv).start()
        from_heads_a_own("dqkv", qkva, qkv, L0 + 5).start()
        grads_move(1)
        for k in (1, 2, 3):
            recv(dob.at[ds128(T * lax.rem(g + 4 - k, 4), T)], EX["do"][1] + k)
        attend_back(qkvb, attb, dob, c * 128, 1, (0, 1), 6, dk, dv, delta)
        grads_move(2)
        attend_back(qkvb, attb, dob, (1 - c) * 128, 1, (c,), 8, dk, dv, delta)
        grads_move(3)

    pl.run_scoped(back, pltpu.VMEM((N, 128), f32), pltpu.VMEM((N, 128), f32), pltpu.VMEM((8, N), f32))
    xatt.wait_send()
    for d in xattb:
        d.wait_send()
    send_do(done=True)
    xb2 = [from_heads_b("dqkv", qkvb, 0, k) for k in (1, 2, 3)]
    for d in xb2:
        d.start()
    lb2 = from_heads_b_own(qkvb, L0 + 6)
    lb2.start()

    gsend = cot
    for s in range(3):
        normed_rows(s)

    def rows_back(s):
        r = pl.ds(s * T, T)
        e_ = nt(qkv[0, r, :], wblock(R["wq"], slice(0, W)))
        e_ += nt(qkv[1, r, :], wblock(R["wq"], slice(W, 2 * W)))
        e_ += nt(qkv[2, r, :], wblock(R["wq"], slice(2 * W, 3 * W)))
        n, inv = normalise(rows[s].astype(f32))
        gsend[s] = (mid[r, :] + norm_back(e_, n, inv, vec(V_NG))).astype(bf16)
        move_home(s, gsend.at[s], grh, S_GR, I_GR)
        parts = (
            (V_NG, col_sum(e_ * n)),
            (V_NS, col_sum(e_)),
            (V_QB, col_sum(qkv[0, r, :].astype(f32))),
            (V_VB, col_sum(qkv[2, r, :].astype(f32))),
        )
        for i, part in parts:
            if s == 0:
                vg[i : i + 1, :] = part
            else:
                vg[i : i + 1, :] += part

    for m in range(3):
        move_out_done(m, R["cnth"].at[m], cnt, S_CNT, I_CNT)
        move_out_done(m, R["cotangent"].at[m], cot, S_COT, I_COT)
    from_heads_a_own("dqkv", qkva, qkv, L0 + 5).wait()
    wait_a("dqkv", qkv, False)
    rows_back(0)
    rows_back(1)
    lb2.wait()
    wait_b_tokens("dqkv", 3)
    for j in range(3):
        merge_b(qkv, j, j)
    rows_back(2)
    for j in range(3):
        w = tn(nbuf[...].reshape(3 * T, W), qkv[j]).astype(bf16)
        R["wq"][:, :, j * W : (j + 1) * W] = w.reshape(dps, KR, W)
    if aligned:
        rs1(Q_)
        grads_move(4)
        rs2(Q_)
        grads_move(5)
        rs3(Q_)
        rs4(Q_)
        y_send("Q", 2)
        y_send("Q", 3)
        y_final(Q_, outs[Q_])
    else:
        save = [pltpu.make_async_copy(arrays[i], R[n], rs.at[L0 + 8 + i]) for i, n in enumerate(("gq", "go", "gu", "gd"))]
        for d in save:
            d.start()
        for d in save:
            d.wait()
    vg[12:16, :] = jnp.zeros((4, W), f32)
    from_heads_a("dqkv", qkva, qkv).wait_send()
    for d in xb2:
        d.wait_send()
    for s in range(3):
        move_home_done(s, gsend.at[s], grh, S_GR, I_GR)
    for m in range(3):
        arrived_home(m, act, I_ACT)
        arrived_home(m, grh, I_GR)
    assert count[0] <= cfg["sems"], count[0]


def scatter_kernel(keep, grads, out):
    places = lax.broadcasted_iota(i32, (out.shape[1], keep.shape[2]), 0)
    out[0] = nn((places == keep[0]).astype(f32).astype(bf16), grads[0])


def body(patches, keep_index, shard_counts, cotangent, *shards):
    ng, ns, wq, qb, vb, wo, ob, mg, ms, wu, ub, wd, db = shards
    batches, _, patch, width = patches.shape
    tokens = keep_index.shape[2]
    dp_size, blk_size = lax.axis_size("dp"), lax.axis_size("blk")
    devices = dp_size * blk_size
    ff = wu.shape[1]
    aligned = dp_size == 8 and blk_size == 4
    dps = 8
    kr, fr = width // dps, ff // dps
    vectors = jnp.stack([ng, ns, qb, vb, ob, mg, ms, db])
    if aligned:
        own = jnp.pad(vectors, ((0, 0), (0, 128 - vectors.shape[1])))
        own_ub = jnp.pad(ub[None], ((0, 7), (0, 128 - ub.shape[0])))
        table = jnp.concatenate([own, own_ub])
        weights = (wq, wo, wu, wd)
        pieces = [w.size // 128 for w in weights] + [16]
        flat = [sum(pieces[:i]) for i in range(6)]
    else:
        axes = ("dp", "blk")
        table = lax.all_gather(vectors, axes, axis=1, tiled=True).astype(f32)
        table_ub = lax.all_gather(ub, axes, axis=0, tiled=True).astype(f32).reshape(ff // width, width)
        table = jnp.concatenate([table, table_ub, jnp.zeros((16 - 8 - ff // width, width), f32)])
        weights = tuple(lax.all_gather(w, axes, axis=0, tiled=True) for w in (wq, wo, wu, wd))
        weights = tuple(w.reshape(dps, -1, w.shape[1]) for w in weights)
        flat = None
    cfg = dict(aligned=aligned, dps=dps, tokens=tokens, width=width, ff=ff, patch=patch, flat=flat, sems=260)
    keep = keep_index
    ins = [
        ("patches", patches[:, 0], ANY),
        ("keep", keep, VMEM),
        ("counts", shard_counts[:, 0], SMEM),
        ("cotangent", cotangent[:, 0], ANY),
    ]
    ins += [(n, w, VMEM if aligned else ANY) for n, w in zip(("sq", "so", "su", "sd"), weights)]
    ins.append(("sv", table, VMEM))
    out = [
        ("act", (3, tokens, width), bf16, ANY),
        ("grh", (3, tokens, width), bf16, ANY),
        ("vg", (16, width), f32, VMEM),
    ]
    full = {"q": (dps, kr, 3 * width), "o": (dps, kr, width), "u": (dps, kr, ff), "d": (dps, fr, width)}
    for i, n in enumerate("qoud"):
        if aligned:
            out.append(("g" + n, weights[i].shape, f32, VMEM))
        else:
            out.append(("g" + n, full[n], bf16, ANY))
    t3 = 3 * tokens
    scratch = [("w" + n, full[n], bf16) for n in "qoud"]
    scratch += [
        ("rows", (3, tokens, width), bf16),
        ("cot", (3, tokens, width), bf16),
        ("cnt", (3, 16, 128), bf16),
        ("cnth", (3, 16, 128), bf16),
        ("nbuf", (3, tokens, width), bf16),
        ("qkv", (3, t3, width), bf16),
        ("qkva", (3, 4 * tokens, width // 2), bf16),
        ("qkvb", (3, 4 * tokens, 256), bf16),
        ("atta", (1, 4 * tokens, width // 2), bf16),
        ("attb", (1, 4 * tokens, 256), bf16),
        ("att", (1, t3, width), bf16),
        ("fromb", (4, 3, tokens, 256), bf16),
        ("doa", (4 * tokens, width // 2), bf16),
        ("dob", (4 * tokens, 256), bf16),
        ("mid", (t3, width), f32),
        ("vt", (16, width), f32),
        ("lse", (16, 4 * tokens), f32),
        ("bias", (2, 4 * tokens, 128), bf16),
        ("ub", (dps, fr), f32),
    ]
    if aligned:
        scratch += [
            ("zbuf", (4, flat[5], 128), bf16),
            ("zrr", (3, flat[4], 128), bf16),
            ("zrl", (3, flat[4], 128), bf16),
            ("vw", (dps, 64, 128), bf16),
        ]
        scratch += [("rb1" + n, (4, *full[n][1:]), bf16) for n in "qoud"]
        scratch += [("rb2" + n, (3, *full[n][1:]), bf16) for n in "qoud"]
    names = [n for n, _, _ in scratch] + ["ss", "rs"]
    shapes = [pltpu.VMEM(s, d) for _, s, d in scratch] + [pltpu.SemaphoreType.DMA((cfg["sems"],))] * 2
    flops = 6 * 3 * tokens * (4 * width * width + 2 * width * ff)
    results = pl.pallas_call(
        functools.partial(layer_kernel, cfg, [n for n, _, _ in ins], [n for n, *_ in out], names),
        out_shape=[jax.ShapeDtypeStruct(s, d) for _, s, d, _ in out],
        in_specs=[s for _, _, s in ins],
        out_specs=[s for *_, s in out],
        scratch_shapes=shapes,
        compiler_params=pltpu.CompilerParams(collective_id=0, has_side_effects=True, vmem_limit_bytes=64 * 1024 * 1024 - 512 * 1024),
        cost_estimate=pl.CostEstimate(flops=flops, bytes_accessed=50_000_000, transcendentals=0),
        name="layer",
    )(*[a for _, a, _ in ins])
    act, grh, vg, gq, go, gu, gd = results
    patch_grad = pl.pallas_call(
        scatter_kernel,
        grid=(3,),
        in_specs=[pl.BlockSpec((1, 1, tokens), lambda m: (m, 0, 0)), pl.BlockSpec((1, tokens, width), lambda m: (m, 0, 0))],
        out_specs=pl.BlockSpec((1, patch, width), lambda m: (m, 0, 0)),
        out_shape=jax.ShapeDtypeStruct((3, patch, width), f32),
        compiler_params=pltpu.CompilerParams(vmem_limit_bytes=32 * 1024 * 1024),
        name="scatter",
    )(keep, grh)
    small = jnp.concatenate([vg[:8].reshape(8, devices, -1).transpose(1, 0, 2).reshape(devices, -1), vg[8 : 8 + ff // width].reshape(devices, -1)], axis=1)
    small = lax.psum_scatter(small, ("dp", "blk"), scatter_dimension=0, tiled=True)[0]
    n = width // devices
    piece = [small[i * n : (i + 1) * n] for i in range(8)] + [small[8 * n :]]
    if not aligned:
        axes = ("dp", "blk")
        gq, go, gu, gd = (
            lax.psum_scatter(w.reshape(-1, w.shape[-1]).astype(f32), axes, scatter_dimension=0, tiled=True) for w in (gq, go, gu, gd)
        )
    return (
        act[:, None],
        patch_grad[:, None],
        piece[V_NG],
        piece[V_NS],
        gq,
        piece[V_QB],
        piece[V_VB],
        go,
        piece[V_OB],
        piece[V_MG],
        piece[V_MS],
        gu,
        piece[V_UB],
        gd,
        piece[V_DB],
    )


def solution(mesh):
    vec, mat = P(("dp", "blk")), P(("dp", "blk"), None)
    tok = P(None, "dp", "blk", None)
    params = (vec, vec, mat, vec, vec, mat, vec, vec, vec, mat, vec, mat, vec)
    in_specs = (tok, P(None, "dp", "blk"), P(None, "dp", None), tok) + params
    out_specs = (tok, tok) + params
    return jax.shard_map(body, mesh=mesh, in_specs=in_specs, out_specs=out_specs, check_vma=False)
```

```python
import functools

import jax
import jax.numpy as jnp
from jax import lax
from jax.experimental import pallas as pl
from jax.experimental.pallas import tpu as pltpu
from jax.sharding import PartitionSpec as P

MESH = pl.DeviceIdType.MESH
ANY = pl.BlockSpec(memory_space=pl.ANY)
VMEM = pl.BlockSpec(memory_space=pltpu.VMEM)
SMEM = pl.BlockSpec(memory_space=pltpu.SMEM)
f32, bf16, i32 = jnp.float32, jnp.bfloat16, jnp.int32

EPSILON = 1e-06
LOG2E = 1.4426950408889634
NEG = -1e30


def nn(a, b):
    return lax.dot_general(a, b, (((1,), (0,)), ((), ())), preferred_element_type=f32)


def nt(a, b):
    return lax.dot_general(a, b, (((1,), (1,)), ((), ())), preferred_element_type=f32)


def tn(a, b):
    return lax.dot_general(a, b, (((0,), (0,)), ((), ())), preferred_element_type=f32)


def mult(x, k):
    return x if isinstance(x, int) else pl.multiple_of(x, k)


def normalise(v):
    centred = v - jnp.mean(v, axis=1, keepdims=True)
    inv = lax.rsqrt(jnp.mean(centred * centred, axis=1, keepdims=True) + EPSILON)
    return centred * inv, inv


def norm_back(e, n, inv, gain):
    f = e * gain
    return inv * (f - jnp.mean(f, axis=1, keepdims=True) - n * jnp.mean(f * n, axis=1, keepdims=True))


def col_sum(v):
    return jnp.sum(v, axis=0, keepdims=True)


V_NG, V_NS, V_QB, V_VB, V_OB, V_MG, V_MS, V_DB, V_UB = range(9)


def layer_kernel(cfg, names_in, names_out, names_scratch, *refs):
    R = dict(zip(names_in + names_out + names_scratch, refs, strict=True))
    aligned, dps = cfg["aligned"], cfg["dps"]
    T, W, F = cfg["tokens"], cfg["width"], cfg["ff"]
    KR = W // dps
    FR = F // dps
    HALF = W // 2
    dp, z = lax.axis_index("dp"), lax.axis_index("blk")
    c = lax.rem(dp, 2)
    base = dp - c
    h, e = lax.div(z, 2), lax.rem(z, 2)
    g = 2 * e + c
    other = base + 1 - c
    ss, rs = R["ss"], R["rs"]
    count = [0]

    def take(n=1):
        count[0] += n
        return count[0] - n

    def rcopy(src, dst, s, r, dev):
        return pltpu.make_async_remote_copy(
            src_ref=src, dst_ref=dst, send_sem=ss.at[s], recv_sem=rs.at[r], device_id=dev, device_id_type=MESH
        )

    def recv(dst, r, dev=None):
        rcopy(dst, dst, 0, r, (other, z) if dev is None else dev).wait_recv()

    bar = pltpu.get_barrier_semaphore()
    peers = []
    for k in range(1, 8):
        j = lax.rem(c * 4 + z + k, 8)
        peers.append((base + lax.div(j, 4), lax.rem(j, 4)))
    if aligned:
        dx = 2 - 4 * lax.rem(lax.div(dp, 2), 2)
        dy = 4 - 8 * lax.div(dp, 4)
        p1, p2, p3 = dp + (1 - c) * dx + c * dy, dp + c * dx + (1 - c) * dy, dp + dx + dy
        peers += [(p1, z), (p2, z)]
    for dev in peers:
        pl.semaphore_signal(bar, inc=1, device_id=dev, device_id_type=MESH)

    def owner(m):
        if m < 2:
            return lax.div(z, 2), 2 * c + m, lax.rem(z, 2)
        return lax.rem(z, 2), 2 * c + lax.div(z, 2), 2

    def home(s):
        if s < 2:
            return h, 2 * c + s
        return h, 2 * e + c

    def move_out(m, src, dst, sid, rid):
        tc, tz, slot = owner(m)
        own = jnp.logical_and(tc == c, tz == z)

        @pl.when(own)
        def _():
            pltpu.make_async_copy(src, dst.at[slot], rs.at[rid + slot]).start()

        @pl.when(jnp.logical_not(own))
        def _():
            rcopy(src, dst.at[slot], sid + m, rid + slot, (base + tc, tz)).start()

    def move_out_done(m, src, dst, sid, rid):
        tc, tz, slot = owner(m)
        own = jnp.logical_and(tc == c, tz == z)

        @pl.when(jnp.logical_not(own))
        def _():
            rcopy(src, dst.at[slot], sid + m, rid + slot, (base + tc, tz)).wait_send()

    def move_home(s, src, dst, sid, rid):
        tc, tz = home(s)
        m = e if s < 2 else 2
        own = jnp.logical_and(tc == c, tz == z)

        @pl.when(own)
        def _():
            pltpu.make_async_copy(src, dst.at[m], ss.at[sid + s]).start()

        @pl.when(jnp.logical_not(own))
        def _():
            rcopy(src, dst.at[m], sid + s, rid + m, (base + tc, tz)).start()

    def move_home_done(s, src, dst, sid, rid):
        tc, tz = home(s)
        m = e if s < 2 else 2
        own = jnp.logical_and(tc == c, tz == z)

        @pl.when(own)
        def _():
            pltpu.make_async_copy(src, dst.at[m], ss.at[sid + s]).wait()

        @pl.when(jnp.logical_not(own))
        def _():
            rcopy(src, dst.at[m], sid + s, rid + m, (base + tc, tz)).wait_send()

    def arrived_home(m, dst, rid):
        tc, tz, _ = owner(m)

        @pl.when(jnp.logical_not(jnp.logical_and(tc == c, tz == z)))
        def _():
            recv(dst.at[m], rid + m)

    arrays = [R["wq"], R["wo"], R["wu"], R["wd"]]
    Q_, O_, U_, D_ = 0, 1, 2, 3
    if aligned:
        zbuf, zrr, zrl = R["zbuf"], R["zrr"], R["zrl"]
        flat = cfg["flat"]
        CH = {"Q": (0, flat[1]), "OU": (flat[1], flat[3]), "D": (flat[3], flat[4]), "V": (flat[4], flat[5])}
        ZR = {k: take(3) - 1 for k in CH}
        ZL = {k: take(3) - 1 for k in CH}
        wide = W // 128
        GC = {"D": (D_, 0, wide), "O": (O_, 0, wide)}
        for i in range(2):
            GC["U%d" % i] = (U_, i * F // 256, (i + 1) * F // 256)
        for i in range(3):
            GC["Q%d" % i] = (Q_, i * wide, (i + 1) * wide)
        YR = {k: take(3) - 1 for k in GC}
        YL = {k: take(3) - 1 for k in GC}
        gathered = arrays + [R["vw"]]
        XY = [take(3) for _ in range(5)]
        CR = [take(4) for _ in range(5)]
        R1 = {k: take(4) for k in GC}
        R2 = {k: take(3) for k in GC}

        def z_send(key, k, done=False):
            r0, r1 = CH[key]
            rows = pl.ds(r0, r1 - r0)
            right = jnp.logical_and(z < 3, z - (k - 1) >= 0)
            left = jnp.logical_and(z > 0, z + (k - 1) <= 3)

            @pl.when(right)
            def _():
                ref = zbuf.at[z - (k - 1), rows]
                d = rcopy(ref, ref, ZR[key] + k, ZR[key] + k, (dp, z + 1))
                d.wait_send() if done else d.start()

            @pl.when(left)
            def _():
                ref = zbuf.at[z + (k - 1), rows]
                d = rcopy(ref, ref, ZL[key] + k, ZL[key] + k, (dp, z - 1))
                d.wait_send() if done else d.start()

        def z_wait(key, k):
            r0, r1 = CH[key]
            rows = pl.ds(r0, r1 - r0)

            @pl.when(z - k >= 0)
            def _():
                recv(zbuf.at[z - k, rows], ZR[key] + k)

            @pl.when(z + k <= 3)
            def _():
                recv(zbuf.at[z + k, rows], ZL[key] + k)

        def flatten(a, ref, slot):
            if a == D_:
                n, rows = W // 128, FR // 4
            elif a == 4:
                n, rows = 1, 16
            else:
                n, rows = ref.shape[-1] // 128, KR // 4
            for t in range(n):
                cols = slice(t * 128, (t + 1) * 128)
                zbuf[slot, flat[a] + t * rows : flat[a] + (t + 1) * rows, :] = ref[:, cols]

        def unflatten(a, block):
            dst = gathered[a]
            if a == D_:
                n, rows = W // 128, FR // 4
            elif a == 4:
                n, rows = 1, 16
            else:
                n, rows = dst.shape[-1] // 128, KR // 4
            for s in range(4):
                for t in range(n):
                    dst[block, s * rows : (s + 1) * rows, t * 128 : (t + 1) * 128] = zbuf[s, flat[a] + t * rows : flat[a] + (t + 1) * rows, :]

        def ag_copies(a):
            ref = gathered[a]

            def core(i):
                block = (dp, p1, p2, p3)[i]
                return rcopy(ref.at[block], ref.at[block], CR[a] + i, CR[a] + i, (other, z))

            return {
                "p1": lambda: rcopy(ref.at[dp], ref.at[dp], XY[a], XY[a], (p1, z)),
                "p2": lambda: rcopy(ref.at[dp], ref.at[dp], XY[a] + 1, XY[a] + 1, (p2, z)),
                "fw": lambda: rcopy(ref.at[p1], ref.at[p1], XY[a] + 2, XY[a] + 2, (p2, z)),
                "c0": lambda: core(0),
                "c1": lambda: core(1),
                "c2": lambda: core(2),
                "c3": lambda: core(3),
            }

        def ag1(a):
            d = ag_copies(a)
            d["p1"]().start()
            d["p2"]().start()
            d["c0"]().start()

        def ag2(a):
            d = ag_copies(a)
            ref = gathered[a]
            recv(ref.at[p1], XY[a])
            d["fw"]().start()
            d["c1"]().start()
            recv(ref.at[p2], XY[a] + 1)
            d["c2"]().start()

        def ag3(a):
            d = ag_copies(a)
            recv(gathered[a].at[p3], XY[a] + 2)
            d["c3"]().start()

        def ag4(a):
            d = ag_copies(a)
            for i, block in enumerate((dp, p2, p1, p3)):
                recv(gathered[a].at[block + other - dp], CR[a] + i)
            for k in d.values():
                k().wait_send()

        def blk_of(i):
            return 2 * i + c

        bufs1 = [R["rb1" + n] for n in "qoud"]
        bufs2 = [R["rb2" + n] for n in "qoud"]

        def cols_of(key):
            _, t0, t1 = GC[key]
            return pl.ds(t0 * 128, (t1 - t0) * 128)

        def block_of(key, block):
            return arrays[GC[key][0]].at[block, :, cols_of(key)]

        def view(bufs, key, i):
            return bufs[GC[key][0]].at[i, :, cols_of(key)]

        def rs_core(key, i):
            return rcopy(block_of(key, 2 * i + 1 - c), view(bufs1, key, i), R1[key] + i, R1[key] + i, (other, z))

        def rs1(key):
            for i in range(4):
                rs_core(key, i).start()

        def addto(key, block, parts):
            ref, cols = arrays[GC[key][0]], cols_of(key)
            rows = ref.shape[1]
            step = 48

            @pl.loop(0, rows // step)
            def _(q):
                r = pl.ds(mult(q * step, step), step)
                total = ref[block, r, cols].astype(f32)
                for p, i in parts:
                    total = total + p[GC[key][0]][i, r, cols].astype(f32)
                ref[block, r, cols] = total.astype(bf16)

        def rs_xy(key):
            i0 = R2[key]
            return {
                "diag": lambda: rcopy(block_of(key, p3), view(bufs2, key, 0), i0, i0, (p2, z)),
                "p2": lambda: rcopy(block_of(key, p2), view(bufs2, key, 1), i0 + 1, i0 + 1, (p2, z)),
                "p1": lambda: rcopy(block_of(key, p1), view(bufs2, key, 2), i0 + 2, i0 + 2, (p1, z)),
            }

        def rs2_pair(key, i):
            recv(view(bufs1, key, i), R1[key] + i)
            addto(key, blk_of(i), [(bufs1, i)])

            @pl.when(blk_of(i) == p3)
            def _():
                rs_xy(key)["diag"]().start()

            @pl.when(blk_of(i) == p2)
            def _():
                rs_xy(key)["p2"]().start()

        def rs2(key):
            for i in range(4):
                rs2_pair(key, i)

        def rs3(key):
            recv(view(bufs2, key, 0), R2[key])
            addto(key, p1, [(bufs2, 0)])
            rs_xy(key)["p1"]().start()

        def span(key):
            a, t0, t1 = GC[key]
            n = arrays[a].shape[1] // 4
            return a, n, flat[a] + t0 * n, (t1 - t0) * n

        def rs4(key):
            recv(view(bufs2, key, 1), R2[key] + 1)
            recv(view(bufs2, key, 2), R2[key] + 2)
            addto(key, dp, [(bufs2, 1), (bufs2, 2)])
            a, n, _, _ = span(key)
            for slot in range(4):
                for t in range(GC[key][1], GC[key][2]):
                    piece = arrays[a][dp, slot * n : (slot + 1) * n, t * 128 : (t + 1) * 128]
                    zbuf[slot, flat[a] + t * n : flat[a] + (t + 1) * n, :] = piece
            y_send(key, 1)

        def y_send(key, k, done=False):
            _, _, r0, rn = span(key)
            rows = pl.ds(r0, rn)
            to_right = z + 4 - k
            to_left = z - 4 + k

            @pl.when(jnp.logical_and(z < 3, to_right <= 3))
            def _():
                if k > 1 and not done:

                    @pl.when(z >= 1)
                    def _():
                        recv(zrr.at[k - 2, rows], YR[key] + k - 1)
                        zbuf[to_right, rows, :] = (zbuf[to_right, rows, :].astype(f32) + zrr[k - 2, rows, :].astype(f32)).astype(bf16)

                d = rcopy(zbuf.at[to_right, rows], zrr.at[k - 1, rows], YR[key] + k, YR[key] + k, (dp, z + 1))
                d.wait_send() if done else d.start()

            @pl.when(jnp.logical_and(z > 0, to_left >= 0))
            def _():
                if k > 1 and not done:

                    @pl.when(z <= 2)
                    def _():
                        recv(zrl.at[k - 2, rows], YL[key] + k - 1)
                        zbuf[to_left, rows, :] = (zbuf[to_left, rows, :].astype(f32) + zrl[k - 2, rows, :].astype(f32)).astype(bf16)

                d = rcopy(zbuf.at[to_left, rows], zrl.at[k - 1, rows], YL[key] + k, YL[key] + k, (dp, z - 1))
                d.wait_send() if done else d.start()

        def y_final(key):
            a, n, r0, rn = span(key)
            rows = pl.ds(r0, rn)

            @pl.when(z >= 1)
            def _():
                recv(zrr.at[2, rows], YR[key] + 3)

            @pl.when(z <= 2)
            def _():
                recv(zrl.at[2, rows], YL[key] + 3)

            for t in range(GC[key][1], GC[key][2]):
                piece = slice(flat[a] + t * n, flat[a] + (t + 1) * n)
                total = zbuf[z, piece, :].astype(f32)
                total = total + jnp.where(z >= 1, zrr[2, piece, :].astype(f32), 0.0)
                total = total + jnp.where(z <= 2, zrl[2, piece, :].astype(f32), 0.0)
                outs[a][:, t * 128 : (t + 1) * 128] = total

        def rs_done(key):
            for k in (1, 2, 3):
                y_send(key, k, done=True)
            for i in range(4):
                rs_core(key, i).wait_send()
            for d in rs_xy(key).values():
                d().wait_send()

        outs = [R["gq"], R["go"], R["gu"], R["gd"]]

    I_ROWS, I_CNT, I_COT, I_ACT, I_GR = (take(3) for _ in range(5))
    S_ROWS, S_CNT, S_COT, S_ACT, S_GR = (take(3) for _ in range(5))
    EX = {}
    for k in ("qkv", "att", "do", "dqkv"):
        EX[k] = (take(1), take(4), take(4))
    L0 = take(12)

    rows, cot, cnt, nbuf = R["rows"], R["cot"], R["cnt"], R["nbuf"]
    qkv, qkva, qkvb = R["qkv"], R["qkva"], R["qkvb"]
    atta, attb, att, fromb = R["atta"], R["attb"], R["att"], R["fromb"]
    doa, dob, mid, vt, vg = R["doa"], R["dob"], R["mid"], R["vt"], R["vg"]
    lse, grh, keep, act = R["lse"], R["grh"], R["keep"], R["act"]
    lane = lax.broadcasted_iota(i32, (1, 128), 1)

    if aligned:
        for a, name in enumerate(("sq", "so", "su", "sd", "sv")):
            flatten(a, R[name], z)
    for m in range(3):
        for b in range(4):
            R["cnth"][m, b : b + 1, :] = jnp.full((1, 128), R["counts"][m, b], i32).astype(f32).astype(bf16)
        R["cnth"][m, 4:, :] = jnp.zeros((12, 128), bf16)

    def pick_rows(pbuf, psem):
        copies = [pltpu.make_async_copy(R["patches"].at[m], pbuf.at[m], psem.at[m]) for m in range(3)]
        for d in copies:
            d.start()
        pl.semaphore_wait(bar, len(peers))
        if aligned:
            z_send("Q", 1)
            z_send("V", 1)
        for m in range(3):
            copies[m].wait()
            spread = (lax.broadcasted_iota(i32, (cfg["patch"], T), 0) == keep[m]).astype(f32).astype(bf16)
            att[0, m * T : (m + 1) * T, :] = tn(spread, pbuf[m]).astype(bf16)

    pl.run_scoped(pick_rows, pltpu.VMEM((3, cfg["patch"], W), bf16), pltpu.SemaphoreType.DMA((3,)))

    def send_rows():
        for m in (2, 0, 1):
            move_out(m, att.at[0, pl.ds(m * T, T)], rows, S_ROWS, I_ROWS)
            move_out(m, R["cnth"].at[m], cnt, S_CNT, I_CNT)

    def send_cot():
        for m in (2, 0, 1):
            move_out(m, R["cotangent"].at[m], cot, S_COT, I_COT)

    if aligned:
        for key in "QV":
            z_wait(key, 1)
            z_send(key, 2)
        z_send("OU", 1)
        for key in "QV":
            z_wait(key, 2)
            z_send(key, 3)
        z_wait("OU", 1)
        z_send("OU", 2)
        for key in "QV":
            z_wait(key, 3)
        unflatten(Q_, dp)
        ag1(Q_)
        unflatten(4, dp)
        ag1(4)
        z_wait("OU", 2)
        z_send("OU", 3)
        send_rows()
        z_send("D", 1)
    else:
        full = [pltpu.make_async_copy(R[n], arrays[i], rs.at[L0 + 8 + i]) for i, n in enumerate(("sq", "so", "su", "sd"))]
        for d in full:
            d.start()
        send_rows()
        send_cot()
    if aligned:
        ag2(Q_)
        ag2(4)
        z_wait("OU", 3)
        for a in (U_, O_):
            unflatten(a, dp)
            ag1(a)
        ag3(Q_)
        ag3(4)
        ag4(4)
        v = R["vw"][...].reshape(32 * 16, 128)
        to = lax.broadcasted_iota(i32, (128, W), 1)
        frm = lax.broadcasted_iota(i32, (128, W), 0)
        dev = lax.broadcasted_iota(i32, (512, W), 0) // 16
        col = lax.broadcasted_iota(i32, (512, W), 1)
        n1, n2 = W // 32, F // 32
        x1 = nn(v, (lax.rem(to, n1) == frm).astype(f32).astype(bf16))
        x1 = jnp.where(dev == col // n1, x1, 0.0)
        vt[0:16, :] = jnp.sum(x1.reshape(32, 16, W), axis=0)
        x2 = nn(v, (lax.rem(to, n2) == frm).astype(f32).astype(bf16))
        x2 = jnp.where(lax.rem(dev, W // n2) == col // n2, x2, 0.0)
        x2 = jnp.sum(x2.reshape(4, 8, 16, W), axis=1)
        for q in range(4):
            vt[V_UB + q : V_UB + q + 1, :] = x2[q, V_UB : V_UB + 1, :]
    else:
        vt[...] = R["sv"][...]

    def vec(i):
        return vt[i : i + 1, :]

    def normed_rows(s):
        n, _ = normalise(rows[s].astype(f32))
        nbuf[s] = (n * vec(V_NG) + vec(V_NS)).astype(bf16)

    for s in (2, 0, 1):
        recv(rows.at[s], I_ROWS + s)
        recv(cnt.at[s], I_CNT + s)
        normed_rows(s)
        if s == 2:
            if aligned:
                ag4(Q_)
            else:
                for d in full:
                    d.wait()

    def wblock(ref, cols=None):
        v = ref[...] if cols is None else ref[:, :, cols]
        return v.reshape(-1, v.shape[-1])

    def project(s):
        for j in range(3):
            v = nn(nbuf[s], wblock(R["wq"], slice(j * W, (j + 1) * W)))
            if j == 0:
                v = v + vec(V_QB)
            if j == 2:
                v = v + vec(V_VB)
            qkv[j, pl.ds(mult(s * T, T), T), :] = v.astype(bf16)

    def dev_of(i):
        return (base + lax.rem(i, 2), 2 * h + lax.div(i, 2))

    def ds128(x, n):
        return pl.ds(mult(x, 128), n)

    def to_heads_a(kind, src, dst):
        i0 = EX[kind][0]
        full_ = [slice(None)] * (len(src.shape) - 2)
        sref = src.at[(*full_, pl.ds(0, 2 * T), ds128(HALF * (1 - c), HALF))]
        dref = dst.at[(*full_, ds128(2 * T * c, 2 * T))]
        return rcopy(sref, dref, i0, i0, (other, z))

    def to_heads_a_own(kind, src, dst, lid):
        full_ = [slice(None)] * (len(src.shape) - 2)
        sref = src.at[(*full_, pl.ds(0, 2 * T), ds128(HALF * c, HALF))]
        dref = dst.at[(*full_, ds128(2 * T * c, 2 * T))]
        return pltpu.make_async_copy(sref, dref, rs.at[lid])

    def to_heads_b(kind, src, dst, k):
        _, rid, sid = EX[kind]
        full_ = [slice(None)] * (len(src.shape) - 2)
        t = lax.rem(g + k, 4)
        sref = src.at[(*full_, pl.ds(2 * T, T), ds128(HALF * lax.div(t, 2) + 128 * lax.rem(t, 2), 256))]
        dref = dst.at[(*full_, ds128(T * g, T))]
        return rcopy(sref, dref, sid + k, rid + k, dev_of(t))

    def to_heads_b_own(kind, src, dst, lid):
        full_ = [slice(None)] * (len(src.shape) - 2)
        sref = src.at[(*full_, pl.ds(2 * T, T), ds128(HALF * e + 128 * c, 256))]
        dref = dst.at[(*full_, ds128(T * g, T))]
        return pltpu.make_async_copy(sref, dref, rs.at[lid])

    def from_heads_a(kind, src, dst):
        i0 = EX[kind][0]
        full_ = [slice(None)] * (len(src.shape) - 2)
        sref = src.at[(*full_, ds128(2 * T * (1 - c), 2 * T))]
        dref = dst.at[(*full_, pl.ds(0, 2 * T), ds128(HALF * c, HALF))]
        return rcopy(sref, dref, i0, i0, (other, z))

    def from_heads_a_own(kind, src, dst, lid):
        full_ = [slice(None)] * (len(src.shape) - 2)
        sref = src.at[(*full_, ds128(2 * T * c, 2 * T))]
        dref = dst.at[(*full_, pl.ds(0, 2 * T), ds128(HALF * c, HALF))]
        return pltpu.make_async_copy(sref, dref, rs.at[lid])

    def from_heads_b(kind, src, j0, k):
        _, rid, sid = EX[kind]
        t = lax.rem(g + k, 4)
        n = src.shape[0]
        sref = src.at[:, ds128(T * t, T)]
        dref = fromb.at[g, pl.ds(0, n)]
        return rcopy(sref, dref, sid + k, rid + k, dev_of(t))

    def from_heads_b_own(src, lid):
        n = src.shape[0]
        return pltpu.make_async_copy(src.at[:, ds128(T * g, T)], fromb.at[g, pl.ds(0, n)], rs.at[lid])

    def wait_a(kind, dst, heads):
        full_ = [slice(None)] * (len(dst.shape) - 2)
        if heads:
            dref = dst.at[(*full_, ds128(2 * T * (1 - c), 2 * T))]
        else:
            dref = dst.at[(*full_, pl.ds(0, 2 * T), ds128(HALF * (1 - c), HALF))]
        recv(dref, EX[kind][0])

    def wait_b_heads(kind, dst):
        full_ = [slice(None)] * (len(dst.shape) - 2)
        for k in (1, 2, 3):
            recv(dst.at[(*full_, ds128(T * lax.rem(g + 4 - k, 4), T))], EX[kind][1] + k)

    def wait_b_tokens(kind, n):
        for k in (1, 2, 3):
            recv(fromb.at[lax.rem(g + 4 - k, 4), pl.ds(0, n)], EX[kind][1] + k)

    def merge_b(dst, j, n_from):
        for q in range(2):
            lo, hi = fromb[2 * q, n_from], fromb[2 * q + 1, n_from]
            at = q * HALF
            dst[j, 2 * T : 3 * T, at : at + 128] = lo[:, 0:128]
            dst[j, 2 * T : 3 * T, at + 128 : at + 256] = jnp.where(lane < 64, lo[:, 128:256], hi[:, 0:128])
            dst[j, 2 * T : 3 * T, at + 256 : at + 384] = hi[:, 128:256]

    for m in range(3):
        move_out_done(m, att.at[0, pl.ds(m * T, T)], rows, S_ROWS, I_ROWS)
    project(2)
    xb = [to_heads_b("qkv", qkv, qkvb, k) for k in (1, 2, 3)]
    for d in xb:
        d.start()
    lb = to_heads_b_own("qkv", qkv, qkvb, L0 + 1)
    lb.start()

    @pl.loop(0, 2)
    def _(s):
        project(s)

    xa = to_heads_a("qkv", qkv, qkva)
    xa.start()
    la = to_heads_a_own("qkv", qkv, qkva, L0)
    la.start()

    def weights_ready(step):
        if not aligned:
            return
        if step == 0:
            z_wait("D", 1)
            z_send("D", 2)
            for a in (U_, O_):
                ag2(a)
        elif step == 1:
            z_wait("D", 2)
            z_send("D", 3)
            send_cot()
            for a in (U_, O_):
                ag3(a)
        elif step == 2:
            z_wait("D", 3)
            unflatten(D_, dp)
            ag1(D_)
        elif step == 3:
            ag2(D_)
        elif step == 4:
            for a in (U_, O_):
                ag4(a)
        elif step == 5:
            ag3(D_)
        elif step == 6:
            ag4(D_)
            for key in CH:
                for k in (1, 2, 3):
                    z_send(key, k, done=True)

    def key_bias(slot):
        parts = []
        at = lax.broadcasted_iota(i32, (T, 128), 0).astype(f32)
        for b in range(4):
            limit = cnt[slot, b : b + 1, :].astype(f32)
            parts.append(jnp.where(at < limit, 0.0, NEG))
        return jnp.concatenate(parts, axis=0).astype(bf16)

    bias = R["bias"]
    bias[0] = key_bias(0)
    bias[1] = key_bias(2)
    QT = 256
    N = 4 * T

    def half(i, x):
        return jnp.where(lane // 64 == i, x, jnp.zeros_like(x))

    def key_side(k2, b, i):
        spot = 64 * (1 - i)
        return jnp.where(lane // 64 == i, k2, jnp.where(lane == spot, b, jnp.zeros_like(b)))

    def query_side(q2, i):
        spot = 64 * (1 - i)
        return jnp.where(lane // 64 == i, q2, jnp.where(lane == spot, 1.0, 0.0).astype(bf16))

    SC = 0.125 * LOG2E

    def attend(src, dst, col, bi, sel, lrow):
        cols = ds128(col, 128)
        k2 = src[1, :, cols]
        b = bias[bi]
        keys = [key_side(k2, b, i) for i in sel]

        @pl.loop(0, N // QT)
        def _(q):
            r = ds128(q * QT, QT)
            q2 = src[0, r, cols]
            v2 = src[2, :, cols]
            outs = []
            for n, i in enumerate(sel):
                s = nt(query_side(q2, i), keys[n])
                top = jnp.max(s, axis=1, keepdims=True) * SC
                p = jnp.exp2(s * SC - top)
                total = jnp.sum(p, axis=1, keepdims=True)
                outs.append(nn(p.astype(bf16), v2) / total)
                full_total = jnp.broadcast_to(top + jnp.log2(total), (QT, 128)).T
                lse[pl.ds(lrow + n, 1), r] = full_total[0:1, :]
            if len(sel) == 2:
                o = jnp.where(lane < 64, outs[0], outs[1])
            else:
                o = jnp.where(lane // 64 == sel[0], outs[0], 0.0)
            dst[0, r, cols] = o.astype(bf16)

    la.wait()
    wait_a("qkv", qkva, True)

    for t in range(3):
        attend(qkva, atta, t * 128, 0, (0, 1), 2 * t)
        weights_ready(t)
    xatt = from_heads_a("att", atta, att)
    xatt.start()
    latt = from_heads_a_own("att", atta, att, L0 + 2)
    latt.start()
    lb.wait()
    wait_b_heads("qkv", qkvb)
    attend(qkvb, attb, c * 128, 1, (0, 1), 6)
    weights_ready(3)
    attend(qkvb, attb, (1 - c) * 128, 1, (c,), 8)
    xattb = [from_heads_b("att", attb, 0, k) for k in (1, 2, 3)]
    for d in xattb:
        d.start()
    lattb = from_heads_b_own(attb, L0 + 3)
    lattb.start()
    weights_ready(4)
    xa.wait_send()
    for d in xb:
        d.wait_send()
    latt.wait()
    wait_a("att", att, False)

    def slot_rows(s):
        return pl.ds(mult(s * T, T), T)

    def live_of(s):
        b = 2 * c + s if s < 2 else g
        at = lax.broadcasted_iota(i32, (T, 128), 0).astype(f32)
        pick = jnp.zeros((1, 128), f32)
        for i in range(4):
            pick = pick + jnp.where(b == i, cnt[s, i : i + 1, :].astype(f32), 0.0)
        return jnp.where(at < pick, 1.0, 0.0)[:, 0:1]

    for s in range(3):
        if s == 2:
            lattb.wait()
            wait_b_tokens("att", 1)
            merge_b(att, 0, 0)
            weights_ready(5)
        r = pl.ds(s * T, T)
        v = nn(att[0, r, :], wblock(R["wo"])) + vec(V_OB) + rows[s].astype(f32)
        mid[r, :] = v
        n, _ = normalise(v)
        nbuf[s] = (n * vec(V_MG) + vec(V_MS)).astype(bf16)
    weights_ready(6)
    for s in (2, 0, 1):
        recv(cot.at[s], I_COT + s)
        o = live_of(s) * cot[s].astype(f32)
        cot[s] = o.astype(bf16)
        part = col_sum(o)
        if s == 2:
            vg[V_DB : V_DB + 1, :] = part
        else:
            vg[V_DB : V_DB + 1, :] += part

    FT = FR

    def feed(res, gn2, n2t, tile):
        act_s, gh_s = tile.at[0], tile.at[1]
        for s in range(3):
            n2t[:, s * T : (s + 1) * T] = nbuf[s].T
        res[...] = jnp.zeros_like(res)
        gn2[...] = jnp.zeros_like(gn2)
        outer = branch = cot
        ub = R["ub"]

        def tile_pair(i):
            @pl.loop(2 * i, 2 * i + 2)
            def _(j):
                one_tile(j)

        def one_tile(j):
            cols = ds128(j * FT, FT)
            up = wblock(R["wu"], cols)
            down = R["wd"][j]
            ub_j = ub[pl.ds(j, 1), :]

            @pl.loop(0, 3, init_carry=jnp.zeros((1, FT), f32))
            def bias_part(s, carry):
                r = slot_rows(s)
                hid = nn(nbuf[s], up) + ub_j
                phi_c = 0.5 * (1.0 + lax.erf(hid * 0.7071067811865476))
                act_low = (hid * phi_c).astype(bf16)
                act_s[r, :] = act_low
                res[r, :] += nn(act_low, down)
                slope = phi_c + hid * jnp.exp2(hid * hid * (-0.5 * LOG2E)) * 0.3989422804014327
                gh = (nt(outer[s], down) * slope).astype(bf16)
                gh_s[r, :] = gh
                gn2[r, :] += nt(gh, up)
                return carry + col_sum(gh.astype(f32))

            ub[pl.ds(j, 1), :] = bias_part
            R["wd"][j] = tn(act_s[...], outer[...].reshape(3 * T, W)).astype(bf16)
            R["wu"][:, :, cols] = nn(n2t[...], gh_s[...]).astype(bf16).reshape(dps, KR, FT)

        for i in range(dps // 2):
            tile_pair(i)
            if aligned:
                rs_core("D", i).start()
                if i == 1 or i == 3:
                    rs1("U%d" % (i // 2))
                if i > 0:
                    rs2_pair("D", i - 1)
                if i == 2:
                    rs2("U0")

        for s in (2, 0, 1):
            r = pl.ds(s * T, T)
            v = mid[r, :]
            y = live_of(s) * (v + res[r, :] + vec(V_DB))
            n2t[r, :] = y.astype(bf16)
            n, inv = normalise(v)
            e_ = gn2[r, :]
            gm = outer[s].astype(f32) + norm_back(e_, n, inv, vec(V_MG))
            mid[r, :] = gm
            low = gm.astype(bf16)
            branch[s] = low
            for i, part in ((V_MG, col_sum(e_ * n)), (V_MS, col_sum(e_)), (V_OB, col_sum(low.astype(f32)))):
                if s == 2:
                    vg[i : i + 1, :] = part
                else:
                    vg[i : i + 1, :] += part
            nbuf[s] = nt(low, wblock(R["wo"])).astype(bf16)
            send_do(s)
        for q in range(2):
            piece = tn(att[0, :, q * HALF : (q + 1) * HALF], branch[...].reshape(3 * T, W)).astype(bf16)
            R["wo"][q * (dps // 2) : (q + 1) * (dps // 2)] = piece.reshape(dps // 2, KR, W)
        att[0] = n2t[...]
        for s in (2, 0, 1):
            move_home(s, att.at[0, pl.ds(s * T, T)], act, S_ACT, I_ACT)
        grads_move(0)

    def act_done():
        for s in range(3):
            move_home_done(s, att.at[0, pl.ds(s * T, T)], act, S_ACT, I_ACT)

    do3 = R["nbuf"]

    def do_copies(s):
        if s < 2:
            i0 = EX["do"][0] if s == 0 else L0 + 4
            return [rcopy(do3.at[s, :, ds128(HALF * (1 - c), HALF)], doa.at[ds128(2 * T * c + s * T, T)], i0, i0, (other, z))]
        out = []
        for k in (1, 2, 3):
            t = lax.rem(g + k, 4)
            cols = ds128(HALF * lax.div(t, 2) + 128 * lax.rem(t, 2), 256)
            out.append(rcopy(do3.at[2, :, cols], dob.at[ds128(T * g, T)], EX["do"][2] + k, EX["do"][1] + k, dev_of(t)))
        return out

    def send_do(s):
        for d in do_copies(s):
            d.start()

    def grads_move(step):
        if not aligned:
            return
        if step == 0:
            rs1("O")
            rs2_pair("D", 3)
            rs3("U0")
            rs2("U1")
            rs3("D")
        elif step == 1:
            rs2("O")
            rs4("U0")
            rs3("U1")
        elif step == 2:
            rs4("D")
            rs3("O")
            y_send("U0", 2)
        elif step == 3:
            rs4("U1")
            y_send("D", 2)
            y_send("U0", 3)
        elif step == 4:
            rs4("O")
            y_send("D", 3)
            y_send("U1", 2)
            y_final("U0")
        elif step == 5:
            y_send("O", 2)
            y_send("U1", 3)
            y_final("D")
        elif step == 6:
            y_send("O", 3)
            y_final("U1")
            y_final("O")

    per = W // FT
    for q in range(dps):
        R["ub"][q : q + 1, :] = vt[V_UB + q // per : V_UB + q // per + 1, (q % per) * FT : (q % per + 1) * FT]
    pl.run_scoped(
        feed,
        pltpu.VMEM((3 * T, W), f32),
        pltpu.VMEM((3 * T, W), f32),
        pltpu.VMEM((W, 3 * T), bf16),
        pltpu.VMEM((2, 3 * T, FT), bf16),
    )
    for q in range(dps):
        vg[V_UB + q // per : V_UB + q // per + 1, (q % per) * FT : (q % per + 1) * FT] = R["ub"][q : q + 1, :]

    for j in range(2):
        doa[ds128(2 * T * c + j * T, T), :] = do3[j, :, ds128(HALF * c, HALF)]
    dob[ds128(T * g, T), :] = do3[2, :, ds128(HALF * e + 128 * c, 256)]
    recv(doa.at[ds128(2 * T * (1 - c), T)], EX["do"][0])
    recv(doa.at[ds128(2 * T * (1 - c) + T, T)], L0 + 4)

    def attend_back(src, o_ref, d_ref, col, bi, sel, lrow, dk, dv, delta):
        cols = ds128(col, 128)
        k2 = src[1, :, cols]
        v2 = src[2, :, cols]
        kt = k2.T
        b = bias[bi]
        keys = [key_side(k2, b, i) for i in sel]
        dk[...] = jnp.zeros_like(dk)
        dv[...] = jnp.zeros_like(dv)
        prod = o_ref[0, :, cols].astype(f32) * d_ref[:, cols].astype(f32)
        hi = prod.astype(bf16)
        lo = (prod - hi.astype(f32)).astype(bf16)
        row = lax.broadcasted_iota(i32, (8, 128), 0)
        if len(sel) == 2:
            pickm = (row == lax.broadcasted_iota(i32, (8, 128), 1) // 64).astype(f32).astype(bf16)
        else:
            pickm = jnp.where(jnp.logical_and(row == 0, lane // 64 == sel[0]), 1.0, 0.0).astype(bf16)
        delta[...] = nt(pickm, hi) + nt(pickm, lo)

        @pl.loop(0, N // QT)
        def _(q):
            r = ds128(q * QT, QT)
            q2 = src[0, r, cols]
            d2 = d_ref[r, cols]
            dks, dvs, dqs = [], [], []
            for n, i in enumerate(sel):
                qm, dm = half(i, q2), half(i, d2)
                s = nt(keys[n], query_side(q2, i))
                p = jnp.exp2(s * SC - lse[pl.ds(lrow + n, 1), r])
                dp_ = nt(v2, dm)
                ds_ = (p * (dp_ - delta[pl.ds(n, 1), r])).astype(bf16)
                dvs.append(nn(p.astype(bf16), dm))
                dks.append(nn(ds_, qm))
                dqs.append(nn(kt, ds_).T if len(sel) == 1 else nn(kt[64 * i : 64 * i + 64], ds_))
            if len(sel) == 2:
                dk[...] += dks[0] + dks[1]
                dv[...] += dvs[0] + dvs[1]
                dq = jnp.concatenate(dqs, axis=0).T
            else:
                dk[...] += dks[0]
                dv[...] += dvs[0]
                dq = half(sel[0], dqs[0])
            src[0, r, cols] = (dq * 0.125).astype(bf16)

        src[1, :, cols] = (dk[...] * 0.125).astype(bf16)
        src[2, :, cols] = dv[...].astype(bf16)

    def back(dk, dv, delta):
        attend_back(qkva, atta, doa, 0, 0, (0, 1), 0, dk, dv, delta)
        grads_move(1)
        for k in (1, 2, 3):
            recv(dob.at[ds128(T * lax.rem(g + 4 - k, 4), T)], EX["do"][1] + k)
        attend_back(qkvb, attb, dob, c * 128, 1, (0, 1), 6, dk, dv, delta)
        grads_move(2)
        attend_back(qkvb, attb, dob, (1 - c) * 128, 1, (c,), 8, dk, dv, delta)
        for d in xattb:
            d.wait_send()
        for k in (1, 2, 3):
            from_heads_b("dqkv", qkvb, 0, k).start()
        from_heads_b_own(qkvb, L0 + 6).start()
        grads_move(3)
        attend_back(qkva, atta, doa, 128, 0, (0, 1), 2, dk, dv, delta)
        grads_move(4)
        attend_back(qkva, atta, doa, 256, 0, (0, 1), 4, dk, dv, delta)

    pl.run_scoped(back, pltpu.VMEM((N, 128), f32), pltpu.VMEM((N, 128), f32), pltpu.VMEM((8, N), f32))
    xdq = from_heads_a("dqkv", qkva, qkv)
    xdq.start()
    ldq = from_heads_a_own("dqkv", qkva, qkv, L0 + 5)
    ldq.start()
    grads_move(5)
    xatt.wait_send()
    for s in range(3):
        for d in do_copies(s):
            d.wait_send()

    gsend = cot
    for s in range(3):
        normed_rows(s)

    def rows_grad(s):
        r = pl.ds(s * T, T)
        v = nt(qkv[0, r, :], wblock(R["wq"], slice(0, W)))
        v += nt(qkv[1, r, :], wblock(R["wq"], slice(W, 2 * W)))
        return v + nt(qkv[2, r, :], wblock(R["wq"], slice(2 * W, 3 * W)))

    def rows_back(s, e_):
        r = pl.ds(s * T, T)
        n, inv = normalise(rows[s].astype(f32))
        gsend[s] = (mid[r, :] + norm_back(e_, n, inv, vec(V_NG))).astype(bf16)
        move_home(s, gsend.at[s], grh, S_GR, I_GR)
        parts = (
            (V_NG, col_sum(e_ * n)),
            (V_NS, col_sum(e_)),
            (V_QB, col_sum(qkv[0, r, :].astype(f32))),
            (V_VB, col_sum(qkv[2, r, :].astype(f32))),
        )
        for i, part in parts:
            if s == 2:
                vg[i : i + 1, :] = part
            else:
                vg[i : i + 1, :] += part

    for m in range(3):
        move_out_done(m, R["cnth"].at[m], cnt, S_CNT, I_CNT)
        move_out_done(m, R["cotangent"].at[m], cot, S_COT, I_COT)
    from_heads_b_own(qkvb, L0 + 6).wait()
    wait_b_tokens("dqkv", 3)
    for j in range(3):
        merge_b(qkv, j, j)
    rows_back(2, rows_grad(2))
    ldq.wait()
    wait_a("dqkv", qkv, False)
    vg[12:16, :] = jnp.zeros((4, W), f32)

    def qkv_grad(j):
        w = tn(nbuf[...].reshape(3 * T, W), qkv[j]).astype(bf16)
        R["wq"][:, :, j * W : (j + 1) * W] = w.reshape(dps, KR, W)
        if aligned:
            rs1("Q%d" % j)

    if aligned:
        vx = R["vx"]
        I_VEC = take(3)
        I_VEZ = take(4)
        pairs = (other, dp + dx, dp + dy)

    def vec_copy(i):
        return rcopy(vg, vx.at[i], I_VEC + i, I_VEC + i, (pairs[i], z))

    def vec_add(i):
        vec_copy(i).wait()
        vg[...] += vx[i]

    def vec_z(k):
        return rcopy(vg, vx.at[2 + k], I_VEZ + k, I_VEZ + k, (dp, lax.rem(z + k, 4)))

    def back_last(ebuf):
        for s in range(2):
            ebuf[s] = rows_grad(s)
        qkv_grad(2)
        qkv_grad(1)
        if aligned:
            rs2("Q2")
        qkv_grad(0)
        if aligned:
            rs2("Q1")
        rows_back(0, ebuf[0])
        if aligned:
            rs3("Q2")
            rs2("Q0")
        rows_back(1, ebuf[1])
        if aligned:
            vec_copy(0).start()
            rs3("Q1")
            rs4("Q2")
            vec_add(0)
            vec_copy(1).start()
            rs3("Q0")
            grads_move(6)
            rs4("Q1")
            y_send("Q2", 2)
            vec_add(1)
            vec_copy(2).start()
            rs4("Q0")
            y_send("Q1", 2)
            y_send("Q2", 3)
            vec_add(2)
            for k in (1, 2, 3):
                vec_z(k).start()
            y_send("Q0", 2)
            y_send("Q1", 3)
            y_final("Q2")
            y_send("Q0", 3)
            y_final("Q1")
            for k in (1, 2, 3):
                recv(vx.at[2 + k], I_VEZ + k)
            for k in (1, 2, 3):
                vec_z(k).wait_send()
            total = vg[...]
            for k in (1, 2, 3):
                total = total + vx[2 + k]
            at = dp * 4 + z
            n1, n2 = W // 32, F // 32
            R["vs"][...] = pltpu.roll(total, lax.rem(W - at * n1, W), axis=1)[:, 0:128]
            line = lax.broadcasted_iota(i32, (16, W), 0)
            per_row = W // n2
            ubr = jnp.sum(jnp.where(line == V_UB + lax.div(at, per_row), total, 0.0), axis=0, keepdims=True)
            ubr = jnp.broadcast_to(ubr, (8, W))
            R["vs"][8:16, :] = pltpu.roll(ubr, lax.rem(W - lax.rem(at, per_row) * n2, W), axis=1)[:, 0:128]
            y_final("Q0")
            for key in GC:
                rs_done(key)

    pl.run_scoped(back_last, pltpu.VMEM((2, T, W), f32))
    if not aligned:
        save = [pltpu.make_async_copy(arrays[i], R[n], rs.at[L0 + 8 + i]) for i, n in enumerate(("gq", "go", "gu", "gd"))]
        for d in save:
            d.start()
        for d in save:
            d.wait()
    xdq.wait_send()
    for k in (1, 2, 3):
        from_heads_b("dqkv", qkvb, 0, k).wait_send()
    act_done()
    for s in range(3):
        move_home_done(s, gsend.at[s], grh, S_GR, I_GR)
    for m in range(3):
        arrived_home(m, act, I_ACT)
        arrived_home(m, grh, I_GR)
    assert count[0] <= cfg["sems"], count[0]


def finish_kernel(sizes, keep, grads, act_in, *refs):
    n = 0 if sizes is None else 5
    act_out, out = refs[n], refs[n + 1]
    places = lax.broadcasted_iota(i32, (out.shape[1], keep.shape[2]), 0)
    out[0] = nn((places == keep[0]).astype(f32).astype(bf16), grads[0])
    act_out[...] = act_in[...]
    if sizes is not None:

        @pl.when(pl.program_id(0) == 0)
        def _():
            for i in range(4):
                refs[n + 2 + i][...] = refs[i][...]
            for i, width in enumerate(sizes):
                refs[n + 6 + i][...] = refs[4][i : i + 1, 0:width]


def body(patches, keep_index, shard_counts, cotangent, *shards):
    ng, ns, wq, qb, vb, wo, ob, mg, ms, wu, ub, wd, db = shards
    batches, _, patch, width = patches.shape
    tokens = keep_index.shape[2]
    dp_size, blk_size = lax.axis_size("dp"), lax.axis_size("blk")
    devices = dp_size * blk_size
    ff = wu.shape[1]
    aligned = dp_size == 8 and blk_size == 4
    dps = 8
    kr, fr = width // dps, ff // dps
    vectors = jnp.stack([ng, ns, qb, vb, ob, mg, ms, db])
    if aligned:
        own = jnp.pad(vectors, ((0, 0), (0, 128 - vectors.shape[1])))
        own_ub = jnp.pad(ub[None], ((0, 7), (0, 128 - ub.shape[0])))
        table = jnp.concatenate([own, own_ub])
        weights = (wq, wo, wu, wd)
        pieces = [w.size // 128 for w in weights] + [16]
        flat = [sum(pieces[:i]) for i in range(6)]
    else:
        axes = ("dp", "blk")
        table = lax.all_gather(vectors, axes, axis=1, tiled=True).astype(f32)
        table_ub = lax.all_gather(ub, axes, axis=0, tiled=True).astype(f32).reshape(ff // width, width)
        table = jnp.concatenate([table, table_ub, jnp.zeros((16 - 8 - ff // width, width), f32)])
        weights = tuple(lax.all_gather(w, axes, axis=0, tiled=True) for w in (wq, wo, wu, wd))
        weights = tuple(w.reshape(dps, -1, w.shape[1]) for w in weights)
        flat = None
    cfg = dict(aligned=aligned, dps=dps, tokens=tokens, width=width, ff=ff, patch=patch, flat=flat, sems=320)
    keep = keep_index
    ins = [
        ("patches", patches[:, 0], ANY),
        ("keep", keep, VMEM),
        ("counts", shard_counts[:, 0], SMEM),
        ("cotangent", cotangent[:, 0], ANY),
    ]
    ins += [(n, w, VMEM if aligned else ANY) for n, w in zip(("sq", "so", "su", "sd"), weights)]
    ins.append(("sv", table, VMEM))
    out = [
        ("act", (3, tokens, width), bf16, ANY),
        ("grh", (3, tokens, width), bf16, ANY),
        ("vg", (16, width), f32, VMEM),
    ]
    full = {"q": (dps, kr, 3 * width), "o": (dps, kr, width), "u": (dps, kr, ff), "d": (dps, fr, width)}
    for i, n in enumerate("qoud"):
        if aligned:
            out.append(("g" + n, weights[i].shape, f32, VMEM))
        else:
            out.append(("g" + n, full[n], bf16, ANY))
    if aligned:
        out.append(("vs", (16, 128), f32, VMEM))
    t3 = 3 * tokens
    scratch = [("w" + n, full[n], bf16) for n in "qoud"]
    scratch += [
        ("rows", (3, tokens, width), bf16),
        ("cot", (3, tokens, width), bf16),
        ("cnt", (3, 16, 128), bf16),
        ("cnth", (3, 16, 128), bf16),
        ("nbuf", (3, tokens, width), bf16),
        ("qkv", (3, t3, width), bf16),
        ("qkva", (3, 4 * tokens, width // 2), bf16),
        ("qkvb", (3, 4 * tokens, 256), bf16),
        ("atta", (1, 4 * tokens, width // 2), bf16),
        ("attb", (1, 4 * tokens, 256), bf16),
        ("att", (1, t3, width), bf16),
        ("fromb", (4, 3, tokens, 256), bf16),
        ("doa", (4 * tokens, width // 2), bf16),
        ("dob", (4 * tokens, 256), bf16),
        ("mid", (t3, width), f32),
        ("vt", (16, width), f32),
        ("lse", (16, 4 * tokens), f32),
        ("bias", (2, 4 * tokens, 128), bf16),
        ("ub", (dps, fr), f32),
    ]
    if aligned:
        scratch += [
            ("zbuf", (4, flat[5], 128), bf16),
            ("zrr", (3, flat[4], 128), bf16),
            ("zrl", (3, flat[4], 128), bf16),
            ("vw", (dps, 64, 128), bf16),
            ("vx", (6, 16, width), f32),
        ]
        scratch += [("rb1" + n, (4, *full[n][1:]), bf16) for n in "qoud"]
        scratch += [("rb2" + n, (3, *full[n][1:]), bf16) for n in "qoud"]
    names = [n for n, _, _ in scratch] + ["ss", "rs"]
    shapes = [pltpu.VMEM(s, d) for _, s, d in scratch] + [pltpu.SemaphoreType.DMA((cfg["sems"],))] * 2
    flops = 6 * 3 * tokens * (4 * width * width + 2 * width * ff)
    results = pl.pallas_call(
        functools.partial(layer_kernel, cfg, [n for n, _, _ in ins], [n for n, *_ in out], names),
        out_shape=[jax.ShapeDtypeStruct(s, d) for _, s, d, _ in out],
        in_specs=[s for _, _, s in ins],
        out_specs=[s for *_, s in out],
        scratch_shapes=shapes,
        compiler_params=pltpu.CompilerParams(collective_id=0, has_side_effects=True, vmem_limit_bytes=64 * 1024 * 1024 - 512 * 1024),
        cost_estimate=pl.CostEstimate(flops=flops, bytes_accessed=50_000_000, transcendentals=0),
        name="layer",
    )(*[a for _, a, _ in ins])
    act, grh, vg, gq, go, gu, gd = results[:7]
    whole = lambda v: pl.BlockSpec(v, lambda m: (0,) * len(v))
    step = lambda *v: pl.BlockSpec((1, *v), lambda m: (m, 0, 0))
    n = width // devices
    sizes = [n] * 8 + [ff // devices] if aligned else None
    extra = [gq, go, gu, gd, results[7]] if aligned else []
    shapes = [(3, tokens, width, bf16), (3, patch, width, f32)]
    specs = [step(tokens, width), step(patch, width)]
    if aligned:
        shapes += [(*v.shape, f32) for v in extra[:4]] + [(1, v, f32) for v in sizes]
        specs += [whole(v.shape) for v in extra[:4]] + [whole((1, v)) for v in sizes]
    done = pl.pallas_call(
        functools.partial(finish_kernel, sizes),
        grid=(3,),
        in_specs=[step(1, tokens), step(tokens, width), step(tokens, width)] + [whole(v.shape) for v in extra],
        out_specs=specs,
        out_shape=[jax.ShapeDtypeStruct(v[:-1], v[-1]) for v in shapes],
        compiler_params=pltpu.CompilerParams(vmem_limit_bytes=32 * 1024 * 1024),
        name="finish",
    )(keep, grh, act, *extra)
    act, patch_grad = done[:2]
    if aligned:
        gq, go, gu, gd = done[2:6]
        piece = [v.reshape(-1) for v in done[6:]]
    else:
        axes = ("dp", "blk")
        small = [vg[:8].reshape(8, devices, n).transpose(1, 0, 2).reshape(devices, -1), vg[8 : 8 + ff // width].reshape(devices, -1)]
        small = lax.psum_scatter(jnp.concatenate(small, axis=1), axes, scatter_dimension=0, tiled=True)[0]
        piece = [small[i * n : (i + 1) * n] for i in range(8)] + [small[8 * n :]]
        gq, go, gu, gd = (
            lax.psum_scatter(w.reshape(-1, w.shape[-1]).astype(f32), axes, scatter_dimension=0, tiled=True) for w in (gq, go, gu, gd)
        )
    return (
        act[:, None],
        patch_grad[:, None],
        piece[V_NG],
        piece[V_NS],
        gq,
        piece[V_QB],
        piece[V_VB],
        go,
        piece[V_OB],
        piece[V_MG],
        piece[V_MS],
        gu,
        piece[V_UB],
        gd,
        piece[V_DB],
    )


def solution(mesh):
    vec, mat = P(("dp", "blk")), P(("dp", "blk"), None)
    tok = P(None, "dp", "blk", None)
    params = (vec, vec, mat, vec, vec, mat, vec, vec, vec, mat, vec, mat, vec)
    in_specs = (tok, P(None, "dp", "blk"), P(None, "dp", None), tok) + params
    out_specs = (tok, tok) + params
    return jax.shard_map(body, mesh=mesh, in_specs=in_specs, out_specs=out_specs, check_vma=False)
```

```python
import functools

import jax
import jax.numpy as jnp
from jax import lax
from jax.experimental import pallas as pl
from jax.experimental.pallas import tpu as pltpu
from jax.sharding import PartitionSpec as P

MESH = pl.DeviceIdType.MESH
ANY = pl.BlockSpec(memory_space=pl.ANY)
VMEM = pl.BlockSpec(memory_space=pltpu.VMEM)
SMEM = pl.BlockSpec(memory_space=pltpu.SMEM)
f32, bf16, i32 = jnp.float32, jnp.bfloat16, jnp.int32

EPSILON = 1e-06
LOG2E = 1.4426950408889634
NEG = -1e30


def nn(a, b):
    return lax.dot_general(a, b, (((1,), (0,)), ((), ())), preferred_element_type=f32)


def nt(a, b):
    return lax.dot_general(a, b, (((1,), (1,)), ((), ())), preferred_element_type=f32)


def tn(a, b):
    return lax.dot_general(a, b, (((0,), (0,)), ((), ())), preferred_element_type=f32)


def mult(x, k):
    return x if isinstance(x, int) else pl.multiple_of(x, k)


def normalise(v):
    centred = v - jnp.mean(v, axis=1, keepdims=True)
    inv = lax.rsqrt(jnp.mean(centred * centred, axis=1, keepdims=True) + EPSILON)
    return centred * inv, inv


def norm_back(e, n, inv, gain):
    f = e * gain
    return inv * (f - jnp.mean(f, axis=1, keepdims=True) - n * jnp.mean(f * n, axis=1, keepdims=True))


def col_sum(v):
    return jnp.sum(v, axis=0, keepdims=True)


def group_tile(t):
    return t % 3 * 6 + t // 6 * 2 + t % 6 // 3


def natural_tile(p):
    return p % 6 // 2 * 6 + p % 2 * 3 + p // 6


V_NG, V_NS, V_QB, V_VB, V_OB, V_MG, V_MS, V_DB, V_UB = range(9)


def layer_kernel(cfg, names_in, names_out, names_scratch, *refs):
    R = dict(zip(names_in + names_out + names_scratch, refs, strict=True))
    aligned, dps = cfg["aligned"], cfg["dps"]
    T, W, F = cfg["tokens"], cfg["width"], cfg["ff"]
    KR = W // dps
    FR = F // dps
    HALF = W // 2
    dp, z = lax.axis_index("dp"), lax.axis_index("blk")
    c = lax.rem(dp, 2)
    base = dp - c
    h, e = lax.div(z, 2), lax.rem(z, 2)
    g = 2 * e + c
    other = base + 1 - c
    ss, rs = R["ss"], R["rs"]
    count = [0]

    def take(n=1):
        count[0] += n
        return count[0] - n

    def rcopy(src, dst, s, r, dev):
        return pltpu.make_async_remote_copy(
            src_ref=src, dst_ref=dst, send_sem=ss.at[s], recv_sem=rs.at[r], device_id=dev, device_id_type=MESH
        )

    def recv(dst, r, dev=None):
        rcopy(dst, dst, 0, r, (other, z) if dev is None else dev).wait_recv()

    bar = pltpu.get_barrier_semaphore()
    peers = []
    for k in range(1, 8):
        j = lax.rem(c * 4 + z + k, 8)
        peers.append((base + lax.div(j, 4), lax.rem(j, 4)))
    if aligned:
        dx = 2 - 4 * lax.rem(lax.div(dp, 2), 2)
        dy = 4 - 8 * lax.div(dp, 4)
        p1, p2, p3 = dp + (1 - c) * dx + c * dy, dp + c * dx + (1 - c) * dy, dp + dx + dy
        peers += [(p1, z), (p2, z)]
    for dev in peers:
        pl.semaphore_signal(bar, inc=1, device_id=dev, device_id_type=MESH)

    def owner(m):
        if m < 2:
            return lax.div(z, 2), 2 * c + m, lax.rem(z, 2)
        return lax.rem(z, 2), 2 * c + lax.div(z, 2), 2

    def home(s):
        if s < 2:
            return h, 2 * c + s
        return h, 2 * e + c

    def move_out(m, src, dst, sid, rid):
        tc, tz, slot = owner(m)
        own = jnp.logical_and(tc == c, tz == z)

        @pl.when(own)
        def _():
            pltpu.make_async_copy(src, dst.at[slot], rs.at[rid + slot]).start()

        @pl.when(jnp.logical_not(own))
        def _():
            rcopy(src, dst.at[slot], sid + m, rid + slot, (base + tc, tz)).start()

    def move_out_done(m, src, dst, sid, rid):
        tc, tz, slot = owner(m)
        own = jnp.logical_and(tc == c, tz == z)

        @pl.when(jnp.logical_not(own))
        def _():
            rcopy(src, dst.at[slot], sid + m, rid + slot, (base + tc, tz)).wait_send()

    def move_home(s, src, dst, sid, rid):
        tc, tz = home(s)
        m = e if s < 2 else 2
        own = jnp.logical_and(tc == c, tz == z)

        @pl.when(own)
        def _():
            pltpu.make_async_copy(src, dst.at[m], ss.at[sid + s]).start()

        @pl.when(jnp.logical_not(own))
        def _():
            rcopy(src, dst.at[m], sid + s, rid + m, (base + tc, tz)).start()

    def move_home_done(s, src, dst, sid, rid):
        tc, tz = home(s)
        m = e if s < 2 else 2
        own = jnp.logical_and(tc == c, tz == z)

        @pl.when(own)
        def _():
            pltpu.make_async_copy(src, dst.at[m], ss.at[sid + s]).wait()

        @pl.when(jnp.logical_not(own))
        def _():
            rcopy(src, dst.at[m], sid + s, rid + m, (base + tc, tz)).wait_send()

    def arrived_home(m, dst, rid):
        tc, tz, _ = owner(m)

        @pl.when(jnp.logical_not(jnp.logical_and(tc == c, tz == z)))
        def _():
            recv(dst.at[m], rid + m)

    arrays = [R["wq"], R["wo"], R["wu"], R["wd"]]
    Q_, O_, U_, D_ = 0, 1, 2, 3
    if aligned:
        zbuf, zrr, zrl = R["zbuf"], R["zrr"], R["zrl"]
        flat = cfg["flat"]
        CH = {"Q": (0, flat[1]), "OU": (flat[1], flat[3]), "D": (flat[3], flat[4]), "V": (flat[4], flat[5])}
        ZR = {k: take(3) - 1 for k in CH}
        ZL = {k: take(3) - 1 for k in CH}
        wide = W // 128
        GC = {"D": (D_, 0, wide), "O": (O_, 0, wide)}
        for i in range(2):
            GC["U%d" % i] = (U_, i * F // 256, (i + 1) * F // 256)
        for i in range(3):
            GC["Q%d" % i] = (Q_, i * wide, (i + 1) * wide)
        YR = {k: take(3) - 1 for k in GC}
        YL = {k: take(3) - 1 for k in GC}
        gathered = arrays + [R["vw"]]
        XY = [take(3) for _ in range(5)]
        CR = [take(4) for _ in range(5)]
        R1 = {k: take(4) for k in GC}
        R2 = {k: take(3) for k in GC}

        def z_send(key, k, done=False):
            r0, r1 = CH[key]
            rows = pl.ds(r0, r1 - r0)
            right = jnp.logical_and(z < 3, z - (k - 1) >= 0)
            left = jnp.logical_and(z > 0, z + (k - 1) <= 3)

            @pl.when(right)
            def _():
                ref = zbuf.at[z - (k - 1), rows]
                d = rcopy(ref, ref, ZR[key] + k, ZR[key] + k, (dp, z + 1))
                d.wait_send() if done else d.start()

            @pl.when(left)
            def _():
                ref = zbuf.at[z + (k - 1), rows]
                d = rcopy(ref, ref, ZL[key] + k, ZL[key] + k, (dp, z - 1))
                d.wait_send() if done else d.start()

        def z_wait(key, k):
            r0, r1 = CH[key]
            rows = pl.ds(r0, r1 - r0)

            @pl.when(z - k >= 0)
            def _():
                recv(zbuf.at[z - k, rows], ZR[key] + k)

            @pl.when(z + k <= 3)
            def _():
                recv(zbuf.at[z + k, rows], ZL[key] + k)

        def flatten(a, ref, slot):
            if a == D_:
                n, rows = W // 128, FR // 4
            elif a == 4:
                n, rows = 1, 16
            else:
                n, rows = ref.shape[-1] // 128, KR // 4
            for t in range(n):
                cols = slice(t * 128, (t + 1) * 128)
                zbuf[slot, flat[a] + t * rows : flat[a] + (t + 1) * rows, :] = ref[:, cols]

        def place(a, t):
            return group_tile(t) if a == Q_ else t

        def unflatten(a, block):
            dst = gathered[a]
            if a == D_:
                n, rows = W // 128, FR // 4
            elif a == 4:
                n, rows = 1, 16
            else:
                n, rows = dst.shape[-1] // 128, KR // 4
            for s in range(4):
                for t in range(n):
                    p = place(a, t) * 128
                    dst[block, s * rows : (s + 1) * rows, p : p + 128] = zbuf[s, flat[a] + t * rows : flat[a] + (t + 1) * rows, :]

        def ag_copies(a):
            ref = gathered[a]

            def core(i):
                block = (dp, p1, p2, p3)[i]
                return rcopy(ref.at[block], ref.at[block], CR[a] + i, CR[a] + i, (other, z))

            return {
                "p1": lambda: rcopy(ref.at[dp], ref.at[dp], XY[a], XY[a], (p1, z)),
                "p2": lambda: rcopy(ref.at[dp], ref.at[dp], XY[a] + 1, XY[a] + 1, (p2, z)),
                "fw": lambda: rcopy(ref.at[p1], ref.at[p1], XY[a] + 2, XY[a] + 2, (p2, z)),
                "c0": lambda: core(0),
                "c1": lambda: core(1),
                "c2": lambda: core(2),
                "c3": lambda: core(3),
            }

        def ag1(a):
            d = ag_copies(a)
            d["p1"]().start()
            d["p2"]().start()
            d["c0"]().start()

        def ag2(a):
            d = ag_copies(a)
            ref = gathered[a]
            recv(ref.at[p1], XY[a])
            d["fw"]().start()
            d["c1"]().start()
            recv(ref.at[p2], XY[a] + 1)
            d["c2"]().start()

        def ag3(a):
            d = ag_copies(a)
            recv(gathered[a].at[p3], XY[a] + 2)
            d["c3"]().start()

        def ag4(a):
            d = ag_copies(a)
            for i, block in enumerate((dp, p2, p1, p3)):
                recv(gathered[a].at[block + other - dp], CR[a] + i)
            for k in d.values():
                k().wait_send()

        def blk_of(i):
            return 2 * i + c

        bufs1 = [R["rb1" + n] for n in "qoud"]
        bufs2 = [R["rb2" + n] for n in "qoud"]

        def cols_of(key):
            _, t0, t1 = GC[key]
            return pl.ds(t0 * 128, (t1 - t0) * 128)

        def block_of(key, block):
            return arrays[GC[key][0]].at[block, :, cols_of(key)]

        def view(bufs, key, i):
            return bufs[GC[key][0]].at[i, :, cols_of(key)]

        def rs_core(key, i):
            return rcopy(block_of(key, 2 * i + 1 - c), view(bufs1, key, i), R1[key] + i, R1[key] + i, (other, z))

        def rs1(key):
            for i in range(4):
                rs_core(key, i).start()

        def addto(key, block, parts):
            ref, cols = arrays[GC[key][0]], cols_of(key)
            rows = ref.shape[1]
            step = 48

            @pl.loop(0, rows // step)
            def _(q):
                r = pl.ds(mult(q * step, step), step)
                total = ref[block, r, cols].astype(f32)
                for p, i in parts:
                    total = total + p[GC[key][0]][i, r, cols].astype(f32)
                ref[block, r, cols] = total.astype(bf16)

        def rs_xy(key):
            i0 = R2[key]
            return {
                "diag": lambda: rcopy(block_of(key, p3), view(bufs2, key, 0), i0, i0, (p2, z)),
                "p2": lambda: rcopy(block_of(key, p2), view(bufs2, key, 1), i0 + 1, i0 + 1, (p2, z)),
                "p1": lambda: rcopy(block_of(key, p1), view(bufs2, key, 2), i0 + 2, i0 + 2, (p1, z)),
            }

        def rs2_pair(key, i):
            recv(view(bufs1, key, i), R1[key] + i)
            addto(key, blk_of(i), [(bufs1, i)])

            @pl.when(blk_of(i) == p3)
            def _():
                rs_xy(key)["diag"]().start()

            @pl.when(blk_of(i) == p2)
            def _():
                rs_xy(key)["p2"]().start()

        def rs2(key):
            for i in range(4):
                rs2_pair(key, i)

        def rs3(key):
            recv(view(bufs2, key, 0), R2[key])
            addto(key, p1, [(bufs2, 0)])
            rs_xy(key)["p1"]().start()

        def span(key):
            a, t0, t1 = GC[key]
            n = arrays[a].shape[1] // 4
            return a, n, flat[a] + t0 * n, (t1 - t0) * n

        def rs4(key):
            recv(view(bufs2, key, 1), R2[key] + 1)
            recv(view(bufs2, key, 2), R2[key] + 2)
            addto(key, dp, [(bufs2, 1), (bufs2, 2)])
            a, n, _, _ = span(key)
            for slot in range(4):
                for t in range(GC[key][1], GC[key][2]):
                    piece = arrays[a][dp, slot * n : (slot + 1) * n, t * 128 : (t + 1) * 128]
                    zbuf[slot, flat[a] + t * n : flat[a] + (t + 1) * n, :] = piece
            y_send(key, 1)

        def y_send(key, k, done=False):
            _, _, r0, rn = span(key)
            rows = pl.ds(r0, rn)
            to_right = z + 4 - k
            to_left = z - 4 + k

            @pl.when(jnp.logical_and(z < 3, to_right <= 3))
            def _():
                if k > 1 and not done:

                    @pl.when(z >= 1)
                    def _():
                        recv(zrr.at[k - 2, rows], YR[key] + k - 1)
                        zbuf[to_right, rows, :] = (zbuf[to_right, rows, :].astype(f32) + zrr[k - 2, rows, :].astype(f32)).astype(bf16)

                d = rcopy(zbuf.at[to_right, rows], zrr.at[k - 1, rows], YR[key] + k, YR[key] + k, (dp, z + 1))
                d.wait_send() if done else d.start()

            @pl.when(jnp.logical_and(z > 0, to_left >= 0))
            def _():
                if k > 1 and not done:

                    @pl.when(z <= 2)
                    def _():
                        recv(zrl.at[k - 2, rows], YL[key] + k - 1)
                        zbuf[to_left, rows, :] = (zbuf[to_left, rows, :].astype(f32) + zrl[k - 2, rows, :].astype(f32)).astype(bf16)

                d = rcopy(zbuf.at[to_left, rows], zrl.at[k - 1, rows], YL[key] + k, YL[key] + k, (dp, z - 1))
                d.wait_send() if done else d.start()

        def y_final(key):
            a, n, r0, rn = span(key)
            rows = pl.ds(r0, rn)

            @pl.when(z >= 1)
            def _():
                recv(zrr.at[2, rows], YR[key] + 3)

            @pl.when(z <= 2)
            def _():
                recv(zrl.at[2, rows], YL[key] + 3)

            for t in range(GC[key][1], GC[key][2]):
                piece = slice(flat[a] + t * n, flat[a] + (t + 1) * n)
                total = zbuf[z, piece, :].astype(f32)
                total = total + jnp.where(z >= 1, zrr[2, piece, :].astype(f32), 0.0)
                total = total + jnp.where(z <= 2, zrl[2, piece, :].astype(f32), 0.0)
                p = natural_tile(t) if a == Q_ else t
                outs[a][:, p * 128 : (p + 1) * 128] = total

        def rs_done(key):
            for k in (1, 2, 3):
                y_send(key, k, done=True)
            for i in range(4):
                rs_core(key, i).wait_send()
            for d in rs_xy(key).values():
                d().wait_send()

        outs = [R["gq"], R["go"], R["gu"], R["gd"]]

    I_ROWS, I_CNT, I_COT, I_ACT, I_GR = (take(3) for _ in range(5))
    S_ROWS, S_CNT, S_COT, S_ACT, S_GR = (take(3) for _ in range(5))
    EX = {}
    for k in ("qkv", "att", "do", "dqkv"):
        EX[k] = (take(1), take(4), take(4))
    L0 = take(12)

    rows, cot, cnt, nbuf = R["rows"], R["cot"], R["cnt"], R["nbuf"]
    qkv, qkva, qkvb = R["qkv"], R["qkva"], R["qkvb"]
    atta, attb, att, fromb = R["atta"], R["attb"], R["att"], R["fromb"]
    doa, dob, mid, vt, vg = R["doa"], R["dob"], R["mid"], R["vt"], R["vg"]
    lse, grh, keep, act, ysend = R["lse"], R["grh"], R["keep"], R["act"], R["ysend"]
    lane = lax.broadcasted_iota(i32, (1, 128), 1)

    if aligned:
        for a, name in enumerate(("sq", "so", "su", "sd", "sv")):
            flatten(a, R[name], z)
    for m in range(3):
        for b in range(4):
            R["cnth"][m, b : b + 1, :] = jnp.full((1, 128), R["counts"][m, b], i32).astype(f32).astype(bf16)
        R["cnth"][m, 4:, :] = jnp.zeros((12, 128), bf16)

    def pick_rows(pbuf, psem):
        copies = [pltpu.make_async_copy(R["patches"].at[m], pbuf.at[m], psem.at[m]) for m in range(3)]
        for d in copies:
            d.start()
        pl.semaphore_wait(bar, len(peers))
        if aligned:
            z_send("Q", 1)
            z_send("V", 1)
        for m in range(3):
            copies[m].wait()
            spread = (lax.broadcasted_iota(i32, (cfg["patch"], T), 0) == keep[m]).astype(f32).astype(bf16)
            att[0, m * T : (m + 1) * T, :] = tn(spread, pbuf[m]).astype(bf16)

    pl.run_scoped(pick_rows, pltpu.VMEM((3, cfg["patch"], W), bf16), pltpu.SemaphoreType.DMA((3,)))

    def send_rows():
        for m in (2, 0, 1):
            move_out(m, att.at[0, pl.ds(m * T, T)], rows, S_ROWS, I_ROWS)
            move_out(m, R["cnth"].at[m], cnt, S_CNT, I_CNT)

    def send_cot(ms=(2, 0, 1)):
        for m in ms:
            move_out(m, R["cotangent"].at[m], cot, S_COT, I_COT)

    if aligned:
        for key in "QV":
            z_wait(key, 1)
            z_send(key, 2)
        z_send("OU", 1)
        for key in "QV":
            z_wait(key, 2)
            z_send(key, 3)
        z_wait("OU", 1)
        z_send("OU", 2)
        z_send("D", 1)
        for key in "QV":
            z_wait(key, 3)
        unflatten(Q_, dp)
        ag1(Q_)
        unflatten(4, dp)
        ag1(4)
        z_wait("OU", 2)
        z_send("OU", 3)
        z_wait("D", 1)
        z_send("D", 2)
        z_wait("OU", 3)
        z_wait("D", 2)
        z_send("D", 3)
        send_rows()
    else:
        full = [pltpu.make_async_copy(R[n], arrays[i], rs.at[L0 + 8 + i]) for i, n in enumerate(("sq", "so", "su", "sd"))]
        for d in full:
            d.start()
        send_rows()
        send_cot()
    if aligned:
        ag2(Q_)
        ag2(4)
        for a in (U_, O_):
            unflatten(a, dp)
        ag3(Q_)
        ag3(4)
        ag4(4)
        ag4(Q_)
        for a in (U_, O_):
            ag1(a)
        v = R["vw"][...].reshape(32 * 16, 128)
        to = lax.broadcasted_iota(i32, (128, W), 1)
        frm = lax.broadcasted_iota(i32, (128, W), 0)
        dev = lax.broadcasted_iota(i32, (512, W), 0) // 16
        col = lax.broadcasted_iota(i32, (512, W), 1)
        n1, n2 = W // 32, F // 32
        x1 = nn(v, (lax.rem(to, n1) == frm).astype(f32).astype(bf16))
        x1 = jnp.where(dev == col // n1, x1, 0.0)
        vt[0:16, :] = jnp.sum(x1.reshape(32, 16, W), axis=0)
        x2 = nn(v, (lax.rem(to, n2) == frm).astype(f32).astype(bf16))
        x2 = jnp.where(lax.rem(dev, W // n2) == col // n2, x2, 0.0)
        x2 = jnp.sum(x2.reshape(4, 8, 16, W), axis=1)
        for q in range(4):
            vt[V_UB + q : V_UB + q + 1, :] = x2[q, V_UB : V_UB + 1, :]
    else:
        vt[...] = R["sv"][...]

    def vec(i):
        return vt[i : i + 1, :]

    def normed_rows(s):
        n, _ = normalise(rows[s].astype(f32))
        nbuf[s] = (n * vec(V_NG) + vec(V_NS)).astype(bf16)

    for s in (2, 0, 1):
        recv(rows.at[s], I_ROWS + s)
        recv(cnt.at[s], I_CNT + s)
        normed_rows(s)
    if not aligned:
        for d in full:
            d.wait()

    def wblock(ref, cols=None):
        v = ref[...] if cols is None else ref[:, :, cols]
        return v.reshape(-1, v.shape[-1])

    def group(t):
        return wblock(R["wq"], slice(t * W, (t + 1) * W))

    def project(s):
        r = pl.ds(mult(s * T, T), T)
        for t in range(3):
            v = nn(nbuf[s], group(t))
            for j in range(3):
                for k in range(2):
                    at = k * HALF + t * 128
                    x = v[:, (2 * j + k) * 128 : (2 * j + k + 1) * 128]
                    if j != 1:
                        row = V_QB if j == 0 else V_VB
                        x = x + vt[row : row + 1, at : at + 128]
                    qkv[j, r, at : at + 128] = x.astype(bf16)

    def dev_of(i):
        return (base + lax.rem(i, 2), 2 * h + lax.div(i, 2))

    def ds128(x, n):
        return pl.ds(mult(x, 128), n)

    def to_heads_a(kind, src, dst):
        i0 = EX[kind][0]
        full_ = [slice(None)] * (len(src.shape) - 2)
        sref = src.at[(*full_, pl.ds(0, 2 * T), ds128(HALF * (1 - c), HALF))]
        dref = dst.at[(*full_, ds128(2 * T * c, 2 * T))]
        return rcopy(sref, dref, i0, i0, (other, z))

    def to_heads_a_own(kind, src, dst, lid):
        full_ = [slice(None)] * (len(src.shape) - 2)
        sref = src.at[(*full_, pl.ds(0, 2 * T), ds128(HALF * c, HALF))]
        dref = dst.at[(*full_, ds128(2 * T * c, 2 * T))]
        return pltpu.make_async_copy(sref, dref, rs.at[lid])

    def to_heads_b(kind, src, dst, k):
        _, rid, sid = EX[kind]
        full_ = [slice(None)] * (len(src.shape) - 2)
        t = lax.rem(g + k, 4)
        sref = src.at[(*full_, pl.ds(2 * T, T), ds128(HALF * lax.div(t, 2) + 128 * lax.rem(t, 2), 256))]
        dref = dst.at[(*full_, ds128(T * g, T))]
        return rcopy(sref, dref, sid + k, rid + k, dev_of(t))

    def to_heads_b_own(kind, src, dst, lid):
        full_ = [slice(None)] * (len(src.shape) - 2)
        sref = src.at[(*full_, pl.ds(2 * T, T), ds128(HALF * e + 128 * c, 256))]
        dref = dst.at[(*full_, ds128(T * g, T))]
        return pltpu.make_async_copy(sref, dref, rs.at[lid])

    def from_heads_a(kind, src, dst):
        i0 = EX[kind][0]
        full_ = [slice(None)] * (len(src.shape) - 2)
        sref = src.at[(*full_, ds128(2 * T * (1 - c), 2 * T))]
        dref = dst.at[(*full_, pl.ds(0, 2 * T), ds128(HALF * c, HALF))]
        return rcopy(sref, dref, i0, i0, (other, z))

    def from_heads_a_own(kind, src, dst, lid):
        full_ = [slice(None)] * (len(src.shape) - 2)
        sref = src.at[(*full_, ds128(2 * T * c, 2 * T))]
        dref = dst.at[(*full_, pl.ds(0, 2 * T), ds128(HALF * c, HALF))]
        return pltpu.make_async_copy(sref, dref, rs.at[lid])

    def from_heads_b(kind, src, j0, k):
        _, rid, sid = EX[kind]
        t = lax.rem(g + k, 4)
        n = src.shape[0]
        sref = src.at[:, ds128(T * t, T)]
        dref = fromb.at[g, pl.ds(0, n)]
        return rcopy(sref, dref, sid + k, rid + k, dev_of(t))

    def from_heads_b_own(src, lid):
        n = src.shape[0]
        return pltpu.make_async_copy(src.at[:, ds128(T * g, T)], fromb.at[g, pl.ds(0, n)], rs.at[lid])

    def wait_a(kind, dst, heads):
        full_ = [slice(None)] * (len(dst.shape) - 2)
        if heads:
            dref = dst.at[(*full_, ds128(2 * T * (1 - c), 2 * T))]
        else:
            dref = dst.at[(*full_, pl.ds(0, 2 * T), ds128(HALF * (1 - c), HALF))]
        recv(dref, EX[kind][0])

    def wait_b_heads(kind, dst):
        full_ = [slice(None)] * (len(dst.shape) - 2)
        for k in (1, 2, 3):
            recv(dst.at[(*full_, ds128(T * lax.rem(g + 4 - k, 4), T))], EX[kind][1] + k)

    def wait_b_tokens(kind, n):
        for k in (1, 2, 3):
            recv(fromb.at[lax.rem(g + 4 - k, 4), pl.ds(0, n)], EX[kind][1] + k)

    def merge_b(dst, j, n_from):
        for q in range(2):
            lo, hi = fromb[2 * q, n_from], fromb[2 * q + 1, n_from]
            at = q * HALF
            dst[j, 2 * T : 3 * T, at : at + 128] = lo[:, 0:128]
            dst[j, 2 * T : 3 * T, at + 128 : at + 256] = jnp.where(lane < 64, lo[:, 128:256], hi[:, 0:128])
            dst[j, 2 * T : 3 * T, at + 256 : at + 384] = hi[:, 128:256]

    for m in range(3):
        move_out_done(m, att.at[0, pl.ds(m * T, T)], rows, S_ROWS, I_ROWS)
    project(2)
    xb = [to_heads_b("qkv", qkv, qkvb, k) for k in (1, 2, 3)]
    for d in xb:
        d.start()
    lb = to_heads_b_own("qkv", qkv, qkvb, L0 + 1)
    lb.start()

    @pl.loop(0, 2)
    def _(s):
        project(s)

    xa = to_heads_a("qkv", qkv, qkva)
    xa.start()
    la = to_heads_a_own("qkv", qkv, qkva, L0)
    la.start()

    def weights_ready(step):
        if not aligned:
            return
        if step == 0:
            for a in (U_, O_):
                ag2(a)
        elif step == 1:
            send_cot((2,))
        elif step == 2:
            z_wait("D", 3)
            unflatten(D_, dp)
            ag1(D_)
        elif step == 3:
            for a in (U_, O_):
                ag3(a)
            ag2(D_)
        elif step == 4:
            send_cot((0, 1))
            for a in (U_, O_):
                ag4(a)
        elif step == 5:
            ag3(D_)
        elif step == 6:
            ag4(D_)
            for key in CH:
                for k in (1, 2, 3):
                    z_send(key, k, done=True)

    def key_bias(slot):
        parts = []
        at = lax.broadcasted_iota(i32, (T, 128), 0).astype(f32)
        for b in range(4):
            limit = cnt[slot, b : b + 1, :].astype(f32)
            parts.append(jnp.where(at < limit, 0.0, NEG))
        return jnp.concatenate(parts, axis=0).astype(bf16)

    bias = R["bias"]
    bias[0] = key_bias(0)
    bias[1] = key_bias(2)
    QT = 256
    N = 4 * T

    def half(i, x):
        return jnp.where(lane // 64 == i, x, jnp.zeros_like(x))

    def key_side(k2, b, i):
        spot = 64 * (1 - i)
        return jnp.where(lane // 64 == i, k2, jnp.where(lane == spot, b, jnp.zeros_like(b)))

    def query_side(q2, i):
        spot = 64 * (1 - i)
        return jnp.where(lane // 64 == i, q2, jnp.where(lane == spot, 1.0, 0.0).astype(bf16))

    SC = 0.125 * LOG2E

    def attend(src, dst, col, bi, sel, lrow):
        cols = ds128(col, 128)
        k2 = src[1, :, cols]
        b = bias[bi]
        keys = [key_side(k2, b, i) for i in sel]

        @pl.loop(0, N // QT)
        def _(q):
            r = ds128(q * QT, QT)
            q2 = src[0, r, cols]
            v2 = src[2, :, cols]
            outs = []
            for n, i in enumerate(sel):
                s = nt(query_side(q2, i), keys[n])
                top = jnp.max(s, axis=1, keepdims=True) * SC
                p = jnp.exp2(s * SC - top)
                total = jnp.sum(p, axis=1, keepdims=True)
                outs.append(nn(p.astype(bf16), v2) / total)
                full_total = jnp.broadcast_to(top + jnp.log2(total), (QT, 128)).T
                lse[pl.ds(lrow + n, 1), r] = full_total[0:1, :]
            if len(sel) == 2:
                o = jnp.where(lane < 64, outs[0], outs[1])
            else:
                o = jnp.where(lane // 64 == sel[0], outs[0], 0.0)
            dst[0, r, cols] = o.astype(bf16)

    weights_ready(2)
    la.wait()
    wait_a("qkv", qkva, True)

    for t in range(2):
        attend(qkva, atta, t * 128, 0, (0, 1), 2 * t)
        weights_ready(t)
    lb.wait()
    wait_b_heads("qkv", qkvb)
    attend(qkvb, attb, c * 128, 1, (0, 1), 6)
    weights_ready(3)
    attend(qkvb, attb, (1 - c) * 128, 1, (c,), 8)
    xattb = [from_heads_b("att", attb, 0, k) for k in (1, 2, 3)]
    for d in xattb:
        d.start()
    lattb = from_heads_b_own(attb, L0 + 3)
    lattb.start()
    attend(qkva, atta, 256, 0, (0, 1), 4)
    xatt = from_heads_a("att", atta, att)
    xatt.start()
    latt = from_heads_a_own("att", atta, att, L0 + 2)
    latt.start()
    weights_ready(4)
    xa.wait_send()
    for d in xb:
        d.wait_send()
    latt.wait()
    wait_a("att", att, False)

    def slot_rows(s):
        return pl.ds(mult(s * T, T), T)

    def live_of(s):
        b = 2 * c + s if s < 2 else g
        at = lax.broadcasted_iota(i32, (T, 128), 0).astype(f32)
        pick = jnp.zeros((1, 128), f32)
        for i in range(4):
            pick = pick + jnp.where(b == i, cnt[s, i : i + 1, :].astype(f32), 0.0)
        return jnp.where(at < pick, 1.0, 0.0)[:, 0:1]

    for s in range(3):
        if s == 2:
            lattb.wait()
            wait_b_tokens("att", 1)
            merge_b(att, 0, 0)
            weights_ready(5)
        r = pl.ds(s * T, T)
        v = nn(att[0, r, :], wblock(R["wo"])) + vec(V_OB) + rows[s].astype(f32)
        mid[r, :] = v
        n, _ = normalise(v)
        nbuf[s] = (n * vec(V_MG) + vec(V_MS)).astype(bf16)
    weights_ready(6)
    FT = FR

    ub = R["ub"]
    outer = branch = cot

    def hidden(s, up, j):
        hid = nn(nbuf[s], up) + ub[pl.ds(j, 1), :]
        phi_c = 0.5 * (1.0 + lax.erf(hid * 0.7071067811865476))
        return hid, phi_c

    def outer_rows():
        for s in (2, 0, 1):
            recv(cot.at[s], I_COT + s)
            o = live_of(s) * cot[s].astype(f32)
            cot[s] = o.astype(bf16)
            part = col_sum(o)
            if s == 2:
                vg[V_DB : V_DB + 1, :] = part
            else:
                vg[V_DB : V_DB + 1, :] += part

    def feed(acc, n2t, tile):
        act_s, gh_s = tile.at[0], tile.at[1]
        for s in range(3):
            n2t[:, s * T : (s + 1) * T] = nbuf[s].T
            acc[s * T : (s + 1) * T, :] = mid[s * T : (s + 1) * T, :] + vec(V_DB)

        @pl.loop(0, dps)
        def _(j):
            up = wblock(R["wu"], ds128(j * FT, FT))
            down = R["wd"][j]

            @pl.loop(0, 3)
            def _(s):
                hid, phi_c = hidden(s, up, j)
                acc[slot_rows(s), :] += nn((hid * phi_c).astype(bf16), down)

        for s in (2, 0, 1):
            r = pl.ds(s * T, T)
            ysend[s] = (live_of(s) * acc[r, :]).astype(bf16)
            move_home(s, ysend.at[s], act, S_ACT, I_ACT)
            acc[r, :] = jnp.zeros((T, W), f32)
        outer_rows()

        def tile_pair(i):
            @pl.loop(2 * i, 2 * i + 2)
            def _(j):
                one_tile(j)

        def one_tile(j):
            cols = ds128(j * FT, FT)
            up = wblock(R["wu"], cols)
            down = R["wd"][j]

            @pl.loop(0, 3, init_carry=jnp.zeros((1, FT), f32))
            def bias_part(s, carry):
                r = slot_rows(s)
                hid, phi_c = hidden(s, up, j)
                act_s[r, :] = (hid * phi_c).astype(bf16)
                slope = phi_c + hid * jnp.exp2(hid * hid * (-0.5 * LOG2E)) * 0.3989422804014327
                gh = (nt(outer[s], down) * slope).astype(bf16)
                gh_s[r, :] = gh
                acc[r, :] += nt(gh, up)
                return carry + col_sum(gh.astype(f32))

            ub[pl.ds(j, 1), :] = bias_part
            R["wd"][j] = tn(act_s[...], outer[...].reshape(3 * T, W)).astype(bf16)
            R["wu"][:, :, cols] = nn(n2t[...], gh_s[...]).astype(bf16).reshape(dps, KR, FT)

        for i in range(dps // 2):
            tile_pair(i)
            if aligned:
                rs_core("D", i).start()
                if i == 1 or i == 3:
                    rs1("U%d" % (i // 2))
                if i > 0:
                    rs2_pair("D", i - 1)
                if i == 2:
                    rs2("U0")
                if i == 3:
                    rs3("U0")

        for s in (2, 0, 1):
            r = pl.ds(s * T, T)
            n, inv = normalise(mid[r, :])
            e_ = acc[r, :]
            gm = outer[s].astype(f32) + norm_back(e_, n, inv, vec(V_MG))
            mid[r, :] = gm
            low = gm.astype(bf16)
            branch[s] = low
            for i, part in ((V_MG, col_sum(e_ * n)), (V_MS, col_sum(e_)), (V_OB, col_sum(low.astype(f32)))):
                if s == 2:
                    vg[i : i + 1, :] = part
                else:
                    vg[i : i + 1, :] += part
            nbuf[s] = nt(low, wblock(R["wo"])).astype(bf16)
            send_do(s)
        for q in range(2):
            piece = tn(att[0, :, q * HALF : (q + 1) * HALF], branch[...].reshape(3 * T, W)).astype(bf16)
            R["wo"][q * (dps // 2) : (q + 1) * (dps // 2)] = piece.reshape(dps // 2, KR, W)
        grads_move(0)

    def act_done():
        for s in range(3):
            move_home_done(s, ysend.at[s], act, S_ACT, I_ACT)

    do3 = R["nbuf"]

    def do_copies(s):
        if s < 2:
            i0 = EX["do"][0] if s == 0 else L0 + 4
            return [rcopy(do3.at[s, :, ds128(HALF * (1 - c), HALF)], doa.at[ds128(2 * T * c + s * T, T)], i0, i0, (other, z))]
        out = []
        for k in (1, 2, 3):
            t = lax.rem(g + k, 4)
            cols = ds128(HALF * lax.div(t, 2) + 128 * lax.rem(t, 2), 256)
            out.append(rcopy(do3.at[2, :, cols], dob.at[ds128(T * g, T)], EX["do"][2] + k, EX["do"][1] + k, dev_of(t)))
        return out

    def send_do(s):
        for d in do_copies(s):
            d.start()

    def grads_move(step):
        if not aligned:
            return
        if step == 0:
            rs1("O")
            rs2_pair("D", 3)
            rs2("U1")
        elif step == 1:
            rs4("U0")
            rs2("O")
        elif step == 2:
            rs3("D")
            rs3("U1")
            y_send("U0", 2)
        elif step == 3:
            rs3("O")
        elif step == 4:
            rs4("D")
            rs4("U1")
            rs4("O")
            y_send("U0", 3)
        elif step == 5:
            y_send("D", 2)
            y_send("U1", 2)
            y_send("O", 2)
        elif step == 6:
            y_send("D", 3)
            y_send("U1", 3)
            y_send("O", 3)
        elif step == 8:
            for key in ("U0", "D", "U1", "O"):
                y_final(key)

    per = W // FT
    for q in range(dps):
        R["ub"][q : q + 1, :] = vt[V_UB + q // per : V_UB + q // per + 1, (q % per) * FT : (q % per + 1) * FT]
    pl.run_scoped(
        feed,
        pltpu.VMEM((3 * T, W), f32),
        pltpu.VMEM((W, 3 * T), bf16),
        pltpu.VMEM((2, 3 * T, FT), bf16),
    )
    for q in range(dps):
        vg[V_UB + q // per : V_UB + q // per + 1, (q % per) * FT : (q % per + 1) * FT] = R["ub"][q : q + 1, :]

    for j in range(2):
        doa[ds128(2 * T * c + j * T, T), :] = do3[j, :, ds128(HALF * c, HALF)]
    dob[ds128(T * g, T), :] = do3[2, :, ds128(HALF * e + 128 * c, 256)]

    def attend_back(src, o_ref, d_ref, col, bi, sel, lrow, dk, dv, delta):
        cols = ds128(col, 128)
        k2 = src[1, :, cols]
        v2 = src[2, :, cols]
        kt = k2.T
        b = bias[bi]
        keys = [key_side(k2, b, i) for i in sel]
        dk[...] = jnp.zeros_like(dk)
        dv[...] = jnp.zeros_like(dv)
        prod = o_ref[0, :, cols].astype(f32) * d_ref[:, cols].astype(f32)
        hi = prod.astype(bf16)
        lo = (prod - hi.astype(f32)).astype(bf16)
        row = lax.broadcasted_iota(i32, (8, 128), 0)
        if len(sel) == 2:
            pickm = (row == lax.broadcasted_iota(i32, (8, 128), 1) // 64).astype(f32).astype(bf16)
        else:
            pickm = jnp.where(jnp.logical_and(row == 0, lane // 64 == sel[0]), 1.0, 0.0).astype(bf16)
        delta[...] = nt(pickm, hi) + nt(pickm, lo)

        @pl.loop(0, N // QT)
        def _(q):
            r = ds128(q * QT, QT)
            q2 = src[0, r, cols]
            d2 = d_ref[r, cols]
            dks, dvs, dqs = [], [], []
            for n, i in enumerate(sel):
                qm, dm = half(i, q2), half(i, d2)
                s = nt(keys[n], query_side(q2, i))
                p = jnp.exp2(s * SC - lse[pl.ds(lrow + n, 1), r])
                dp_ = nt(v2, dm)
                ds_ = (p * (dp_ - delta[pl.ds(n, 1), r])).astype(bf16)
                dvs.append(nn(p.astype(bf16), dm))
                dks.append(nn(ds_, qm))
                dqs.append(nn(kt, ds_).T if len(sel) == 1 else nn(kt[64 * i : 64 * i + 64], ds_))
            if len(sel) == 2:
                dk[...] += dks[0] + dks[1]
                dv[...] += dvs[0] + dvs[1]
                dq = jnp.concatenate(dqs, axis=0).T
            else:
                dk[...] += dks[0]
                dv[...] += dvs[0]
                dq = half(sel[0], dqs[0])
            src[0, r, cols] = (dq * 0.125).astype(bf16)

        src[1, :, cols] = (dk[...] * 0.125).astype(bf16)
        src[2, :, cols] = dv[...].astype(bf16)

    I_DQA = take(6)

    def dq_copy(t):
        sref = qkva.at[:, ds128(2 * T * (1 - c), 2 * T), pl.ds(t * 128, 128)]
        dref = qkv.at[:, pl.ds(0, 2 * T), ds128(HALF * c + t * 128, 128)]
        return rcopy(sref, dref, I_DQA + t, I_DQA + t, (other, z))

    def dq_own(t):
        sref = qkva.at[:, ds128(2 * T * c, 2 * T), pl.ds(t * 128, 128)]
        dref = qkv.at[:, pl.ds(0, 2 * T), ds128(HALF * c + t * 128, 128)]
        return pltpu.make_async_copy(sref, dref, rs.at[I_DQA + 3 + t])

    def strips(t, r):
        return jnp.concatenate([qkv[j, r, k * HALF + t * 128 : k * HALF + (t + 1) * 128] for j in range(3) for k in range(2)], axis=1)

    gsend = cot
    if aligned:
        vx = R["vx"]
        I_VEC = take(3)
        I_VEZ = take(4)
        pairs = (other, dp + dx, dp + dy)

    def vec_copy(i):
        return rcopy(vg, vx.at[i], I_VEC + i, I_VEC + i, (pairs[i], z))

    def vec_add(i):
        vec_copy(i).wait()
        vg[...] += vx[i]

    def vec_z(k):
        return rcopy(vg, vx.at[2 + k], I_VEZ + k, I_VEZ + k, (dp, lax.rem(z + k, 4)))

    def rows_back(s, e_):
        r = pl.ds(s * T, T)
        n, inv = normalise(rows[s].astype(f32))
        gsend[s] = (mid[r, :] + norm_back(e_, n, inv, vec(V_NG))).astype(bf16)
        move_home(s, gsend.at[s], grh, S_GR, I_GR)
        parts = (
            (V_NG, col_sum(e_ * n)),
            (V_NS, col_sum(e_)),
            (V_QB, col_sum(qkv[0, r, :].astype(f32))),
            (V_VB, col_sum(qkv[2, r, :].astype(f32))),
        )
        for i, part in parts:
            if s == 2:
                vg[i : i + 1, :] = part
            else:
                vg[i : i + 1, :] += part

    def close_group(t, ebuf):
        dq_own(t).wait()
        recv(qkv.at[:, pl.ds(0, 2 * T), ds128(HALF * (1 - c) + t * 128, 128)], I_DQA + t)
        for s in range(2):
            part = nt(strips(t, pl.ds(s * T, T)), group(t))
            if t == 0:
                ebuf[s] = part
            else:
                ebuf[s] += part
        w = tn(nbuf[...].reshape(3 * T, W), strips(t, pl.ds(0, 3 * T))).astype(bf16)
        R["wq"][:, :, t * W : (t + 1) * W] = w.reshape(dps, KR, W)
        if aligned:
            rs1("Q%d" % t)

    def back(dk, dv, delta, ebuf):
        for k in (1, 2, 3):
            recv(dob.at[ds128(T * lax.rem(g + 4 - k, 4), T)], EX["do"][1] + k)
        attend_back(qkvb, attb, dob, c * 128, 1, (0, 1), 6, dk, dv, delta)
        grads_move(1)
        attend_back(qkvb, attb, dob, (1 - c) * 128, 1, (c,), 8, dk, dv, delta)
        for d in xattb:
            d.wait_send()
        for k in (1, 2, 3):
            from_heads_b("dqkv", qkvb, 0, k).start()
        from_heads_b_own(qkvb, L0 + 6).start()
        grads_move(2)
        recv(doa.at[ds128(2 * T * (1 - c), T)], EX["do"][0])
        recv(doa.at[ds128(2 * T * (1 - c) + T, T)], L0 + 4)
        attend_back(qkva, atta, doa, 0, 0, (0, 1), 0, dk, dv, delta)
        dq_copy(0).start()
        dq_own(0).start()
        grads_move(3)
        for s in range(3):
            for d in do_copies(s):
                d.wait_send()
        for s in range(3):
            normed_rows(s)
        for m in range(3):
            move_out_done(m, R["cnth"].at[m], cnt, S_CNT, I_CNT)
            move_out_done(m, R["cotangent"].at[m], cot, S_COT, I_COT)
        attend_back(qkva, atta, doa, 128, 0, (0, 1), 2, dk, dv, delta)
        dq_copy(1).start()
        dq_own(1).start()
        grads_move(4)
        from_heads_b_own(qkvb, L0 + 6).wait()
        wait_b_tokens("dqkv", 3)
        for j in range(3):
            merge_b(qkv, j, j)
        r = pl.ds(2 * T, T)
        e_ = nt(strips(0, r), group(0)) + nt(strips(1, r), group(1)) + nt(strips(2, r), group(2))
        rows_back(2, e_)
        close_group(0, ebuf)
        grads_move(5)
        attend_back(qkva, atta, doa, 256, 0, (0, 1), 4, dk, dv, delta)
        dq_copy(2).start()
        dq_own(2).start()
        close_group(1, ebuf)
        if aligned:
            rs2("Q0")
        close_group(2, ebuf)
        grads_move(6)
        rows_back(0, ebuf[0])
        if aligned:
            rs3("Q0")
            rs2("Q1")
        rows_back(1, ebuf[1])
        vg[12:16, :] = jnp.zeros((4, W), f32)
        if aligned:
            vec_copy(0).start()
            rs2("Q2")
            rs4("Q0")
            rs3("Q1")
            vec_add(0)
            vec_copy(1).start()
            rs3("Q2")
            rs4("Q1")
            y_send("Q0", 2)
            vec_add(1)
            vec_copy(2).start()
            rs4("Q2")
            y_send("Q1", 2)
            y_send("Q0", 3)
            vec_add(2)
            for k in (1, 2, 3):
                vec_z(k).start()
            grads_move(8)
            y_send("Q2", 2)
            y_send("Q1", 3)
            y_final("Q0")
            y_send("Q2", 3)
            y_final("Q1")
            for k in (1, 2, 3):
                recv(vx.at[2 + k], I_VEZ + k)
            for k in (1, 2, 3):
                vec_z(k).wait_send()
            total = vg[...]
            for k in (1, 2, 3):
                total = total + vx[2 + k]
            at = dp * 4 + z
            n1, n2 = W // 32, F // 32
            R["vs"][...] = pltpu.roll(total, lax.rem(W - at * n1, W), axis=1)[:, 0:128]
            line = lax.broadcasted_iota(i32, (16, W), 0)
            per_row = W // n2
            ubr = jnp.sum(jnp.where(line == V_UB + lax.div(at, per_row), total, 0.0), axis=0, keepdims=True)
            ubr = jnp.broadcast_to(ubr, (8, W))
            R["vs"][8:16, :] = pltpu.roll(ubr, lax.rem(W - lax.rem(at, per_row) * n2, W), axis=1)[:, 0:128]
            y_final("Q2")
            for key in GC:
                rs_done(key)

    pl.run_scoped(back, pltpu.VMEM((N, 128), f32), pltpu.VMEM((N, 128), f32), pltpu.VMEM((8, N), f32), pltpu.VMEM((2, T, W), f32))
    xatt.wait_send()
    if not aligned:
        save = [pltpu.make_async_copy(arrays[i], R[n], rs.at[L0 + 8 + i]) for i, n in enumerate(("gq", "go", "gu", "gd"))]
        for d in save:
            d.start()
        for d in save:
            d.wait()
    for t in range(3):
        dq_copy(t).wait_send()
    for k in (1, 2, 3):
        from_heads_b("dqkv", qkvb, 0, k).wait_send()
    act_done()
    for s in range(3):
        move_home_done(s, gsend.at[s], grh, S_GR, I_GR)
    for m in range(3):
        arrived_home(m, act, I_ACT)
        arrived_home(m, grh, I_GR)
    assert count[0] <= cfg["sems"], count[0]


def finish_kernel(sizes, keep, grads, act_in, *refs):
    n = 0 if sizes is None else 5
    act_out, out = refs[n], refs[n + 1]
    places = lax.broadcasted_iota(i32, (out.shape[1], keep.shape[2]), 0)
    out[0] = nn((places == keep[0]).astype(f32).astype(bf16), grads[0])
    act_out[...] = act_in[...]
    if sizes is not None:

        @pl.when(pl.program_id(0) == 0)
        def _():
            for i in range(4):
                refs[n + 2 + i][...] = refs[i][...]
            for i, width in enumerate(sizes):
                refs[n + 6 + i][...] = refs[4][i : i + 1, 0:width]


def body(patches, keep_index, shard_counts, cotangent, *shards):
    ng, ns, wq, qb, vb, wo, ob, mg, ms, wu, ub, wd, db = shards
    batches, _, patch, width = patches.shape
    tokens = keep_index.shape[2]
    dp_size, blk_size = lax.axis_size("dp"), lax.axis_size("blk")
    devices = dp_size * blk_size
    ff = wu.shape[1]
    aligned = dp_size == 8 and blk_size == 4
    dps = 8
    kr, fr = width // dps, ff // dps
    vectors = jnp.stack([ng, ns, qb, vb, ob, mg, ms, db])
    if aligned:
        own = jnp.pad(vectors, ((0, 0), (0, 128 - vectors.shape[1])))
        own_ub = jnp.pad(ub[None], ((0, 7), (0, 128 - ub.shape[0])))
        table = jnp.concatenate([own, own_ub])
        weights = (wq, wo, wu, wd)
        pieces = [w.size // 128 for w in weights] + [16]
        flat = [sum(pieces[:i]) for i in range(6)]
    else:
        axes = ("dp", "blk")
        table = lax.all_gather(vectors, axes, axis=1, tiled=True).astype(f32)
        table_ub = lax.all_gather(ub, axes, axis=0, tiled=True).astype(f32).reshape(ff // width, width)
        table = jnp.concatenate([table, table_ub, jnp.zeros((16 - 8 - ff // width, width), f32)])
        weights = tuple(lax.all_gather(w, axes, axis=0, tiled=True) for w in (wq, wo, wu, wd))
        weights = tuple(w.reshape(dps, -1, w.shape[1]) for w in weights)
        held = weights[0].reshape(dps, kr, 3, 2, 3, width // 6).transpose(0, 1, 4, 2, 3, 5).reshape(dps, kr, 3 * width)
        weights = (held, *weights[1:])
        flat = None
    cfg = dict(aligned=aligned, dps=dps, tokens=tokens, width=width, ff=ff, patch=patch, flat=flat, sems=320)
    keep = keep_index
    ins = [
        ("patches", patches[:, 0], ANY),
        ("keep", keep, VMEM),
        ("counts", shard_counts[:, 0], SMEM),
        ("cotangent", cotangent[:, 0], ANY),
    ]
    ins += [(n, w, VMEM if aligned else ANY) for n, w in zip(("sq", "so", "su", "sd"), weights)]
    ins.append(("sv", table, VMEM))
    out = [
        ("act", (3, tokens, width), bf16, ANY),
        ("grh", (3, tokens, width), bf16, ANY),
        ("vg", (16, width), f32, VMEM),
    ]
    full = {"q": (dps, kr, 3 * width), "o": (dps, kr, width), "u": (dps, kr, ff), "d": (dps, fr, width)}
    for i, n in enumerate("qoud"):
        if aligned:
            out.append(("g" + n, weights[i].shape, f32, VMEM))
        else:
            out.append(("g" + n, full[n], bf16, ANY))
    if aligned:
        out.append(("vs", (16, 128), f32, VMEM))
    t3 = 3 * tokens
    scratch = [("w" + n, full[n], bf16) for n in "qoud"]
    scratch += [
        ("rows", (3, tokens, width), bf16),
        ("cot", (3, tokens, width), bf16),
        ("cnt", (3, 16, 128), bf16),
        ("cnth", (3, 16, 128), bf16),
        ("nbuf", (3, tokens, width), bf16),
        ("qkv", (3, t3, width), bf16),
        ("qkva", (3, 4 * tokens, width // 2), bf16),
        ("qkvb", (3, 4 * tokens, 256), bf16),
        ("atta", (1, 4 * tokens, width // 2), bf16),
        ("attb", (1, 4 * tokens, 256), bf16),
        ("att", (1, t3, width), bf16),
        ("fromb", (4, 3, tokens, 256), bf16),
        ("doa", (4 * tokens, width // 2), bf16),
        ("dob", (4 * tokens, 256), bf16),
        ("mid", (t3, width), f32),
        ("ysend", (3, tokens, width), bf16),
        ("vt", (16, width), f32),
        ("lse", (16, 4 * tokens), f32),
        ("bias", (2, 4 * tokens, 128), bf16),
        ("ub", (dps, fr), f32),
    ]
    if aligned:
        scratch += [
            ("zbuf", (4, flat[5], 128), bf16),
            ("zrr", (3, flat[4], 128), bf16),
            ("zrl", (3, flat[4], 128), bf16),
            ("vw", (dps, 64, 128), bf16),
            ("vx", (6, 16, width), f32),
        ]
        scratch += [("rb1" + n, (4, *full[n][1:]), bf16) for n in "qoud"]
        scratch += [("rb2" + n, (3, *full[n][1:]), bf16) for n in "qoud"]
    names = [n for n, _, _ in scratch] + ["ss", "rs"]
    shapes = [pltpu.VMEM(s, d) for _, s, d in scratch] + [pltpu.SemaphoreType.DMA((cfg["sems"],))] * 2
    flops = 6 * 3 * tokens * (4 * width * width + 2 * width * ff)
    results = pl.pallas_call(
        functools.partial(layer_kernel, cfg, [n for n, _, _ in ins], [n for n, *_ in out], names),
        out_shape=[jax.ShapeDtypeStruct(s, d) for _, s, d, _ in out],
        in_specs=[s for _, _, s in ins],
        out_specs=[s for *_, s in out],
        scratch_shapes=shapes,
        compiler_params=pltpu.CompilerParams(collective_id=0, has_side_effects=True, vmem_limit_bytes=64 * 1024 * 1024 - 512 * 1024),
        cost_estimate=pl.CostEstimate(flops=flops, bytes_accessed=50_000_000, transcendentals=0),
        name="layer",
    )(*[a for _, a, _ in ins])
    act, grh, vg, gq, go, gu, gd = results[:7]
    whole = lambda v: pl.BlockSpec(v, lambda m: (0,) * len(v))
    step = lambda *v: pl.BlockSpec((1, *v), lambda m: (m, 0, 0))
    n = width // devices
    sizes = [n] * 8 + [ff // devices] if aligned else None
    extra = [gq, go, gu, gd, results[7]] if aligned else []
    shapes = [(3, tokens, width, bf16), (3, patch, width, f32)]
    specs = [step(tokens, width), step(patch, width)]
    if aligned:
        shapes += [(*v.shape, f32) for v in extra[:4]] + [(1, v, f32) for v in sizes]
        specs += [whole(v.shape) for v in extra[:4]] + [whole((1, v)) for v in sizes]
    done = pl.pallas_call(
        functools.partial(finish_kernel, sizes),
        grid=(3,),
        in_specs=[step(1, tokens), step(tokens, width), step(tokens, width)] + [whole(v.shape) for v in extra],
        out_specs=specs,
        out_shape=[jax.ShapeDtypeStruct(v[:-1], v[-1]) for v in shapes],
        compiler_params=pltpu.CompilerParams(vmem_limit_bytes=32 * 1024 * 1024),
        name="finish",
    )(keep, grh, act, *extra)
    act, patch_grad = done[:2]
    if aligned:
        gq, go, gu, gd = done[2:6]
        piece = [v.reshape(-1) for v in done[6:]]
    else:
        axes = ("dp", "blk")
        small = [vg[:8].reshape(8, devices, n).transpose(1, 0, 2).reshape(devices, -1), vg[8 : 8 + ff // width].reshape(devices, -1)]
        small = lax.psum_scatter(jnp.concatenate(small, axis=1), axes, scatter_dimension=0, tiled=True)[0]
        piece = [small[i * n : (i + 1) * n] for i in range(8)] + [small[8 * n :]]
        gq = gq.reshape(dps, kr, 3, 3, 2, width // 6).transpose(0, 1, 3, 4, 2, 5).reshape(dps, kr, 3 * width)
        gq, go, gu, gd = (
            lax.psum_scatter(w.reshape(-1, w.shape[-1]).astype(f32), axes, scatter_dimension=0, tiled=True) for w in (gq, go, gu, gd)
        )
    return (
        act[:, None],
        patch_grad[:, None],
        piece[V_NG],
        piece[V_NS],
        gq,
        piece[V_QB],
        piece[V_VB],
        go,
        piece[V_OB],
        piece[V_MG],
        piece[V_MS],
        gu,
        piece[V_UB],
        gd,
        piece[V_DB],
    )


def solution(mesh):
    vec, mat = P(("dp", "blk")), P(("dp", "blk"), None)
    tok = P(None, "dp", "blk", None)
    params = (vec, vec, mat, vec, vec, mat, vec, vec, vec, mat, vec, mat, vec)
    in_specs = (tok, P(None, "dp", "blk"), P(None, "dp", None), tok) + params
    out_specs = (tok, tok) + params
    return jax.shard_map(body, mesh=mesh, in_specs=in_specs, out_specs=out_specs, check_vma=False)
```

```python
import functools

import jax
import jax.numpy as jnp
from jax import lax
from jax.experimental import pallas as pl
from jax.experimental.pallas import tpu as pltpu
from jax.sharding import PartitionSpec as P

MESH = pl.DeviceIdType.MESH
ANY = pl.BlockSpec(memory_space=pl.ANY)
VMEM = pl.BlockSpec(memory_space=pltpu.VMEM)
SMEM = pl.BlockSpec(memory_space=pltpu.SMEM)
f32, bf16, i32 = jnp.float32, jnp.bfloat16, jnp.int32

EPSILON = 1e-06
LOG2E = 1.4426950408889634
NEG = -1e30


def nn(a, b):
    return lax.dot_general(a, b, (((1,), (0,)), ((), ())), preferred_element_type=f32)


def nt(a, b):
    return lax.dot_general(a, b, (((1,), (1,)), ((), ())), preferred_element_type=f32)


def tn(a, b):
    return lax.dot_general(a, b, (((0,), (0,)), ((), ())), preferred_element_type=f32)


def mult(x, k):
    return x if isinstance(x, int) else pl.multiple_of(x, k)


def normalise(v):
    centred = v - jnp.mean(v, axis=1, keepdims=True)
    inv = lax.rsqrt(jnp.mean(centred * centred, axis=1, keepdims=True) + EPSILON)
    return centred * inv, inv


def norm_back(e, n, inv, gain):
    f = e * gain
    return inv * (f - jnp.mean(f, axis=1, keepdims=True) - n * jnp.mean(f * n, axis=1, keepdims=True))


def col_sum(v):
    return jnp.sum(v, axis=0, keepdims=True)


def group_tile(t):
    return t % 3 * 6 + t // 6 * 2 + t % 6 // 3


def natural_tile(p):
    return p % 6 // 2 * 6 + p % 2 * 3 + p // 6


V_NG, V_NS, V_QB, V_VB, V_OB, V_MG, V_MS, V_DB, V_UB = range(9)


def layer_kernel(cfg, names_in, names_out, names_scratch, *refs):
    R = dict(zip(names_in + names_out + names_scratch, refs, strict=True))
    aligned, dps = cfg["aligned"], cfg["dps"]
    T, W, F = cfg["tokens"], cfg["width"], cfg["ff"]
    KR = W // dps
    FR = F // dps
    HALF = W // 2
    dp, z = lax.axis_index("dp"), lax.axis_index("blk")
    c = lax.rem(dp, 2)
    base = dp - c
    h, e = lax.div(z, 2), lax.rem(z, 2)
    g = 2 * e + c
    other = base + 1 - c
    ss, rs = R["ss"], R["rs"]
    count = [0]

    def take(n=1):
        count[0] += n
        return count[0] - n

    def rcopy(src, dst, s, r, dev):
        return pltpu.make_async_remote_copy(
            src_ref=src, dst_ref=dst, send_sem=ss.at[s], recv_sem=rs.at[r], device_id=dev, device_id_type=MESH
        )

    def recv(dst, r, dev=None):
        rcopy(dst, dst, 0, r, (other, z) if dev is None else dev).wait_recv()

    bar = pltpu.get_barrier_semaphore()
    peers = []
    for k in range(1, 8):
        j = lax.rem(c * 4 + z + k, 8)
        peers.append((base + lax.div(j, 4), lax.rem(j, 4)))
    if aligned:
        dx = 2 - 4 * lax.rem(lax.div(dp, 2), 2)
        dy = 4 - 8 * lax.div(dp, 4)
        p1, p2, p3 = dp + (1 - c) * dx + c * dy, dp + c * dx + (1 - c) * dy, dp + dx + dy
        peers += [(p1, z), (p2, z)]
    for dev in peers:
        pl.semaphore_signal(bar, inc=1, device_id=dev, device_id_type=MESH)

    def owner(m):
        if m < 2:
            return lax.div(z, 2), 2 * c + m, lax.rem(z, 2)
        return lax.rem(z, 2), 2 * c + lax.div(z, 2), 2

    def home(s):
        if s < 2:
            return h, 2 * c + s
        return h, 2 * e + c

    def move_out(m, src, dst, sid, rid):
        tc, tz, slot = owner(m)
        own = jnp.logical_and(tc == c, tz == z)

        @pl.when(own)
        def _():
            pltpu.make_async_copy(src, dst.at[slot], rs.at[rid + slot]).start()

        @pl.when(jnp.logical_not(own))
        def _():
            rcopy(src, dst.at[slot], sid + m, rid + slot, (base + tc, tz)).start()

    def move_out_done(m, src, dst, sid, rid):
        tc, tz, slot = owner(m)
        own = jnp.logical_and(tc == c, tz == z)

        @pl.when(jnp.logical_not(own))
        def _():
            rcopy(src, dst.at[slot], sid + m, rid + slot, (base + tc, tz)).wait_send()

    def move_home(s, src, dst, sid, rid):
        tc, tz = home(s)
        m = e if s < 2 else 2
        own = jnp.logical_and(tc == c, tz == z)

        @pl.when(own)
        def _():
            pltpu.make_async_copy(src, dst.at[m], ss.at[sid + s]).start()

        @pl.when(jnp.logical_not(own))
        def _():
            rcopy(src, dst.at[m], sid + s, rid + m, (base + tc, tz)).start()

    def move_home_done(s, src, dst, sid, rid):
        tc, tz = home(s)
        m = e if s < 2 else 2
        own = jnp.logical_and(tc == c, tz == z)

        @pl.when(own)
        def _():
            pltpu.make_async_copy(src, dst.at[m], ss.at[sid + s]).wait()

        @pl.when(jnp.logical_not(own))
        def _():
            rcopy(src, dst.at[m], sid + s, rid + m, (base + tc, tz)).wait_send()

    def arrived_home(m, dst, rid):
        tc, tz, _ = owner(m)

        @pl.when(jnp.logical_not(jnp.logical_and(tc == c, tz == z)))
        def _():
            recv(dst.at[m], rid + m)

    arrays = [R["wq"], R["wo"], R["wu"], R["wd"]]
    Q_, O_, U_, D_ = 0, 1, 2, 3
    if aligned:
        zbuf, zrr, zrl = R["zbuf"], R["zrr"], R["zrl"]
        flat = cfg["flat"]
        CH = {"Q": (0, flat[1]), "OU": (flat[1], flat[3]), "D": (flat[3], flat[4]), "V": (flat[4], flat[5])}
        ZR = {k: take(3) - 1 for k in CH}
        ZL = {k: take(3) - 1 for k in CH}
        wide = W // 128
        GC = {"D": (D_, 0, wide), "O": (O_, 0, wide)}
        for i in range(2):
            GC["U%d" % i] = (U_, i * F // 256, (i + 1) * F // 256)
        for i in range(3):
            GC["Q%d" % i] = (Q_, i * wide, (i + 1) * wide)
        YR = {k: take(3) - 1 for k in GC}
        YL = {k: take(3) - 1 for k in GC}
        gathered = arrays + [R["vw"]]
        XY = [take(3) for _ in range(5)]
        CR = [take(4) for _ in range(5)]
        R1 = {k: take(4) for k in GC}
        R2 = {k: take(3) for k in GC}

        def z_send(key, k, done=False):
            r0, r1 = CH[key]
            rows = pl.ds(r0, r1 - r0)
            right = jnp.logical_and(z < 3, z - (k - 1) >= 0)
            left = jnp.logical_and(z > 0, z + (k - 1) <= 3)

            @pl.when(right)
            def _():
                ref = zbuf.at[z - (k - 1), rows]
                d = rcopy(ref, ref, ZR[key] + k, ZR[key] + k, (dp, z + 1))
                d.wait_send() if done else d.start()

            @pl.when(left)
            def _():
                ref = zbuf.at[z + (k - 1), rows]
                d = rcopy(ref, ref, ZL[key] + k, ZL[key] + k, (dp, z - 1))
                d.wait_send() if done else d.start()

        def z_wait(key, k):
            r0, r1 = CH[key]
            rows = pl.ds(r0, r1 - r0)

            @pl.when(z - k >= 0)
            def _():
                recv(zbuf.at[z - k, rows], ZR[key] + k)

            @pl.when(z + k <= 3)
            def _():
                recv(zbuf.at[z + k, rows], ZL[key] + k)

        def flatten(a, ref, slot):
            if a == D_:
                n, rows = W // 128, FR // 4
            elif a == 4:
                n, rows = 1, 16
            else:
                n, rows = ref.shape[-1] // 128, KR // 4
            for t in range(n):
                cols = slice(t * 128, (t + 1) * 128)
                zbuf[slot, flat[a] + t * rows : flat[a] + (t + 1) * rows, :] = ref[:, cols]

        def place(a, t):
            return group_tile(t) if a == Q_ else t

        def unflatten(a, block):
            dst = gathered[a]
            if a == D_:
                n, rows = W // 128, FR // 4
            elif a == 4:
                n, rows = 1, 16
            else:
                n, rows = dst.shape[-1] // 128, KR // 4
            for s in range(4):
                for t in range(n):
                    p = place(a, t) * 128
                    dst[block, s * rows : (s + 1) * rows, p : p + 128] = zbuf[s, flat[a] + t * rows : flat[a] + (t + 1) * rows, :]

        def ag_copies(a):
            ref = gathered[a]

            def core(i):
                block = (dp, p1, p2, p3)[i]
                return rcopy(ref.at[block], ref.at[block], CR[a] + i, CR[a] + i, (other, z))

            return {
                "p1": lambda: rcopy(ref.at[dp], ref.at[dp], XY[a], XY[a], (p1, z)),
                "p2": lambda: rcopy(ref.at[dp], ref.at[dp], XY[a] + 1, XY[a] + 1, (p2, z)),
                "fw": lambda: rcopy(ref.at[p1], ref.at[p1], XY[a] + 2, XY[a] + 2, (p2, z)),
                "c0": lambda: core(0),
                "c1": lambda: core(1),
                "c2": lambda: core(2),
                "c3": lambda: core(3),
            }

        def ag1(a):
            d = ag_copies(a)
            d["p1"]().start()
            d["p2"]().start()
            d["c0"]().start()

        def ag2(a):
            d = ag_copies(a)
            ref = gathered[a]
            recv(ref.at[p1], XY[a])
            d["fw"]().start()
            d["c1"]().start()
            recv(ref.at[p2], XY[a] + 1)
            d["c2"]().start()

        def ag3(a):
            d = ag_copies(a)
            recv(gathered[a].at[p3], XY[a] + 2)
            d["c3"]().start()

        def ag4(a):
            d = ag_copies(a)
            for i, block in enumerate((dp, p2, p1, p3)):
                recv(gathered[a].at[block + other - dp], CR[a] + i)
            for k in d.values():
                k().wait_send()

        def blk_of(i):
            return 2 * i + c

        bufs1 = [R["rb1" + n] for n in "qoud"]
        bufs2 = [R["rb2" + n] for n in "qoud"]

        def cols_of(key):
            _, t0, t1 = GC[key]
            return pl.ds(t0 * 128, (t1 - t0) * 128)

        def block_of(key, block):
            return arrays[GC[key][0]].at[block, :, cols_of(key)]

        def view(bufs, key, i):
            return bufs[GC[key][0]].at[i, :, cols_of(key)]

        def rs_core(key, i):
            return rcopy(block_of(key, 2 * i + 1 - c), view(bufs1, key, i), R1[key] + i, R1[key] + i, (other, z))

        def rs1(key):
            for i in range(4):
                rs_core(key, i).start()

        def addto(key, block, parts):
            ref, cols = arrays[GC[key][0]], cols_of(key)
            rows = ref.shape[1]
            step = 48

            @pl.loop(0, rows // step)
            def _(q):
                r = pl.ds(mult(q * step, step), step)
                total = ref[block, r, cols].astype(f32)
                for p, i in parts:
                    total = total + p[GC[key][0]][i, r, cols].astype(f32)
                ref[block, r, cols] = total.astype(bf16)

        def rs_xy(key):
            i0 = R2[key]
            return {
                "diag": lambda: rcopy(block_of(key, p3), view(bufs2, key, 0), i0, i0, (p2, z)),
                "p2": lambda: rcopy(block_of(key, p2), view(bufs2, key, 1), i0 + 1, i0 + 1, (p2, z)),
                "p1": lambda: rcopy(block_of(key, p1), view(bufs2, key, 2), i0 + 2, i0 + 2, (p1, z)),
            }

        def rs2_pair(key, i):
            recv(view(bufs1, key, i), R1[key] + i)
            addto(key, blk_of(i), [(bufs1, i)])

            @pl.when(blk_of(i) == p3)
            def _():
                rs_xy(key)["diag"]().start()

            @pl.when(blk_of(i) == p2)
            def _():
                rs_xy(key)["p2"]().start()

        def rs2(key):
            for i in range(4):
                rs2_pair(key, i)

        def rs3(key):
            recv(view(bufs2, key, 0), R2[key])
            addto(key, p1, [(bufs2, 0)])
            rs_xy(key)["p1"]().start()

        def span(key):
            a, t0, t1 = GC[key]
            n = arrays[a].shape[1] // 4
            return a, n, flat[a] + t0 * n, (t1 - t0) * n

        def rs4(key):
            recv(view(bufs2, key, 1), R2[key] + 1)
            recv(view(bufs2, key, 2), R2[key] + 2)
            addto(key, dp, [(bufs2, 1), (bufs2, 2)])
            a, n, _, _ = span(key)
            for slot in range(4):
                for t in range(GC[key][1], GC[key][2]):
                    piece = arrays[a][dp, slot * n : (slot + 1) * n, t * 128 : (t + 1) * 128]
                    zbuf[slot, flat[a] + t * n : flat[a] + (t + 1) * n, :] = piece
            y_send(key, 1)

        def y_send(key, k, done=False):
            _, _, r0, rn = span(key)
            rows = pl.ds(r0, rn)
            to_right = z + 4 - k
            to_left = z - 4 + k

            @pl.when(jnp.logical_and(z < 3, to_right <= 3))
            def _():
                if k > 1 and not done:

                    @pl.when(z >= 1)
                    def _():
                        recv(zrr.at[k - 2, rows], YR[key] + k - 1)
                        zbuf[to_right, rows, :] = (zbuf[to_right, rows, :].astype(f32) + zrr[k - 2, rows, :].astype(f32)).astype(bf16)

                d = rcopy(zbuf.at[to_right, rows], zrr.at[k - 1, rows], YR[key] + k, YR[key] + k, (dp, z + 1))
                d.wait_send() if done else d.start()

            @pl.when(jnp.logical_and(z > 0, to_left >= 0))
            def _():
                if k > 1 and not done:

                    @pl.when(z <= 2)
                    def _():
                        recv(zrl.at[k - 2, rows], YL[key] + k - 1)
                        zbuf[to_left, rows, :] = (zbuf[to_left, rows, :].astype(f32) + zrl[k - 2, rows, :].astype(f32)).astype(bf16)

                d = rcopy(zbuf.at[to_left, rows], zrl.at[k - 1, rows], YL[key] + k, YL[key] + k, (dp, z - 1))
                d.wait_send() if done else d.start()

        def y_final(key):
            a, n, r0, rn = span(key)
            rows = pl.ds(r0, rn)

            @pl.when(z >= 1)
            def _():
                recv(zrr.at[2, rows], YR[key] + 3)

            @pl.when(z <= 2)
            def _():
                recv(zrl.at[2, rows], YL[key] + 3)

            for t in range(GC[key][1], GC[key][2]):
                piece = slice(flat[a] + t * n, flat[a] + (t + 1) * n)
                total = zbuf[z, piece, :].astype(f32)
                total = total + jnp.where(z >= 1, zrr[2, piece, :].astype(f32), 0.0)
                total = total + jnp.where(z <= 2, zrl[2, piece, :].astype(f32), 0.0)
                p = natural_tile(t) if a == Q_ else t
                outs[a][:, p * 128 : (p + 1) * 128] = total

        def rs_done(key):
            for k in (1, 2, 3):
                y_send(key, k, done=True)
            for i in range(4):
                rs_core(key, i).wait_send()
            for d in rs_xy(key).values():
                d().wait_send()

        outs = [R["gq"], R["go"], R["gu"], R["gd"]]

    I_ROWS, I_CNT, I_COT, I_ACT, I_GR = (take(3) for _ in range(5))
    S_ROWS, S_CNT, S_COT, S_ACT, S_GR = (take(3) for _ in range(5))
    EX = {}
    for k in ("qkv", "att", "do", "dqkv"):
        EX[k] = (take(1), take(4), take(4))
    L0 = take(12)

    rows, cot, cnt, nbuf = R["rows"], R["cot"], R["cnt"], R["nbuf"]
    qkv, qkva, qkvb = R["qkv"], R["qkva"], R["qkvb"]
    atta, attb, att, fromb = R["atta"], R["attb"], R["att"], R["fromb"]
    doa, dob, mid, vt, vg = R["doa"], R["dob"], R["mid"], R["vt"], R["vg"]
    lse, grh, keep, act, ysend = R["lse"], R["grh"], R["keep"], R["act"], R["ysend"]
    lane = lax.broadcasted_iota(i32, (1, 128), 1)

    if aligned:
        for a, name in enumerate(("sq", "so", "su", "sd", "sv")):
            flatten(a, R[name], z)
    for m in range(3):
        for b in range(4):
            R["cnth"][m, b : b + 1, :] = jnp.full((1, 128), R["counts"][m, 0, b], i32).astype(f32).astype(bf16)
        R["cnth"][m, 4:, :] = jnp.zeros((12, 128), bf16)

    def pick_rows(pbuf, psem):
        copies = [pltpu.make_async_copy(R["patches"].at[m], pbuf.at[m], psem.at[m]) for m in range(3)]
        for d in copies:
            d.start()
        pl.semaphore_wait(bar, len(peers))
        if aligned:
            z_send("Q", 1)
            z_send("V", 1)
        for m in range(3):
            copies[m].wait()
            spread = (lax.broadcasted_iota(i32, (cfg["patch"], T), 0) == keep[m]).astype(f32).astype(bf16)
            att[0, m * T : (m + 1) * T, :] = tn(spread, pbuf[m]).astype(bf16)

    pl.run_scoped(pick_rows, pltpu.VMEM((3, cfg["patch"], W), bf16), pltpu.SemaphoreType.DMA((3,)))

    def send_rows():
        for m in (2, 0, 1):
            move_out(m, att.at[0, pl.ds(m * T, T)], rows, S_ROWS, I_ROWS)
            move_out(m, R["cnth"].at[m], cnt, S_CNT, I_CNT)

    def send_cot(ms=(2, 0, 1)):
        for m in ms:
            move_out(m, R["cotangent"].at[m], cot, S_COT, I_COT)

    if aligned:
        for key in "QV":
            z_wait(key, 1)
            z_send(key, 2)
        z_send("OU", 1)
        for key in "QV":
            z_wait(key, 2)
            z_send(key, 3)
        z_wait("OU", 1)
        z_send("OU", 2)
        z_send("D", 1)
        for key in "QV":
            z_wait(key, 3)
        unflatten(Q_, dp)
        ag1(Q_)
        unflatten(4, dp)
        ag1(4)
        z_wait("OU", 2)
        z_send("OU", 3)
        z_wait("D", 1)
        z_send("D", 2)
        z_wait("OU", 3)
        z_wait("D", 2)
        z_send("D", 3)
        send_rows()
    else:
        full = [pltpu.make_async_copy(R[n], arrays[i], rs.at[L0 + 8 + i]) for i, n in enumerate(("sq", "so", "su", "sd"))]
        for d in full:
            d.start()
        send_rows()
        send_cot()
    if aligned:
        ag2(Q_)
        ag2(4)
        for a in (U_, O_):
            unflatten(a, dp)
        ag3(Q_)
        ag3(4)
        ag4(4)
        ag4(Q_)
        for a in (U_, O_):
            ag1(a)
        v = R["vw"][...].reshape(32 * 16, 128)
        to = lax.broadcasted_iota(i32, (128, W), 1)
        frm = lax.broadcasted_iota(i32, (128, W), 0)
        dev = lax.broadcasted_iota(i32, (512, W), 0) // 16
        col = lax.broadcasted_iota(i32, (512, W), 1)
        n1, n2 = W // 32, F // 32
        x1 = nn(v, (lax.rem(to, n1) == frm).astype(f32).astype(bf16))
        x1 = jnp.where(dev == col // n1, x1, 0.0)
        vt[0:16, :] = jnp.sum(x1.reshape(32, 16, W), axis=0)
        x2 = nn(v, (lax.rem(to, n2) == frm).astype(f32).astype(bf16))
        x2 = jnp.where(lax.rem(dev, W // n2) == col // n2, x2, 0.0)
        x2 = jnp.sum(x2.reshape(4, 8, 16, W), axis=1)
        for q in range(4):
            vt[V_UB + q : V_UB + q + 1, :] = x2[q, V_UB : V_UB + 1, :]
    else:
        vt[...] = R["sv"][...]

    def vec(i):
        return vt[i : i + 1, :]

    def normed_rows(s):
        n, _ = normalise(rows[s].astype(f32))
        nbuf[s] = (n * vec(V_NG) + vec(V_NS)).astype(bf16)

    for s in (2, 0, 1):
        recv(rows.at[s], I_ROWS + s)
        recv(cnt.at[s], I_CNT + s)
        normed_rows(s)
    if not aligned:
        for d in full:
            d.wait()

    def wblock(ref, cols=None):
        v = ref[...] if cols is None else ref[:, :, cols]
        return v.reshape(-1, v.shape[-1])

    def group(t):
        return wblock(R["wq"], slice(t * W, (t + 1) * W))

    def project(s):
        r = pl.ds(mult(s * T, T), T)
        for t in range(3):
            v = nn(nbuf[s], group(t))
            for j in range(3):
                for k in range(2):
                    at = k * HALF + t * 128
                    x = v[:, (2 * j + k) * 128 : (2 * j + k + 1) * 128]
                    if j != 1:
                        row = V_QB if j == 0 else V_VB
                        x = x + vt[row : row + 1, at : at + 128]
                    qkv[j, r, at : at + 128] = x.astype(bf16)

    def dev_of(i):
        return (base + lax.rem(i, 2), 2 * h + lax.div(i, 2))

    def ds128(x, n):
        return pl.ds(mult(x, 128), n)

    def to_heads_a(kind, src, dst):
        i0 = EX[kind][0]
        full_ = [slice(None)] * (len(src.shape) - 2)
        sref = src.at[(*full_, pl.ds(0, 2 * T), ds128(HALF * (1 - c), HALF))]
        dref = dst.at[(*full_, ds128(2 * T * c, 2 * T))]
        return rcopy(sref, dref, i0, i0, (other, z))

    def to_heads_a_own(kind, src, dst, lid):
        full_ = [slice(None)] * (len(src.shape) - 2)
        sref = src.at[(*full_, pl.ds(0, 2 * T), ds128(HALF * c, HALF))]
        dref = dst.at[(*full_, ds128(2 * T * c, 2 * T))]
        return pltpu.make_async_copy(sref, dref, rs.at[lid])

    def to_heads_b(kind, src, dst, k):
        _, rid, sid = EX[kind]
        full_ = [slice(None)] * (len(src.shape) - 2)
        t = lax.rem(g + k, 4)
        sref = src.at[(*full_, pl.ds(2 * T, T), ds128(HALF * lax.div(t, 2) + 128 * lax.rem(t, 2), 256))]
        dref = dst.at[(*full_, ds128(T * g, T))]
        return rcopy(sref, dref, sid + k, rid + k, dev_of(t))

    def to_heads_b_own(kind, src, dst, lid):
        full_ = [slice(None)] * (len(src.shape) - 2)
        sref = src.at[(*full_, pl.ds(2 * T, T), ds128(HALF * e + 128 * c, 256))]
        dref = dst.at[(*full_, ds128(T * g, T))]
        return pltpu.make_async_copy(sref, dref, rs.at[lid])

    def from_heads_a(kind, src, dst):
        i0 = EX[kind][0]
        full_ = [slice(None)] * (len(src.shape) - 2)
        sref = src.at[(*full_, ds128(2 * T * (1 - c), 2 * T))]
        dref = dst.at[(*full_, pl.ds(0, 2 * T), ds128(HALF * c, HALF))]
        return rcopy(sref, dref, i0, i0, (other, z))

    def from_heads_a_own(kind, src, dst, lid):
        full_ = [slice(None)] * (len(src.shape) - 2)
        sref = src.at[(*full_, ds128(2 * T * c, 2 * T))]
        dref = dst.at[(*full_, pl.ds(0, 2 * T), ds128(HALF * c, HALF))]
        return pltpu.make_async_copy(sref, dref, rs.at[lid])

    def from_heads_b(kind, src, j0, k):
        _, rid, sid = EX[kind]
        t = lax.rem(g + k, 4)
        n = src.shape[0]
        sref = src.at[:, ds128(T * t, T)]
        dref = fromb.at[g, pl.ds(0, n)]
        return rcopy(sref, dref, sid + k, rid + k, dev_of(t))

    def from_heads_b_own(src, lid):
        n = src.shape[0]
        return pltpu.make_async_copy(src.at[:, ds128(T * g, T)], fromb.at[g, pl.ds(0, n)], rs.at[lid])

    def wait_a(kind, dst, heads):
        full_ = [slice(None)] * (len(dst.shape) - 2)
        if heads:
            dref = dst.at[(*full_, ds128(2 * T * (1 - c), 2 * T))]
        else:
            dref = dst.at[(*full_, pl.ds(0, 2 * T), ds128(HALF * (1 - c), HALF))]
        recv(dref, EX[kind][0])

    def wait_b_heads(kind, dst):
        full_ = [slice(None)] * (len(dst.shape) - 2)
        for k in (1, 2, 3):
            recv(dst.at[(*full_, ds128(T * lax.rem(g + 4 - k, 4), T))], EX[kind][1] + k)

    def wait_b_tokens(kind, n):
        for k in (1, 2, 3):
            recv(fromb.at[lax.rem(g + 4 - k, 4), pl.ds(0, n)], EX[kind][1] + k)

    def merge_b(dst, j, n_from):
        for q in range(2):
            lo, hi = fromb[2 * q, n_from], fromb[2 * q + 1, n_from]
            at = q * HALF
            dst[j, 2 * T : 3 * T, at : at + 128] = lo[:, 0:128]
            dst[j, 2 * T : 3 * T, at + 128 : at + 256] = jnp.where(lane < 64, lo[:, 128:256], hi[:, 0:128])
            dst[j, 2 * T : 3 * T, at + 256 : at + 384] = hi[:, 128:256]

    for m in range(3):
        move_out_done(m, att.at[0, pl.ds(m * T, T)], rows, S_ROWS, I_ROWS)
    project(2)
    xb = [to_heads_b("qkv", qkv, qkvb, k) for k in (1, 2, 3)]
    for d in xb:
        d.start()
    lb = to_heads_b_own("qkv", qkv, qkvb, L0 + 1)
    lb.start()

    @pl.loop(0, 2)
    def _(s):
        project(s)

    xa = to_heads_a("qkv", qkv, qkva)
    xa.start()
    la = to_heads_a_own("qkv", qkv, qkva, L0)
    la.start()

    def weights_ready(step):
        if not aligned:
            return
        if step == 0:
            for a in (U_, O_):
                ag2(a)
        elif step == 1:
            send_cot((2,))
        elif step == 2:
            z_wait("D", 3)
            unflatten(D_, dp)
            ag1(D_)
        elif step == 3:
            for a in (U_, O_):
                ag3(a)
            ag2(D_)
        elif step == 4:
            send_cot((0, 1))
            for a in (U_, O_):
                ag4(a)
        elif step == 5:
            ag3(D_)
        elif step == 6:
            ag4(D_)
            for key in CH:
                for k in (1, 2, 3):
                    z_send(key, k, done=True)

    def key_bias(slot):
        parts = []
        at = lax.broadcasted_iota(i32, (T, 128), 0).astype(f32)
        for b in range(4):
            limit = cnt[slot, b : b + 1, :].astype(f32)
            parts.append(jnp.where(at < limit, 0.0, NEG))
        return jnp.concatenate(parts, axis=0).astype(bf16)

    bias = R["bias"]
    bias[0] = key_bias(0)
    bias[1] = key_bias(2)
    QT = 256
    N = 4 * T

    def half(i, x):
        return jnp.where(lane // 64 == i, x, jnp.zeros_like(x))

    def key_side(k2, b, i):
        spot = 64 * (1 - i)
        return jnp.where(lane // 64 == i, k2, jnp.where(lane == spot, b, jnp.zeros_like(b)))

    def query_side(q2, i):
        spot = 64 * (1 - i)
        return jnp.where(lane // 64 == i, q2, jnp.where(lane == spot, 1.0, 0.0).astype(bf16))

    SC = 0.125 * LOG2E

    def attend(src, dst, col, bi, sel, lrow):
        cols = ds128(col, 128)
        k2 = src[1, :, cols]
        b = bias[bi]
        keys = [key_side(k2, b, i) for i in sel]

        @pl.loop(0, N // QT)
        def _(q):
            r = ds128(q * QT, QT)
            q2 = src[0, r, cols]
            v2 = src[2, :, cols]
            outs = []
            for n, i in enumerate(sel):
                s = nt(query_side(q2, i), keys[n])
                top = jnp.max(s, axis=1, keepdims=True) * SC
                p = jnp.exp2(s * SC - top)
                total = jnp.sum(p, axis=1, keepdims=True)
                outs.append(nn(p.astype(bf16), v2) / total)
                full_total = jnp.broadcast_to(top + jnp.log2(total), (QT, 128)).T
                lse[pl.ds(lrow + n, 1), r] = full_total[0:1, :]
            if len(sel) == 2:
                o = jnp.where(lane < 64, outs[0], outs[1])
            else:
                o = jnp.where(lane // 64 == sel[0], outs[0], 0.0)
            dst[0, r, cols] = o.astype(bf16)

    weights_ready(2)
    la.wait()
    wait_a("qkv", qkva, True)

    for t in range(2):
        attend(qkva, atta, t * 128, 0, (0, 1), 2 * t)
        weights_ready(t)
    lb.wait()
    wait_b_heads("qkv", qkvb)
    attend(qkvb, attb, c * 128, 1, (0, 1), 6)
    weights_ready(3)
    attend(qkvb, attb, (1 - c) * 128, 1, (c,), 8)
    xattb = [from_heads_b("att", attb, 0, k) for k in (1, 2, 3)]
    for d in xattb:
        d.start()
    lattb = from_heads_b_own(attb, L0 + 3)
    lattb.start()
    attend(qkva, atta, 256, 0, (0, 1), 4)
    xatt = from_heads_a("att", atta, att)
    xatt.start()
    latt = from_heads_a_own("att", atta, att, L0 + 2)
    latt.start()
    weights_ready(4)
    xa.wait_send()
    for d in xb:
        d.wait_send()
    latt.wait()
    wait_a("att", att, False)

    def slot_rows(s):
        return pl.ds(mult(s * T, T), T)

    def live_of(s):
        b = 2 * c + s if s < 2 else g
        at = lax.broadcasted_iota(i32, (T, 128), 0).astype(f32)
        pick = jnp.zeros((1, 128), f32)
        for i in range(4):
            pick = pick + jnp.where(b == i, cnt[s, i : i + 1, :].astype(f32), 0.0)
        return jnp.where(at < pick, 1.0, 0.0)[:, 0:1]

    for s in range(3):
        if s == 2:
            lattb.wait()
            wait_b_tokens("att", 1)
            merge_b(att, 0, 0)
            weights_ready(5)
        r = pl.ds(s * T, T)
        v = nn(att[0, r, :], wblock(R["wo"])) + vec(V_OB) + rows[s].astype(f32)
        mid[r, :] = v
        n, _ = normalise(v)
        nbuf[s] = (n * vec(V_MG) + vec(V_MS)).astype(bf16)
    weights_ready(6)
    FT = FR

    ub = R["ub"]
    outer = branch = cot

    def hidden(s, up, j):
        hid = nn(nbuf[s], up) + ub[pl.ds(j, 1), :]
        phi_c = 0.5 * (1.0 + lax.erf(hid * 0.7071067811865476))
        return hid, phi_c

    def outer_rows():
        for s in (2, 0, 1):
            recv(cot.at[s], I_COT + s)
            o = live_of(s) * cot[s].astype(f32)
            cot[s] = o.astype(bf16)
            part = col_sum(o)
            if s == 2:
                vg[V_DB : V_DB + 1, :] = part
            else:
                vg[V_DB : V_DB + 1, :] += part

    def feed(acc, n2t, tile):
        act_s, gh_s = tile.at[0], tile.at[1]
        for s in range(3):
            n2t[:, s * T : (s + 1) * T] = nbuf[s].T
            acc[s * T : (s + 1) * T, :] = mid[s * T : (s + 1) * T, :] + vec(V_DB)

        @pl.loop(0, dps)
        def _(j):
            up = wblock(R["wu"], ds128(j * FT, FT))
            down = R["wd"][j]

            @pl.loop(0, 3)
            def _(s):
                hid, phi_c = hidden(s, up, j)
                acc[slot_rows(s), :] += nn((hid * phi_c).astype(bf16), down)

        for s in (2, 0, 1):
            r = pl.ds(s * T, T)
            ysend[s] = (live_of(s) * acc[r, :]).astype(bf16)
            move_home(s, ysend.at[s], act, S_ACT, I_ACT)
            acc[r, :] = jnp.zeros((T, W), f32)
        outer_rows()

        def tile_pair(i):
            @pl.loop(2 * i, 2 * i + 2)
            def _(j):
                one_tile(j)

        def one_tile(j):
            cols = ds128(j * FT, FT)
            up = wblock(R["wu"], cols)
            down = R["wd"][j]

            @pl.loop(0, 3, init_carry=jnp.zeros((1, FT), f32))
            def bias_part(s, carry):
                r = slot_rows(s)
                hid, phi_c = hidden(s, up, j)
                act_s[r, :] = (hid * phi_c).astype(bf16)
                slope = phi_c + hid * jnp.exp2(hid * hid * (-0.5 * LOG2E)) * 0.3989422804014327
                gh = (nt(outer[s], down) * slope).astype(bf16)
                gh_s[r, :] = gh
                acc[r, :] += nt(gh, up)
                return carry + col_sum(gh.astype(f32))

            ub[pl.ds(j, 1), :] = bias_part
            R["wd"][j] = tn(act_s[...], outer[...].reshape(3 * T, W)).astype(bf16)
            R["wu"][:, :, cols] = nn(n2t[...], gh_s[...]).astype(bf16).reshape(dps, KR, FT)

        for i in range(dps // 2):
            tile_pair(i)
            if aligned:
                rs_core("D", i).start()
                if i == 1 or i == 3:
                    rs1("U%d" % (i // 2))
                if i > 0:
                    rs2_pair("D", i - 1)
                if i == 2:
                    rs2("U0")
                if i == 3:
                    rs3("U0")

        for s in (2, 0, 1):
            r = pl.ds(s * T, T)
            n, inv = normalise(mid[r, :])
            e_ = acc[r, :]
            gm = outer[s].astype(f32) + norm_back(e_, n, inv, vec(V_MG))
            mid[r, :] = gm
            low = gm.astype(bf16)
            branch[s] = low
            for i, part in ((V_MG, col_sum(e_ * n)), (V_MS, col_sum(e_)), (V_OB, col_sum(low.astype(f32)))):
                if s == 2:
                    vg[i : i + 1, :] = part
                else:
                    vg[i : i + 1, :] += part
            nbuf[s] = nt(low, wblock(R["wo"])).astype(bf16)
            send_do(s)
        for q in range(2):
            piece = tn(att[0, :, q * HALF : (q + 1) * HALF], branch[...].reshape(3 * T, W)).astype(bf16)
            R["wo"][q * (dps // 2) : (q + 1) * (dps // 2)] = piece.reshape(dps // 2, KR, W)
        grads_move(0)

    def act_done():
        for s in range(3):
            move_home_done(s, ysend.at[s], act, S_ACT, I_ACT)

    do3 = R["nbuf"]

    def do_copies(s):
        if s < 2:
            i0 = EX["do"][0] if s == 0 else L0 + 4
            return [rcopy(do3.at[s, :, ds128(HALF * (1 - c), HALF)], doa.at[ds128(2 * T * c + s * T, T)], i0, i0, (other, z))]
        out = []
        for k in (1, 2, 3):
            t = lax.rem(g + k, 4)
            cols = ds128(HALF * lax.div(t, 2) + 128 * lax.rem(t, 2), 256)
            out.append(rcopy(do3.at[2, :, cols], dob.at[ds128(T * g, T)], EX["do"][2] + k, EX["do"][1] + k, dev_of(t)))
        return out

    def send_do(s):
        for d in do_copies(s):
            d.start()

    def grads_move(step):
        if not aligned:
            return
        if step == 0:
            rs1("O")
            rs2_pair("D", 3)
            rs2("U1")
            rs4("U0")
        elif step == 1:
            y_send("U0", 2)
        elif step == 2:
            rs2("O")
            rs3("D")
        elif step == 3:
            rs3("U1")
            rs3("O")
        elif step == 4:
            y_send("U0", 3)
            rs4("D")
            rs4("U1")
            rs4("O")
        elif step == 5:
            y_send("D", 2)
            y_send("U1", 2)
            y_send("O", 2)
        elif step == 6:
            y_send("U1", 3)
            y_final("U0")
        elif step == 7:
            y_send("D", 3)
            y_send("O", 3)
            y_final("U1")
        elif step == 8:
            y_final("D")
            y_final("O")

    per = W // FT
    for q in range(dps):
        R["ub"][q : q + 1, :] = vt[V_UB + q // per : V_UB + q // per + 1, (q % per) * FT : (q % per + 1) * FT]
    pl.run_scoped(
        feed,
        pltpu.VMEM((3 * T, W), f32),
        pltpu.VMEM((W, 3 * T), bf16),
        pltpu.VMEM((2, 3 * T, FT), bf16),
    )
    for q in range(dps):
        vg[V_UB + q // per : V_UB + q // per + 1, (q % per) * FT : (q % per + 1) * FT] = R["ub"][q : q + 1, :]

    for j in range(2):
        doa[ds128(2 * T * c + j * T, T), :] = do3[j, :, ds128(HALF * c, HALF)]
    dob[ds128(T * g, T), :] = do3[2, :, ds128(HALF * e + 128 * c, 256)]

    def attend_back(src, o_ref, d_ref, col, bi, sel, lrow, dk, dv, delta):
        cols = ds128(col, 128)
        k2 = src[1, :, cols]
        v2 = src[2, :, cols]
        kt = k2.T
        b = bias[bi]
        keys = [key_side(k2, b, i) for i in sel]
        dk[...] = jnp.zeros_like(dk)
        dv[...] = jnp.zeros_like(dv)
        prod = o_ref[0, :, cols].astype(f32) * d_ref[:, cols].astype(f32)
        hi = prod.astype(bf16)
        lo = (prod - hi.astype(f32)).astype(bf16)
        row = lax.broadcasted_iota(i32, (8, 128), 0)
        if len(sel) == 2:
            pickm = (row == lax.broadcasted_iota(i32, (8, 128), 1) // 64).astype(f32).astype(bf16)
        else:
            pickm = jnp.where(jnp.logical_and(row == 0, lane // 64 == sel[0]), 1.0, 0.0).astype(bf16)
        delta[...] = nt(pickm, hi) + nt(pickm, lo)

        @pl.loop(0, N // QT)
        def _(q):
            r = ds128(q * QT, QT)
            q2 = src[0, r, cols]
            d2 = d_ref[r, cols]
            dks, dvs, dqs = [], [], []
            for n, i in enumerate(sel):
                qm, dm = half(i, q2), half(i, d2)
                s = nt(keys[n], query_side(q2, i))
                p = jnp.exp2(s * SC - lse[pl.ds(lrow + n, 1), r])
                dp_ = nt(v2, dm)
                ds_ = (p * (dp_ - delta[pl.ds(n, 1), r])).astype(bf16)
                dvs.append(nn(p.astype(bf16), dm))
                dks.append(nn(ds_, qm))
                dqs.append(nn(kt, ds_).T if len(sel) == 1 else nn(kt[64 * i : 64 * i + 64], ds_))
            if len(sel) == 2:
                dk[...] += dks[0] + dks[1]
                dv[...] += dvs[0] + dvs[1]
                dq = jnp.concatenate(dqs, axis=0).T
            else:
                dk[...] += dks[0]
                dv[...] += dvs[0]
                dq = half(sel[0], dqs[0])
            src[0, r, cols] = (dq * 0.125).astype(bf16)

        src[1, :, cols] = (dk[...] * 0.125).astype(bf16)
        src[2, :, cols] = dv[...].astype(bf16)

    I_DQA = take(6)

    def dq_copy(t):
        sref = qkva.at[:, ds128(2 * T * (1 - c), 2 * T), pl.ds(t * 128, 128)]
        dref = qkv.at[:, pl.ds(0, 2 * T), ds128(HALF * c + t * 128, 128)]
        return rcopy(sref, dref, I_DQA + t, I_DQA + t, (other, z))

    def dq_own(t):
        sref = qkva.at[:, ds128(2 * T * c, 2 * T), pl.ds(t * 128, 128)]
        dref = qkv.at[:, pl.ds(0, 2 * T), ds128(HALF * c + t * 128, 128)]
        return pltpu.make_async_copy(sref, dref, rs.at[I_DQA + 3 + t])

    def strips(t, r):
        return jnp.concatenate([qkv[j, r, k * HALF + t * 128 : k * HALF + (t + 1) * 128] for j in range(3) for k in range(2)], axis=1)

    gsend = cot
    if aligned:
        vx = R["vx"]
        I_VEC = take(3)
        I_VEZ = take(4)
        pairs = (other, dp + dx, dp + dy)

    def vec_copy(i):
        return rcopy(vg, vx.at[i], I_VEC + i, I_VEC + i, (pairs[i], z))

    def vec_add(i):
        vec_copy(i).wait()
        vg[...] += vx[i]

    def vec_z(k):
        return rcopy(vg, vx.at[2 + k], I_VEZ + k, I_VEZ + k, (dp, lax.rem(z + k, 4)))

    def rows_back(s, e_):
        r = pl.ds(s * T, T)
        n, inv = normalise(rows[s].astype(f32))
        gsend[s] = (mid[r, :] + norm_back(e_, n, inv, vec(V_NG))).astype(bf16)
        move_home(s, gsend.at[s], grh, S_GR, I_GR)
        parts = (
            (V_NG, col_sum(e_ * n)),
            (V_NS, col_sum(e_)),
            (V_QB, col_sum(qkv[0, r, :].astype(f32))),
            (V_VB, col_sum(qkv[2, r, :].astype(f32))),
        )
        for i, part in parts:
            if s == 2:
                vg[i : i + 1, :] = part
            else:
                vg[i : i + 1, :] += part

    def close_group(t, ebuf):
        dq_own(t).wait()
        recv(qkv.at[:, pl.ds(0, 2 * T), ds128(HALF * (1 - c) + t * 128, 128)], I_DQA + t)
        for s in range(2):
            part = nt(strips(t, pl.ds(s * T, T)), group(t))
            if t == 0:
                ebuf[s] = part
            else:
                ebuf[s] += part
        w = tn(nbuf[...].reshape(3 * T, W), strips(t, pl.ds(0, 3 * T))).astype(bf16)
        R["wq"][:, :, t * W : (t + 1) * W] = w.reshape(dps, KR, W)
        if aligned:
            rs1("Q%d" % t)

    def back(dk, dv, delta, ebuf):
        for k in (1, 2, 3):
            recv(dob.at[ds128(T * lax.rem(g + 4 - k, 4), T)], EX["do"][1] + k)
        attend_back(qkvb, attb, dob, c * 128, 1, (0, 1), 6, dk, dv, delta)
        grads_move(1)
        attend_back(qkvb, attb, dob, (1 - c) * 128, 1, (c,), 8, dk, dv, delta)
        for d in xattb:
            d.wait_send()
        for k in (1, 2, 3):
            from_heads_b("dqkv", qkvb, 0, k).start()
        from_heads_b_own(qkvb, L0 + 6).start()
        grads_move(2)
        recv(doa.at[ds128(2 * T * (1 - c), T)], EX["do"][0])
        recv(doa.at[ds128(2 * T * (1 - c) + T, T)], L0 + 4)
        attend_back(qkva, atta, doa, 0, 0, (0, 1), 0, dk, dv, delta)
        dq_copy(0).start()
        dq_own(0).start()
        grads_move(3)
        for s in range(3):
            for d in do_copies(s):
                d.wait_send()
        for s in range(3):
            normed_rows(s)
        for m in range(3):
            move_out_done(m, R["cnth"].at[m], cnt, S_CNT, I_CNT)
            move_out_done(m, R["cotangent"].at[m], cot, S_COT, I_COT)
        attend_back(qkva, atta, doa, 128, 0, (0, 1), 2, dk, dv, delta)
        dq_copy(1).start()
        dq_own(1).start()
        grads_move(4)
        from_heads_b_own(qkvb, L0 + 6).wait()
        wait_b_tokens("dqkv", 3)
        for j in range(3):
            merge_b(qkv, j, j)
        r = pl.ds(2 * T, T)
        e_ = nt(strips(0, r), group(0)) + nt(strips(1, r), group(1)) + nt(strips(2, r), group(2))
        rows_back(2, e_)
        close_group(0, ebuf)
        grads_move(5)
        attend_back(qkva, atta, doa, 256, 0, (0, 1), 4, dk, dv, delta)
        dq_copy(2).start()
        dq_own(2).start()
        close_group(1, ebuf)
        if aligned:
            rs2("Q0")
        close_group(2, ebuf)
        grads_move(6)
        rows_back(0, ebuf[0])
        if aligned:
            rs3("Q0")
            rs2("Q1")
        rows_back(1, ebuf[1])
        vg[12:16, :] = jnp.zeros((4, W), f32)
        if aligned:
            vec_copy(0).start()
            rs2("Q2")
            rs4("Q0")
            rs3("Q1")
            grads_move(7)
            vec_add(0)
            vec_copy(1).start()
            rs3("Q2")
            rs4("Q1")
            y_send("Q0", 2)
            vec_add(1)
            vec_copy(2).start()
            rs4("Q2")
            y_send("Q1", 2)
            y_send("Q0", 3)
            vec_add(2)
            for k in (1, 2, 3):
                vec_z(k).start()
            grads_move(8)
            y_send("Q2", 2)
            y_send("Q1", 3)
            y_final("Q0")
            y_send("Q2", 3)
            y_final("Q1")
            for k in (1, 2, 3):
                recv(vx.at[2 + k], I_VEZ + k)
            for k in (1, 2, 3):
                vec_z(k).wait_send()
            total = vg[...]
            for k in (1, 2, 3):
                total = total + vx[2 + k]
            at = dp * 4 + z
            n1, n2 = W // 32, F // 32
            R["vs"][...] = pltpu.roll(total, lax.rem(W - at * n1, W), axis=1)[:, 0:128]
            line = lax.broadcasted_iota(i32, (16, W), 0)
            per_row = W // n2
            ubr = jnp.sum(jnp.where(line == V_UB + lax.div(at, per_row), total, 0.0), axis=0, keepdims=True)
            ubr = jnp.broadcast_to(ubr, (8, W))
            R["vs"][8:16, :] = pltpu.roll(ubr, lax.rem(W - lax.rem(at, per_row) * n2, W), axis=1)[:, 0:128]
            y_final("Q2")
            for key in GC:
                rs_done(key)

    pl.run_scoped(back, pltpu.VMEM((N, 128), f32), pltpu.VMEM((N, 128), f32), pltpu.VMEM((8, N), f32), pltpu.VMEM((2, T, W), f32))
    xatt.wait_send()
    if not aligned:
        save = [pltpu.make_async_copy(arrays[i], R[n], rs.at[L0 + 8 + i]) for i, n in enumerate(("gq", "go", "gu", "gd"))]
        for d in save:
            d.start()
        for d in save:
            d.wait()
    for t in range(3):
        dq_copy(t).wait_send()
    for k in (1, 2, 3):
        from_heads_b("dqkv", qkvb, 0, k).wait_send()
    act_done()
    for s in range(3):
        move_home_done(s, gsend.at[s], grh, S_GR, I_GR)
    for m in range(3):
        arrived_home(m, act, I_ACT)
        arrived_home(m, grh, I_GR)
    assert count[0] <= cfg["sems"], count[0]


def finish_kernel(sizes, keep, grads, act_in, *refs):
    n = 0 if sizes is None else 5
    act_out, out = refs[n], refs[n + 1]
    places = lax.broadcasted_iota(i32, (out.shape[1], keep.shape[2]), 0)
    out[0] = nn((places == keep[0]).astype(f32).astype(bf16), grads[0])
    act_out[...] = act_in[...]
    if sizes is not None:

        @pl.when(pl.program_id(0) == 0)
        def _():
            for i in range(4):
                refs[n + 2 + i][...] = refs[i][...]
            for i, width in enumerate(sizes):
                refs[n + 6 + i][...] = refs[4][i : i + 1, 0:width]


def body(patches, keep_index, shard_counts, cotangent, *shards):
    ng, ns, wq, qb, vb, wo, ob, mg, ms, wu, ub, wd, db = shards
    batches, _, patch, width = patches.shape
    tokens = keep_index.shape[2]
    dp_size, blk_size = lax.axis_size("dp"), lax.axis_size("blk")
    devices = dp_size * blk_size
    ff = wu.shape[1]
    aligned = dp_size == 8 and blk_size == 4
    dps = 8
    kr, fr = width // dps, ff // dps
    vectors = jnp.stack([ng, ns, qb, vb, ob, mg, ms, db])
    if aligned:
        own = jnp.pad(vectors, ((0, 0), (0, 128 - vectors.shape[1])))
        own_ub = jnp.pad(ub[None], ((0, 7), (0, 128 - ub.shape[0])))
        table = jnp.concatenate([own, own_ub])
        weights = (wq, wo, wu, wd)
        pieces = [w.size // 128 for w in weights] + [16]
        flat = [sum(pieces[:i]) for i in range(6)]
    else:
        axes = ("dp", "blk")
        table = lax.all_gather(vectors, axes, axis=1, tiled=True).astype(f32)
        table_ub = lax.all_gather(ub, axes, axis=0, tiled=True).astype(f32).reshape(ff // width, width)
        table = jnp.concatenate([table, table_ub, jnp.zeros((16 - 8 - ff // width, width), f32)])
        weights = tuple(lax.all_gather(w, axes, axis=0, tiled=True) for w in (wq, wo, wu, wd))
        weights = tuple(w.reshape(dps, -1, w.shape[1]) for w in weights)
        held = weights[0].reshape(dps, kr, 3, 2, 3, width // 6).transpose(0, 1, 4, 2, 3, 5).reshape(dps, kr, 3 * width)
        weights = (held, *weights[1:])
        flat = None
    cfg = dict(aligned=aligned, dps=dps, tokens=tokens, width=width, ff=ff, patch=patch, flat=flat, sems=320)
    keep = keep_index
    ins = [
        ("patches", patches[:, 0], ANY),
        ("keep", keep, VMEM),
        ("counts", shard_counts, SMEM),
        ("cotangent", cotangent[:, 0], ANY),
    ]
    ins += [(n, w, VMEM if aligned else ANY) for n, w in zip(("sq", "so", "su", "sd"), weights)]
    ins.append(("sv", table, VMEM))
    out = [
        ("act", (3, tokens, width), bf16, ANY),
        ("grh", (3, tokens, width), bf16, ANY),
        ("vg", (16, width), f32, VMEM),
    ]
    full = {"q": (dps, kr, 3 * width), "o": (dps, kr, width), "u": (dps, kr, ff), "d": (dps, fr, width)}
    for i, n in enumerate("qoud"):
        if aligned:
            out.append(("g" + n, weights[i].shape, f32, VMEM))
        else:
            out.append(("g" + n, full[n], bf16, ANY))
    if aligned:
        out.append(("vs", (16, 128), f32, VMEM))
    t3 = 3 * tokens
    scratch = [("w" + n, full[n], bf16) for n in "qoud"]
    scratch += [
        ("rows", (3, tokens, width), bf16),
        ("cot", (3, tokens, width), bf16),
        ("cnt", (3, 16, 128), bf16),
        ("cnth", (3, 16, 128), bf16),
        ("nbuf", (3, tokens, width), bf16),
        ("qkv", (3, t3, width), bf16),
        ("qkva", (3, 4 * tokens, width // 2), bf16),
        ("qkvb", (3, 4 * tokens, 256), bf16),
        ("atta", (1, 4 * tokens, width // 2), bf16),
        ("attb", (1, 4 * tokens, 256), bf16),
        ("att", (1, t3, width), bf16),
        ("fromb", (4, 3, tokens, 256), bf16),
        ("doa", (4 * tokens, width // 2), bf16),
        ("dob", (4 * tokens, 256), bf16),
        ("mid", (t3, width), f32),
        ("ysend", (3, tokens, width), bf16),
        ("vt", (16, width), f32),
        ("lse", (16, 4 * tokens), f32),
        ("bias", (2, 4 * tokens, 128), bf16),
        ("ub", (dps, fr), f32),
    ]
    if aligned:
        scratch += [
            ("zbuf", (4, flat[5], 128), bf16),
            ("zrr", (3, flat[4], 128), bf16),
            ("zrl", (3, flat[4], 128), bf16),
            ("vw", (dps, 64, 128), bf16),
            ("vx", (6, 16, width), f32),
        ]
        scratch += [("rb1" + n, (4, *full[n][1:]), bf16) for n in "qoud"]
        scratch += [("rb2" + n, (3, *full[n][1:]), bf16) for n in "qoud"]
    names = [n for n, _, _ in scratch] + ["ss", "rs"]
    shapes = [pltpu.VMEM(s, d) for _, s, d in scratch] + [pltpu.SemaphoreType.DMA((cfg["sems"],))] * 2
    flops = 6 * 3 * tokens * (4 * width * width + 2 * width * ff)
    results = pl.pallas_call(
        functools.partial(layer_kernel, cfg, [n for n, _, _ in ins], [n for n, *_ in out], names),
        out_shape=[jax.ShapeDtypeStruct(s, d) for _, s, d, _ in out],
        in_specs=[s for _, _, s in ins],
        out_specs=[s for *_, s in out],
        scratch_shapes=shapes,
        compiler_params=pltpu.CompilerParams(collective_id=0, has_side_effects=True, vmem_limit_bytes=64 * 1024 * 1024 - 512 * 1024),
        cost_estimate=pl.CostEstimate(flops=flops, bytes_accessed=50_000_000, transcendentals=0),
        name="layer",
    )(*[a for _, a, _ in ins])
    act, grh, vg, gq, go, gu, gd = results[:7]
    whole = lambda v: pl.BlockSpec(v, lambda m: (0,) * len(v))
    step = lambda *v: pl.BlockSpec((1, *v), lambda m: (m, 0, 0))
    n = width // devices
    sizes = [n] * 8 + [ff // devices] if aligned else None
    extra = [gq, go, gu, gd, results[7]] if aligned else []
    shapes = [(3, tokens, width, bf16), (3, patch, width, f32)]
    specs = [step(tokens, width), step(patch, width)]
    if aligned:
        shapes += [(*v.shape, f32) for v in extra[:4]] + [(1, v, f32) for v in sizes]
        specs += [whole(v.shape) for v in extra[:4]] + [whole((1, v)) for v in sizes]
    done = pl.pallas_call(
        functools.partial(finish_kernel, sizes),
        grid=(3,),
        in_specs=[step(1, tokens), step(tokens, width), step(tokens, width)] + [whole(v.shape) for v in extra],
        out_specs=specs,
        out_shape=[jax.ShapeDtypeStruct(v[:-1], v[-1]) for v in shapes],
        compiler_params=pltpu.CompilerParams(vmem_limit_bytes=64 * 1024 * 1024 - 512 * 1024),
        name="finish",
    )(keep, grh, act, *extra)
    act, patch_grad = done[:2]
    if aligned:
        gq, go, gu, gd = done[2:6]
        piece = [v.reshape(-1) for v in done[6:]]
    else:
        axes = ("dp", "blk")
        small = [vg[:8].reshape(8, devices, n).transpose(1, 0, 2).reshape(devices, -1), vg[8 : 8 + ff // width].reshape(devices, -1)]
        small = lax.psum_scatter(jnp.concatenate(small, axis=1), axes, scatter_dimension=0, tiled=True)[0]
        piece = [small[i * n : (i + 1) * n] for i in range(8)] + [small[8 * n :]]
        gq = gq.reshape(dps, kr, 3, 3, 2, width // 6).transpose(0, 1, 3, 4, 2, 5).reshape(dps, kr, 3 * width)
        gq, go, gu, gd = (
            lax.psum_scatter(w.reshape(-1, w.shape[-1]).astype(f32), axes, scatter_dimension=0, tiled=True) for w in (gq, go, gu, gd)
        )
    return (
        act[:, None],
        patch_grad[:, None],
        piece[V_NG],
        piece[V_NS],
        gq,
        piece[V_QB],
        piece[V_VB],
        go,
        piece[V_OB],
        piece[V_MG],
        piece[V_MS],
        gu,
        piece[V_UB],
        gd,
        piece[V_DB],
    )


def solution(mesh):
    vec, mat = P(("dp", "blk")), P(("dp", "blk"), None)
    tok = P(None, "dp", "blk", None)
    params = (vec, vec, mat, vec, vec, mat, vec, vec, vec, mat, vec, mat, vec)
    in_specs = (tok, P(None, "dp", "blk"), P(None, "dp", None), tok) + params
    out_specs = (tok, tok) + params
    return jax.shard_map(body, mesh=mesh, in_specs=in_specs, out_specs=out_specs, check_vma=False)
```

```python
import functools

import jax
import jax.numpy as jnp
from jax import lax
from jax.experimental import pallas as pl
from jax.experimental.pallas import tpu as pltpu
from jax.sharding import PartitionSpec as P

MESH = pl.DeviceIdType.MESH
ANY = pl.BlockSpec(memory_space=pl.ANY)
VMEM = pl.BlockSpec(memory_space=pltpu.VMEM)
SMEM = pl.BlockSpec(memory_space=pltpu.SMEM)
f32, bf16, i32 = jnp.float32, jnp.bfloat16, jnp.int32

EPSILON = 1e-06
LOG2E = 1.4426950408889634
NEG = -1e30


def nn(a, b):
    return lax.dot_general(a, b, (((1,), (0,)), ((), ())), preferred_element_type=f32)


def nt(a, b):
    return lax.dot_general(a, b, (((1,), (1,)), ((), ())), preferred_element_type=f32)


def tn(a, b):
    return lax.dot_general(a, b, (((0,), (0,)), ((), ())), preferred_element_type=f32)


def mult(x, k):
    return x if isinstance(x, int) else pl.multiple_of(x, k)


def normalise(v):
    centred = v - jnp.mean(v, axis=1, keepdims=True)
    inv = lax.rsqrt(jnp.mean(centred * centred, axis=1, keepdims=True) + EPSILON)
    return centred * inv, inv


def norm_back(e, n, inv, gain):
    f = e * gain
    return inv * (f - jnp.mean(f, axis=1, keepdims=True) - n * jnp.mean(f * n, axis=1, keepdims=True))


def col_sum(v):
    return jnp.sum(v, axis=0, keepdims=True)


def group_tile(t):
    return t % 3 * 6 + t // 6 * 2 + t % 6 // 3


def natural_tile(p):
    return p % 6 // 2 * 6 + p % 2 * 3 + p // 6


V_NG, V_NS, V_QB, V_VB, V_OB, V_MG, V_MS, V_DB, V_UB = range(9)


def layer_kernel(cfg, names_in, names_out, names_scratch, *refs):
    R = dict(zip(names_in + names_out + names_scratch, refs, strict=True))
    aligned, dps = cfg["aligned"], cfg["dps"]
    T, W, F = cfg["tokens"], cfg["width"], cfg["ff"]
    KR = W // dps
    FR = F // dps
    HALF = W // 2
    dp, z = lax.axis_index("dp"), lax.axis_index("blk")
    c = lax.rem(dp, 2)
    base = dp - c
    h, e = lax.div(z, 2), lax.rem(z, 2)
    g = 2 * e + c
    other = base + 1 - c
    ss, rs = R["ss"], R["rs"]
    count = [0]

    def take(n=1):
        count[0] += n
        return count[0] - n

    def rcopy(src, dst, s, r, dev):
        return pltpu.make_async_remote_copy(
            src_ref=src, dst_ref=dst, send_sem=ss.at[s], recv_sem=rs.at[r], device_id=dev, device_id_type=MESH
        )

    def recv(dst, r, dev=None):
        rcopy(dst, dst, 0, r, (other, z) if dev is None else dev).wait_recv()

    bar = pltpu.get_barrier_semaphore()
    peers = []
    for k in range(1, 8):
        j = lax.rem(c * 4 + z + k, 8)
        peers.append((base + lax.div(j, 4), lax.rem(j, 4)))
    if aligned:
        dx = 2 - 4 * lax.rem(lax.div(dp, 2), 2)
        dy = 4 - 8 * lax.div(dp, 4)
        p1, p2, p3 = dp + (1 - c) * dx + c * dy, dp + c * dx + (1 - c) * dy, dp + dx + dy
        peers += [(p1, z), (p2, z)]
    for dev in peers:
        pl.semaphore_signal(bar, inc=1, device_id=dev, device_id_type=MESH)

    def owner(m):
        if m < 2:
            return lax.div(z, 2), 2 * c + m, lax.rem(z, 2)
        return lax.rem(z, 2), 2 * c + lax.div(z, 2), 2

    def home(s):
        if s < 2:
            return h, 2 * c + s
        return h, 2 * e + c

    def move_out(m, src, dst, sid, rid):
        tc, tz, slot = owner(m)
        own = jnp.logical_and(tc == c, tz == z)

        @pl.when(own)
        def _():
            pltpu.make_async_copy(src, dst.at[slot], rs.at[rid + slot]).start()

        @pl.when(jnp.logical_not(own))
        def _():
            rcopy(src, dst.at[slot], sid + m, rid + slot, (base + tc, tz)).start()

    def move_out_done(m, src, dst, sid, rid):
        tc, tz, slot = owner(m)
        own = jnp.logical_and(tc == c, tz == z)

        @pl.when(jnp.logical_not(own))
        def _():
            rcopy(src, dst.at[slot], sid + m, rid + slot, (base + tc, tz)).wait_send()

    def move_home(s, src, dst, sid, rid):
        tc, tz = home(s)
        m = e if s < 2 else 2
        own = jnp.logical_and(tc == c, tz == z)

        @pl.when(own)
        def _():
            pltpu.make_async_copy(src, dst.at[m], ss.at[sid + s]).start()

        @pl.when(jnp.logical_not(own))
        def _():
            rcopy(src, dst.at[m], sid + s, rid + m, (base + tc, tz)).start()

    def move_home_done(s, src, dst, sid, rid):
        tc, tz = home(s)
        m = e if s < 2 else 2
        own = jnp.logical_and(tc == c, tz == z)

        @pl.when(own)
        def _():
            pltpu.make_async_copy(src, dst.at[m], ss.at[sid + s]).wait()

        @pl.when(jnp.logical_not(own))
        def _():
            rcopy(src, dst.at[m], sid + s, rid + m, (base + tc, tz)).wait_send()

    def arrived_home(m, dst, rid):
        tc, tz, _ = owner(m)

        @pl.when(jnp.logical_not(jnp.logical_and(tc == c, tz == z)))
        def _():
            recv(dst.at[m], rid + m)

    arrays = [R["wq"], R["wo"], R["wu"], R["wd"]]
    Q_, O_, U_, D_ = 0, 1, 2, 3
    if aligned:
        zbuf, zrr, zrl = R["zbuf"], R["zrr"], R["zrl"]
        flat = cfg["flat"]
        CH = {"Q": (0, flat[1]), "OU": (flat[1], flat[3]), "D": (flat[3], flat[4]), "V": (flat[4], flat[5])}
        ZR = {k: take(3) - 1 for k in CH}
        ZL = {k: take(3) - 1 for k in CH}
        wide = W // 128
        GC = {"D": (D_, 0, wide), "O": (O_, 0, wide)}
        for i in range(2):
            GC["U%d" % i] = (U_, i * F // 256, (i + 1) * F // 256)
        for i in range(3):
            GC["Q%d" % i] = (Q_, i * wide, (i + 1) * wide)
        YR = {k: take(3) - 1 for k in GC}
        YL = {k: take(3) - 1 for k in GC}
        gathered = arrays + [R["vw"]]
        XY = [take(3) for _ in range(5)]
        CR = [take(4) for _ in range(5)]
        R1 = {k: take(4) for k in GC}
        R2 = {k: take(3) for k in GC}

        def z_send(key, k, done=False):
            r0, r1 = CH[key]
            rows = pl.ds(r0, r1 - r0)
            right = jnp.logical_and(z < 3, z - (k - 1) >= 0)
            left = jnp.logical_and(z > 0, z + (k - 1) <= 3)

            @pl.when(right)
            def _():
                ref = zbuf.at[z - (k - 1), rows]
                d = rcopy(ref, ref, ZR[key] + k, ZR[key] + k, (dp, z + 1))
                d.wait_send() if done else d.start()

            @pl.when(left)
            def _():
                ref = zbuf.at[z + (k - 1), rows]
                d = rcopy(ref, ref, ZL[key] + k, ZL[key] + k, (dp, z - 1))
                d.wait_send() if done else d.start()

        def z_wait(key, k):
            r0, r1 = CH[key]
            rows = pl.ds(r0, r1 - r0)

            @pl.when(z - k >= 0)
            def _():
                recv(zbuf.at[z - k, rows], ZR[key] + k)

            @pl.when(z + k <= 3)
            def _():
                recv(zbuf.at[z + k, rows], ZL[key] + k)

        def flatten(a, ref, slot):
            if a == D_:
                n, rows = W // 128, FR // 4
            elif a == 4:
                n, rows = 1, 16
            else:
                n, rows = ref.shape[-1] // 128, KR // 4
            for t in range(n):
                cols = slice(t * 128, (t + 1) * 128)
                zbuf[slot, flat[a] + t * rows : flat[a] + (t + 1) * rows, :] = ref[:, cols]

        def place(a, t):
            return group_tile(t) if a == Q_ else t

        def unflatten(a, block):
            dst = gathered[a]
            if a == D_:
                n, rows = W // 128, FR // 4
            elif a == 4:
                n, rows = 1, 16
            else:
                n, rows = dst.shape[-1] // 128, KR // 4
            for s in range(4):
                for t in range(n):
                    p = place(a, t) * 128
                    dst[block, s * rows : (s + 1) * rows, p : p + 128] = zbuf[s, flat[a] + t * rows : flat[a] + (t + 1) * rows, :]

        def ag_copies(a):
            ref = gathered[a]

            def core(i):
                block = (dp, p1, p2, p3)[i]
                return rcopy(ref.at[block], ref.at[block], CR[a] + i, CR[a] + i, (other, z))

            return {
                "p1": lambda: rcopy(ref.at[dp], ref.at[dp], XY[a], XY[a], (p1, z)),
                "p2": lambda: rcopy(ref.at[dp], ref.at[dp], XY[a] + 1, XY[a] + 1, (p2, z)),
                "fw": lambda: rcopy(ref.at[p1], ref.at[p1], XY[a] + 2, XY[a] + 2, (p2, z)),
                "c0": lambda: core(0),
                "c1": lambda: core(1),
                "c2": lambda: core(2),
                "c3": lambda: core(3),
            }

        def ag1(a):
            d = ag_copies(a)
            d["p1"]().start()
            d["p2"]().start()
            d["c0"]().start()

        def ag2(a):
            d = ag_copies(a)
            ref = gathered[a]
            recv(ref.at[p1], XY[a])
            d["fw"]().start()
            d["c1"]().start()
            recv(ref.at[p2], XY[a] + 1)
            d["c2"]().start()

        def ag3(a):
            d = ag_copies(a)
            recv(gathered[a].at[p3], XY[a] + 2)
            d["c3"]().start()

        def ag4(a):
            d = ag_copies(a)
            for i, block in enumerate((dp, p2, p1, p3)):
                recv(gathered[a].at[block + other - dp], CR[a] + i)
            for k in d.values():
                k().wait_send()

        def blk_of(i):
            return 2 * i + c

        bufs1 = [R["rb1" + n] for n in "qoud"]
        bufs2 = [R["rb2" + n] for n in "qoud"]

        def cols_of(key):
            _, t0, t1 = GC[key]
            return pl.ds(t0 * 128, (t1 - t0) * 128)

        def block_of(key, block):
            return arrays[GC[key][0]].at[block, :, cols_of(key)]

        def view(bufs, key, i):
            return bufs[GC[key][0]].at[i, :, cols_of(key)]

        def rs_core(key, i):
            return rcopy(block_of(key, 2 * i + 1 - c), view(bufs1, key, i), R1[key] + i, R1[key] + i, (other, z))

        def rs1(key):
            for i in range(4):
                rs_core(key, i).start()

        def addto(key, block, parts):
            ref, cols = arrays[GC[key][0]], cols_of(key)
            rows = ref.shape[1]
            step = 48

            @pl.loop(0, rows // step)
            def _(q):
                r = pl.ds(mult(q * step, step), step)
                total = ref[block, r, cols].astype(f32)
                for p, i in parts:
                    total = total + p[GC[key][0]][i, r, cols].astype(f32)
                ref[block, r, cols] = total.astype(bf16)

        def rs_xy(key):
            i0 = R2[key]
            return {
                "diag": lambda: rcopy(block_of(key, p3), view(bufs2, key, 0), i0, i0, (p2, z)),
                "p2": lambda: rcopy(block_of(key, p2), view(bufs2, key, 1), i0 + 1, i0 + 1, (p2, z)),
                "p1": lambda: rcopy(block_of(key, p1), view(bufs2, key, 2), i0 + 2, i0 + 2, (p1, z)),
            }

        def rs2_pair(key, i):
            recv(view(bufs1, key, i), R1[key] + i)
            addto(key, blk_of(i), [(bufs1, i)])

            @pl.when(blk_of(i) == p3)
            def _():
                rs_xy(key)["diag"]().start()

            @pl.when(blk_of(i) == p2)
            def _():
                rs_xy(key)["p2"]().start()

        def rs2(key):
            for i in range(4):
                rs2_pair(key, i)

        def rs3(key):
            recv(view(bufs2, key, 0), R2[key])
            addto(key, p1, [(bufs2, 0)])
            rs_xy(key)["p1"]().start()

        def span(key):
            a, t0, t1 = GC[key]
            n = arrays[a].shape[1] // 4
            return a, n, flat[a] + t0 * n, (t1 - t0) * n

        def rs4(key):
            recv(view(bufs2, key, 1), R2[key] + 1)
            recv(view(bufs2, key, 2), R2[key] + 2)
            addto(key, dp, [(bufs2, 1), (bufs2, 2)])
            a, n, _, _ = span(key)
            for slot in range(4):
                for t in range(GC[key][1], GC[key][2]):
                    piece = arrays[a][dp, slot * n : (slot + 1) * n, t * 128 : (t + 1) * 128]
                    zbuf[slot, flat[a] + t * n : flat[a] + (t + 1) * n, :] = piece
            y_send(key, 1)

        def y_send(key, k, done=False):
            _, _, r0, rn = span(key)
            rows = pl.ds(r0, rn)
            to_right = z + 4 - k
            to_left = z - 4 + k

            @pl.when(jnp.logical_and(z < 3, to_right <= 3))
            def _():
                if k > 1 and not done:

                    @pl.when(z >= 1)
                    def _():
                        recv(zrr.at[k - 2, rows], YR[key] + k - 1)
                        zbuf[to_right, rows, :] = (zbuf[to_right, rows, :].astype(f32) + zrr[k - 2, rows, :].astype(f32)).astype(bf16)

                d = rcopy(zbuf.at[to_right, rows], zrr.at[k - 1, rows], YR[key] + k, YR[key] + k, (dp, z + 1))
                d.wait_send() if done else d.start()

            @pl.when(jnp.logical_and(z > 0, to_left >= 0))
            def _():
                if k > 1 and not done:

                    @pl.when(z <= 2)
                    def _():
                        recv(zrl.at[k - 2, rows], YL[key] + k - 1)
                        zbuf[to_left, rows, :] = (zbuf[to_left, rows, :].astype(f32) + zrl[k - 2, rows, :].astype(f32)).astype(bf16)

                d = rcopy(zbuf.at[to_left, rows], zrl.at[k - 1, rows], YL[key] + k, YL[key] + k, (dp, z - 1))
                d.wait_send() if done else d.start()

        def y_final(key):
            a, n, r0, rn = span(key)
            rows = pl.ds(r0, rn)

            @pl.when(z >= 1)
            def _():
                recv(zrr.at[2, rows], YR[key] + 3)

            @pl.when(z <= 2)
            def _():
                recv(zrl.at[2, rows], YL[key] + 3)

            for t in range(GC[key][1], GC[key][2]):
                piece = slice(flat[a] + t * n, flat[a] + (t + 1) * n)
                total = zbuf[z, piece, :].astype(f32)
                total = total + jnp.where(z >= 1, zrr[2, piece, :].astype(f32), 0.0)
                total = total + jnp.where(z <= 2, zrl[2, piece, :].astype(f32), 0.0)
                p = natural_tile(t) if a == Q_ else t
                outs[a][:, p * 128 : (p + 1) * 128] = total

        def rs_done(key):
            for k in (1, 2, 3):
                y_send(key, k, done=True)
            for i in range(4):
                rs_core(key, i).wait_send()
            for d in rs_xy(key).values():
                d().wait_send()

        outs = [R["gq"], R["go"], R["gu"], R["gd"]]

    I_ROWS, I_CNT, I_COT, I_ACT, I_GR = (take(3) for _ in range(5))
    S_ROWS, S_CNT, S_COT, S_ACT, S_GR = (take(3) for _ in range(5))
    EX = {}
    for k in ("qkv", "att", "do", "dqkv"):
        EX[k] = (take(1), take(4), take(4))
    L0 = take(12)

    rows, cot, cnt, nbuf = R["rows"], R["cot"], R["cnt"], R["nbuf"]
    qkv, qkva, qkvb = R["qkv"], R["qkva"], R["qkvb"]
    atta, attb, att, fromb = R["atta"], R["attb"], R["att"], R["fromb"]
    doa, dob, mid, vt, vg = R["doa"], R["dob"], R["mid"], R["vt"], R["vg"]
    lse, grh, keep, act, ysend = R["lse"], R["grh"], R["keep"], R["act"], R["ysend"]
    lane = lax.broadcasted_iota(i32, (1, 128), 1)

    if aligned:
        for a, name in enumerate(("sq", "so", "su", "sd", "sv")):
            flatten(a, R[name], z)
    for m in range(3):
        for b in range(4):
            R["cnth"][m, b : b + 1, :] = jnp.full((1, 128), R["counts"][m, 0, b], i32).astype(f32).astype(bf16)
        R["cnth"][m, 4:, :] = jnp.zeros((12, 128), bf16)

    def pick_rows(pbuf, psem):
        copies = [pltpu.make_async_copy(R["patches"].at[m], pbuf.at[m], psem.at[m]) for m in range(3)]
        for d in copies:
            d.start()
        pl.semaphore_wait(bar, len(peers))
        if aligned:
            z_send("Q", 1)
            z_send("V", 1)
            z_send("OU", 1)
        for m in range(3):
            copies[m].wait()
            spread = (lax.broadcasted_iota(i32, (cfg["patch"], T), 0) == keep[m]).astype(f32).astype(bf16)
            att[0, m * T : (m + 1) * T, :] = tn(spread, pbuf[m]).astype(bf16)

    pl.run_scoped(pick_rows, pltpu.VMEM((3, cfg["patch"], W), bf16), pltpu.SemaphoreType.DMA((3,)))

    def send_rows():
        for m in (2, 0, 1):
            move_out(m, att.at[0, pl.ds(m * T, T)], rows, S_ROWS, I_ROWS)
            move_out(m, R["cnth"].at[m], cnt, S_CNT, I_CNT)

    def send_cot(ms=(2, 0, 1)):
        for m in ms:
            move_out(m, R["cotangent"].at[m], cot, S_COT, I_COT)

    if aligned:
        z_wait("OU", 1)
        for key in "QV":
            z_wait(key, 1)
            z_send(key, 2)
        z_send("D", 1)
        for key in "QV":
            z_wait(key, 2)
            z_send(key, 3)
        z_send("OU", 2)
        for key in "QV":
            z_wait(key, 3)
        unflatten(Q_, dp)
        ag1(Q_)
        unflatten(4, dp)
        ag1(4)
        z_wait("OU", 2)
        z_wait("D", 1)
        z_send("OU", 3)
        z_send("D", 2)
        z_wait("D", 2)
        z_wait("OU", 3)
        z_send("D", 3)
    else:
        full = [pltpu.make_async_copy(R[n], arrays[i], rs.at[L0 + 8 + i]) for i, n in enumerate(("sq", "so", "su", "sd"))]
        for d in full:
            d.start()
        send_rows()
        send_cot()
    if aligned:
        ag2(Q_)
        ag2(4)
        send_rows()
        unflatten(O_, dp)
        ag1(O_)
        ag3(Q_)
        ag3(4)
        unflatten(U_, dp)
        ag4(4)
        ag4(Q_)
        ag1(U_)
        v = R["vw"][...].reshape(32 * 16, 128)
        to = lax.broadcasted_iota(i32, (128, W), 1)
        frm = lax.broadcasted_iota(i32, (128, W), 0)
        dev = lax.broadcasted_iota(i32, (512, W), 0) // 16
        col = lax.broadcasted_iota(i32, (512, W), 1)
        n1, n2 = W // 32, F // 32
        x1 = nn(v, (lax.rem(to, n1) == frm).astype(f32).astype(bf16))
        x1 = jnp.where(dev == col // n1, x1, 0.0)
        vt[0:16, :] = jnp.sum(x1.reshape(32, 16, W), axis=0)
        x2 = nn(v, (lax.rem(to, n2) == frm).astype(f32).astype(bf16))
        x2 = jnp.where(lax.rem(dev, W // n2) == col // n2, x2, 0.0)
        x2 = jnp.sum(x2.reshape(4, 8, 16, W), axis=1)
        for q in range(4):
            vt[V_UB + q : V_UB + q + 1, :] = x2[q, V_UB : V_UB + 1, :]
    else:
        vt[...] = R["sv"][...]

    def vec(i):
        return vt[i : i + 1, :]

    def normed_rows(s):
        n, _ = normalise(rows[s].astype(f32))
        nbuf[s] = (n * vec(V_NG) + vec(V_NS)).astype(bf16)

    for s in (2, 0, 1):
        recv(rows.at[s], I_ROWS + s)
        recv(cnt.at[s], I_CNT + s)
        normed_rows(s)
    if not aligned:
        for d in full:
            d.wait()

    def wblock(ref, cols=None):
        v = ref[...] if cols is None else ref[:, :, cols]
        return v.reshape(-1, v.shape[-1])

    def group(t):
        return wblock(R["wq"], slice(t * W, (t + 1) * W))

    def project(s):
        r = pl.ds(mult(s * T, T), T)
        for t in range(3):
            v = nn(nbuf[s], group(t))
            for j in range(3):
                for k in range(2):
                    at = k * HALF + t * 128
                    x = v[:, (2 * j + k) * 128 : (2 * j + k + 1) * 128]
                    if j != 1:
                        row = V_QB if j == 0 else V_VB
                        x = x + vt[row : row + 1, at : at + 128]
                    qkv[j, r, at : at + 128] = x.astype(bf16)

    def dev_of(i):
        return (base + lax.rem(i, 2), 2 * h + lax.div(i, 2))

    def ds128(x, n):
        return pl.ds(mult(x, 128), n)

    def to_heads_a(kind, src, dst):
        i0 = EX[kind][0]
        full_ = [slice(None)] * (len(src.shape) - 2)
        sref = src.at[(*full_, pl.ds(0, 2 * T), ds128(HALF * (1 - c), HALF))]
        dref = dst.at[(*full_, ds128(2 * T * c, 2 * T))]
        return rcopy(sref, dref, i0, i0, (other, z))

    def to_heads_a_own(kind, src, dst, lid):
        full_ = [slice(None)] * (len(src.shape) - 2)
        sref = src.at[(*full_, pl.ds(0, 2 * T), ds128(HALF * c, HALF))]
        dref = dst.at[(*full_, ds128(2 * T * c, 2 * T))]
        return pltpu.make_async_copy(sref, dref, rs.at[lid])

    def to_heads_b(kind, src, dst, k):
        _, rid, sid = EX[kind]
        full_ = [slice(None)] * (len(src.shape) - 2)
        t = lax.rem(g + k, 4)
        sref = src.at[(*full_, pl.ds(2 * T, T), ds128(HALF * lax.div(t, 2) + 128 * lax.rem(t, 2), 256))]
        dref = dst.at[(*full_, ds128(T * g, T))]
        return rcopy(sref, dref, sid + k, rid + k, dev_of(t))

    def to_heads_b_own(kind, src, dst, lid):
        full_ = [slice(None)] * (len(src.shape) - 2)
        sref = src.at[(*full_, pl.ds(2 * T, T), ds128(HALF * e + 128 * c, 256))]
        dref = dst.at[(*full_, ds128(T * g, T))]
        return pltpu.make_async_copy(sref, dref, rs.at[lid])

    def from_heads_a(kind, src, dst):
        i0 = EX[kind][0]
        full_ = [slice(None)] * (len(src.shape) - 2)
        sref = src.at[(*full_, ds128(2 * T * (1 - c), 2 * T))]
        dref = dst.at[(*full_, pl.ds(0, 2 * T), ds128(HALF * c, HALF))]
        return rcopy(sref, dref, i0, i0, (other, z))

    def from_heads_a_own(kind, src, dst, lid):
        full_ = [slice(None)] * (len(src.shape) - 2)
        sref = src.at[(*full_, ds128(2 * T * c, 2 * T))]
        dref = dst.at[(*full_, pl.ds(0, 2 * T), ds128(HALF * c, HALF))]
        return pltpu.make_async_copy(sref, dref, rs.at[lid])

    def from_heads_b(kind, src, j0, k):
        _, rid, sid = EX[kind]
        t = lax.rem(g + k, 4)
        n = src.shape[0]
        sref = src.at[:, ds128(T * t, T)]
        dref = fromb.at[g, pl.ds(0, n)]
        return rcopy(sref, dref, sid + k, rid + k, dev_of(t))

    def from_heads_b_own(src, lid):
        n = src.shape[0]
        return pltpu.make_async_copy(src.at[:, ds128(T * g, T)], fromb.at[g, pl.ds(0, n)], rs.at[lid])

    def wait_a(kind, dst, heads):
        full_ = [slice(None)] * (len(dst.shape) - 2)
        if heads:
            dref = dst.at[(*full_, ds128(2 * T * (1 - c), 2 * T))]
        else:
            dref = dst.at[(*full_, pl.ds(0, 2 * T), ds128(HALF * (1 - c), HALF))]
        recv(dref, EX[kind][0])

    def wait_b_heads(kind, dst):
        full_ = [slice(None)] * (len(dst.shape) - 2)
        for k in (1, 2, 3):
            recv(dst.at[(*full_, ds128(T * lax.rem(g + 4 - k, 4), T))], EX[kind][1] + k)

    def wait_b_tokens(kind, n):
        for k in (1, 2, 3):
            recv(fromb.at[lax.rem(g + 4 - k, 4), pl.ds(0, n)], EX[kind][1] + k)

    def merge_b(dst, j, n_from):
        for q in range(2):
            lo, hi = fromb[2 * q, n_from], fromb[2 * q + 1, n_from]
            at = q * HALF
            dst[j, 2 * T : 3 * T, at : at + 128] = lo[:, 0:128]
            dst[j, 2 * T : 3 * T, at + 128 : at + 256] = jnp.where(lane < 64, lo[:, 128:256], hi[:, 0:128])
            dst[j, 2 * T : 3 * T, at + 256 : at + 384] = hi[:, 128:256]

    for m in range(3):
        move_out_done(m, att.at[0, pl.ds(m * T, T)], rows, S_ROWS, I_ROWS)
    project(2)
    xb = [to_heads_b("qkv", qkv, qkvb, k) for k in (1, 2, 3)]
    for d in xb:
        d.start()
    lb = to_heads_b_own("qkv", qkv, qkvb, L0 + 1)
    lb.start()

    @pl.loop(0, 2)
    def _(s):
        project(s)

    xa = to_heads_a("qkv", qkv, qkva)
    xa.start()
    la = to_heads_a_own("qkv", qkv, qkva, L0)
    la.start()

    def weights_ready(step):
        if not aligned:
            return
        if step == 0:
            for a in (U_, O_):
                ag2(a)
            send_cot((2,))
        elif step == 2:
            z_wait("D", 3)
            unflatten(D_, dp)
            ag1(D_)
        elif step == 3:
            ag2(D_)
        elif step == 4:
            for a in (U_, O_):
                ag3(a)
        elif step == 5:
            send_cot((0, 1))
            for a in (U_, O_):
                ag4(a)
            ag3(D_)
        elif step == 6:
            ag4(D_)
            for key in CH:
                for k in (1, 2, 3):
                    z_send(key, k, done=True)

    def key_bias(slot):
        parts = []
        at = lax.broadcasted_iota(i32, (T, 128), 0).astype(f32)
        for b in range(4):
            limit = cnt[slot, b : b + 1, :].astype(f32)
            parts.append(jnp.where(at < limit, 0.0, NEG))
        return jnp.concatenate(parts, axis=0).astype(bf16)

    bias = R["bias"]
    bias[0] = key_bias(0)
    bias[1] = key_bias(2)
    QT = 256
    N = 4 * T

    def half(i, x):
        return jnp.where(lane // 64 == i, x, jnp.zeros_like(x))

    def key_side(k2, b, i):
        spot = 64 * (1 - i)
        return jnp.where(lane // 64 == i, k2, jnp.where(lane == spot, b, jnp.zeros_like(b)))

    def query_side(q2, i):
        spot = 64 * (1 - i)
        return jnp.where(lane // 64 == i, q2, jnp.where(lane == spot, 1.0, 0.0).astype(bf16))

    SC = 0.125 * LOG2E

    def attend(src, dst, col, bi, sel, lrow):
        cols = ds128(col, 128)
        k2 = src[1, :, cols]
        b = bias[bi]
        keys = [key_side(k2, b, i) for i in sel]

        @pl.loop(0, N // QT)
        def _(q):
            r = ds128(q * QT, QT)
            q2 = src[0, r, cols]
            v2 = src[2, :, cols]
            outs = []
            for n, i in enumerate(sel):
                s = nt(query_side(q2, i), keys[n])
                top = jnp.max(s, axis=1, keepdims=True) * SC
                p = jnp.exp2(s * SC - top)
                total = jnp.sum(p, axis=1, keepdims=True)
                outs.append(nn(p.astype(bf16), v2) / total)
                full_total = jnp.broadcast_to(top + jnp.log2(total), (QT, 128)).T
                lse[pl.ds(lrow + n, 1), r] = full_total[0:1, :]
            if len(sel) == 2:
                o = jnp.where(lane < 64, outs[0], outs[1])
            else:
                o = jnp.where(lane // 64 == sel[0], outs[0], 0.0)
            dst[0, r, cols] = o.astype(bf16)

    weights_ready(2)
    la.wait()
    wait_a("qkv", qkva, True)

    for t in range(2):
        attend(qkva, atta, t * 128, 0, (0, 1), 2 * t)
        if t == 0:
            weights_ready(0)
    lb.wait()
    wait_b_heads("qkv", qkvb)
    attend(qkvb, attb, c * 128, 1, (0, 1), 6)
    weights_ready(3)
    attend(qkvb, attb, (1 - c) * 128, 1, (c,), 8)
    xattb = [from_heads_b("att", attb, 0, k) for k in (1, 2, 3)]
    for d in xattb:
        d.start()
    lattb = from_heads_b_own(attb, L0 + 3)
    lattb.start()
    weights_ready(4)
    attend(qkva, atta, 256, 0, (0, 1), 4)
    xatt = from_heads_a("att", atta, att)
    xatt.start()
    latt = from_heads_a_own("att", atta, att, L0 + 2)
    latt.start()
    weights_ready(5)
    xa.wait_send()
    for d in xb:
        d.wait_send()
    latt.wait()
    wait_a("att", att, False)

    def slot_rows(s):
        return pl.ds(mult(s * T, T), T)

    def live_of(s):
        b = 2 * c + s if s < 2 else g
        at = lax.broadcasted_iota(i32, (T, 128), 0).astype(f32)
        pick = jnp.zeros((1, 128), f32)
        for i in range(4):
            pick = pick + jnp.where(b == i, cnt[s, i : i + 1, :].astype(f32), 0.0)
        return jnp.where(at < pick, 1.0, 0.0)[:, 0:1]

    for s in range(3):
        if s == 2:
            lattb.wait()
            wait_b_tokens("att", 1)
            merge_b(att, 0, 0)
        r = pl.ds(s * T, T)
        v = nn(att[0, r, :], wblock(R["wo"])) + vec(V_OB) + rows[s].astype(f32)
        mid[r, :] = v
        n, _ = normalise(v)
        nbuf[s] = (n * vec(V_MG) + vec(V_MS)).astype(bf16)
    weights_ready(6)
    FT = FR

    ub = R["ub"]
    outer = branch = cot

    def hidden(s, up, j):
        hid = nn(nbuf[s], up) + ub[pl.ds(j, 1), :]
        phi_c = 0.5 * (1.0 + lax.erf(hid * 0.7071067811865476))
        return hid, phi_c

    def outer_rows():
        for s in (2, 0, 1):
            recv(cot.at[s], I_COT + s)
            o = live_of(s) * cot[s].astype(f32)
            cot[s] = o.astype(bf16)
            part = col_sum(o)
            if s == 2:
                vg[V_DB : V_DB + 1, :] = part
            else:
                vg[V_DB : V_DB + 1, :] += part

    def feed(acc, n2t, tile):
        act_s, gh_s = tile.at[0], tile.at[1]
        for s in range(3):
            n2t[:, s * T : (s + 1) * T] = nbuf[s].T
            acc[s * T : (s + 1) * T, :] = mid[s * T : (s + 1) * T, :] + vec(V_DB)

        @pl.loop(0, dps)
        def _(j):
            up = wblock(R["wu"], ds128(j * FT, FT))
            down = R["wd"][j]

            @pl.loop(0, 3)
            def _(s):
                hid, phi_c = hidden(s, up, j)
                acc[slot_rows(s), :] += nn((hid * phi_c).astype(bf16), down)

        for s in (2, 0, 1):
            r = pl.ds(s * T, T)
            ysend[s] = (live_of(s) * acc[r, :]).astype(bf16)
            move_home(s, ysend.at[s], act, S_ACT, I_ACT)
            acc[r, :] = jnp.zeros((T, W), f32)
        outer_rows()

        def tile_pair(i):
            @pl.loop(2 * i, 2 * i + 2)
            def _(j):
                one_tile(j)

        def one_tile(j):
            cols = ds128(j * FT, FT)
            up = wblock(R["wu"], cols)
            down = R["wd"][j]

            @pl.loop(0, 3, init_carry=jnp.zeros((1, FT), f32))
            def bias_part(s, carry):
                r = slot_rows(s)
                hid, phi_c = hidden(s, up, j)
                act_s[r, :] = (hid * phi_c).astype(bf16)
                slope = phi_c + hid * jnp.exp2(hid * hid * (-0.5 * LOG2E)) * 0.3989422804014327
                gh = (nt(outer[s], down) * slope).astype(bf16)
                gh_s[r, :] = gh
                acc[r, :] += nt(gh, up)
                return carry + col_sum(gh.astype(f32))

            ub[pl.ds(j, 1), :] = bias_part
            R["wd"][j] = tn(act_s[...], outer[...].reshape(3 * T, W)).astype(bf16)
            R["wu"][:, :, cols] = nn(n2t[...], gh_s[...]).astype(bf16).reshape(dps, KR, FT)

        for i in range(dps // 2):
            tile_pair(i)
            if aligned:
                rs_core("D", i).start()
                if i == 1 or i == 3:
                    rs1("U%d" % (i // 2))
                if i > 0:
                    rs2_pair("D", i - 1)
                if i == 2:
                    rs2("U0")
                if i == 3:
                    rs3("U0")

        for s in (2, 0, 1):
            r = pl.ds(s * T, T)
            n, inv = normalise(mid[r, :])
            e_ = acc[r, :]
            gm = outer[s].astype(f32) + norm_back(e_, n, inv, vec(V_MG))
            mid[r, :] = gm
            low = gm.astype(bf16)
            branch[s] = low
            for i, part in ((V_MG, col_sum(e_ * n)), (V_MS, col_sum(e_)), (V_OB, col_sum(low.astype(f32)))):
                if s == 2:
                    vg[i : i + 1, :] = part
                else:
                    vg[i : i + 1, :] += part
            nbuf[s] = nt(low, wblock(R["wo"])).astype(bf16)
            send_do(s)
        for q in range(2):
            piece = tn(att[0, :, q * HALF : (q + 1) * HALF], branch[...].reshape(3 * T, W)).astype(bf16)
            R["wo"][q * (dps // 2) : (q + 1) * (dps // 2)] = piece.reshape(dps // 2, KR, W)
        grads_move(0)

    def act_done():
        for s in range(3):
            move_home_done(s, ysend.at[s], act, S_ACT, I_ACT)

    do3 = R["nbuf"]

    def do_copies(s):
        if s < 2:
            i0 = EX["do"][0] if s == 0 else L0 + 4
            return [rcopy(do3.at[s, :, ds128(HALF * (1 - c), HALF)], doa.at[ds128(2 * T * c + s * T, T)], i0, i0, (other, z))]
        out = []
        for k in (1, 2, 3):
            t = lax.rem(g + k, 4)
            cols = ds128(HALF * lax.div(t, 2) + 128 * lax.rem(t, 2), 256)
            out.append(rcopy(do3.at[2, :, cols], dob.at[ds128(T * g, T)], EX["do"][2] + k, EX["do"][1] + k, dev_of(t)))
        return out

    def send_do(s):
        for d in do_copies(s):
            d.start()

    def grads_move(step):
        if not aligned:
            return
        if step == 0:
            rs1("O")
            rs2_pair("D", 3)
            rs2("U1")
        elif step == 1:
            rs2("O")
            rs4("U0")
        elif step == 2:
            rs3("D")
        elif step == 3:
            y_send("U0", 2)
            rs3("U1")
            rs3("O")
        elif step == 4:
            rs4("D")
            rs4("U1")
            rs4("O")
        elif step == 5:
            y_send("U0", 3)
            y_send("D", 2)
            y_send("U1", 2)
            y_send("O", 2)
        elif step == 6:
            y_send("U1", 3)
            y_final("U0")
        elif step == 7:
            y_send("D", 3)
            y_send("O", 3)
            y_final("U1")
        elif step == 8:
            y_final("D")
            y_final("O")

    per = W // FT
    for q in range(dps):
        R["ub"][q : q + 1, :] = vt[V_UB + q // per : V_UB + q // per + 1, (q % per) * FT : (q % per + 1) * FT]
    pl.run_scoped(
        feed,
        pltpu.VMEM((3 * T, W), f32),
        pltpu.VMEM((W, 3 * T), bf16),
        pltpu.VMEM((2, 3 * T, FT), bf16),
    )
    for q in range(dps):
        vg[V_UB + q // per : V_UB + q // per + 1, (q % per) * FT : (q % per + 1) * FT] = R["ub"][q : q + 1, :]

    for j in range(2):
        doa[ds128(2 * T * c + j * T, T), :] = do3[j, :, ds128(HALF * c, HALF)]
    dob[ds128(T * g, T), :] = do3[2, :, ds128(HALF * e + 128 * c, 256)]

    def attend_back(src, o_ref, d_ref, col, bi, sel, lrow, dk, dv, delta):
        cols = ds128(col, 128)
        k2 = src[1, :, cols]
        v2 = src[2, :, cols]
        kt = k2.T
        b = bias[bi]
        keys = [key_side(k2, b, i) for i in sel]
        dk[...] = jnp.zeros_like(dk)
        dv[...] = jnp.zeros_like(dv)
        prod = o_ref[0, :, cols].astype(f32) * d_ref[:, cols].astype(f32)
        hi = prod.astype(bf16)
        lo = (prod - hi.astype(f32)).astype(bf16)
        row = lax.broadcasted_iota(i32, (8, 128), 0)
        if len(sel) == 2:
            pickm = (row == lax.broadcasted_iota(i32, (8, 128), 1) // 64).astype(f32).astype(bf16)
        else:
            pickm = jnp.where(jnp.logical_and(row == 0, lane // 64 == sel[0]), 1.0, 0.0).astype(bf16)
        delta[...] = nt(pickm, hi) + nt(pickm, lo)

        @pl.loop(0, N // QT)
        def _(q):
            r = ds128(q * QT, QT)
            q2 = src[0, r, cols]
            d2 = d_ref[r, cols]
            dks, dvs, dqs = [], [], []
            for n, i in enumerate(sel):
                qm, dm = half(i, q2), half(i, d2)
                s = nt(keys[n], query_side(q2, i))
                p = jnp.exp2(s * SC - lse[pl.ds(lrow + n, 1), r])
                dp_ = nt(v2, dm)
                ds_ = (p * (dp_ - delta[pl.ds(n, 1), r])).astype(bf16)
                dvs.append(nn(p.astype(bf16), dm))
                dks.append(nn(ds_, qm))
                dqs.append(nn(kt, ds_).T if len(sel) == 1 else nn(kt[64 * i : 64 * i + 64], ds_))
            if len(sel) == 2:
                dk[...] += dks[0] + dks[1]
                dv[...] += dvs[0] + dvs[1]
                dq = jnp.concatenate(dqs, axis=0).T
            else:
                dk[...] += dks[0]
                dv[...] += dvs[0]
                dq = half(sel[0], dqs[0])
            src[0, r, cols] = (dq * 0.125).astype(bf16)

        src[1, :, cols] = (dk[...] * 0.125).astype(bf16)
        src[2, :, cols] = dv[...].astype(bf16)

    I_DQA = take(6)

    def dq_copy(t):
        sref = qkva.at[:, ds128(2 * T * (1 - c), 2 * T), pl.ds(t * 128, 128)]
        dref = qkv.at[:, pl.ds(0, 2 * T), ds128(HALF * c + t * 128, 128)]
        return rcopy(sref, dref, I_DQA + t, I_DQA + t, (other, z))

    def dq_own(t):
        sref = qkva.at[:, ds128(2 * T * c, 2 * T), pl.ds(t * 128, 128)]
        dref = qkv.at[:, pl.ds(0, 2 * T), ds128(HALF * c + t * 128, 128)]
        return pltpu.make_async_copy(sref, dref, rs.at[I_DQA + 3 + t])

    def strips(t, r):
        return jnp.concatenate([qkv[j, r, k * HALF + t * 128 : k * HALF + (t + 1) * 128] for j in range(3) for k in range(2)], axis=1)

    gsend = cot
    if aligned:
        vx = R["vx"]
        I_VEC = take(3)
        I_VEZ = take(4)
        pairs = (other, dp + dx, dp + dy)

    def vec_copy(i):
        return rcopy(vg, vx.at[i], I_VEC + i, I_VEC + i, (pairs[i], z))

    def vec_add(i):
        vec_copy(i).wait()
        vg[...] += vx[i]

    def vec_z(k):
        return rcopy(vg, vx.at[2 + k], I_VEZ + k, I_VEZ + k, (dp, lax.rem(z + k, 4)))

    def rows_back(s, e_):
        r = pl.ds(s * T, T)
        n, inv = normalise(rows[s].astype(f32))
        gsend[s] = (mid[r, :] + norm_back(e_, n, inv, vec(V_NG))).astype(bf16)
        move_home(s, gsend.at[s], grh, S_GR, I_GR)
        parts = (
            (V_NG, col_sum(e_ * n)),
            (V_NS, col_sum(e_)),
            (V_QB, col_sum(qkv[0, r, :].astype(f32))),
            (V_VB, col_sum(qkv[2, r, :].astype(f32))),
        )
        for i, part in parts:
            if s == 2:
                vg[i : i + 1, :] = part
            else:
                vg[i : i + 1, :] += part

    def close_group(t, ebuf):
        dq_own(t).wait()
        recv(qkv.at[:, pl.ds(0, 2 * T), ds128(HALF * (1 - c) + t * 128, 128)], I_DQA + t)
        for s in range(2):
            part = nt(strips(t, pl.ds(s * T, T)), group(t))
            if t == 0:
                ebuf[s] = part
            else:
                ebuf[s] += part
        w = tn(nbuf[...].reshape(3 * T, W), strips(t, pl.ds(0, 3 * T))).astype(bf16)
        R["wq"][:, :, t * W : (t + 1) * W] = w.reshape(dps, KR, W)
        if aligned:
            rs1("Q%d" % t)

    def back(dk, dv, delta, ebuf):
        for k in (1, 2, 3):
            recv(dob.at[ds128(T * lax.rem(g + 4 - k, 4), T)], EX["do"][1] + k)
        attend_back(qkvb, attb, dob, c * 128, 1, (0, 1), 6, dk, dv, delta)
        grads_move(1)
        attend_back(qkvb, attb, dob, (1 - c) * 128, 1, (c,), 8, dk, dv, delta)
        for d in xattb:
            d.wait_send()
        for k in (1, 2, 3):
            from_heads_b("dqkv", qkvb, 0, k).start()
        from_heads_b_own(qkvb, L0 + 6).start()
        grads_move(2)
        recv(doa.at[ds128(2 * T * (1 - c), T)], EX["do"][0])
        recv(doa.at[ds128(2 * T * (1 - c) + T, T)], L0 + 4)
        attend_back(qkva, atta, doa, 0, 0, (0, 1), 0, dk, dv, delta)
        dq_copy(0).start()
        dq_own(0).start()
        grads_move(3)
        for s in range(3):
            for d in do_copies(s):
                d.wait_send()
        for s in range(3):
            normed_rows(s)
        for m in range(3):
            move_out_done(m, R["cnth"].at[m], cnt, S_CNT, I_CNT)
            move_out_done(m, R["cotangent"].at[m], cot, S_COT, I_COT)
        attend_back(qkva, atta, doa, 128, 0, (0, 1), 2, dk, dv, delta)
        dq_copy(1).start()
        dq_own(1).start()
        grads_move(4)
        from_heads_b_own(qkvb, L0 + 6).wait()
        wait_b_tokens("dqkv", 3)
        for j in range(3):
            merge_b(qkv, j, j)
        r = pl.ds(2 * T, T)
        e_ = nt(strips(0, r), group(0)) + nt(strips(1, r), group(1)) + nt(strips(2, r), group(2))
        rows_back(2, e_)
        close_group(0, ebuf)
        grads_move(5)
        attend_back(qkva, atta, doa, 256, 0, (0, 1), 4, dk, dv, delta)
        dq_copy(2).start()
        dq_own(2).start()
        close_group(1, ebuf)
        if aligned:
            rs2("Q0")
        close_group(2, ebuf)
        grads_move(6)
        rows_back(0, ebuf[0])
        if aligned:
            rs3("Q0")
            rs2("Q1")
        rows_back(1, ebuf[1])
        vg[12:16, :] = jnp.zeros((4, W), f32)
        if aligned:
            vec_copy(0).start()
            rs2("Q2")
            rs4("Q0")
            rs3("Q1")
            grads_move(7)
            vec_add(0)
            vec_copy(1).start()
            rs3("Q2")
            rs4("Q1")
            y_send("Q0", 2)
            vec_add(1)
            vec_copy(2).start()
            rs4("Q2")
            y_send("Q1", 2)
            y_send("Q0", 3)
            vec_add(2)
            for k in (1, 2, 3):
                vec_z(k).start()
            grads_move(8)
            y_send("Q2", 2)
            y_send("Q1", 3)
            y_final("Q0")
            y_send("Q2", 3)
            y_final("Q1")
            for k in (1, 2, 3):
                recv(vx.at[2 + k], I_VEZ + k)
            for k in (1, 2, 3):
                vec_z(k).wait_send()
            total = vg[...]
            for k in (1, 2, 3):
                total = total + vx[2 + k]
            at = dp * 4 + z
            n1, n2 = W // 32, F // 32
            R["vs"][...] = pltpu.roll(total, lax.rem(W - at * n1, W), axis=1)[:, 0:128]
            line = lax.broadcasted_iota(i32, (16, W), 0)
            per_row = W // n2
            ubr = jnp.sum(jnp.where(line == V_UB + lax.div(at, per_row), total, 0.0), axis=0, keepdims=True)
            ubr = jnp.broadcast_to(ubr, (8, W))
            R["vs"][8:16, :] = pltpu.roll(ubr, lax.rem(W - lax.rem(at, per_row) * n2, W), axis=1)[:, 0:128]
            y_final("Q2")
            for key in GC:
                rs_done(key)

    pl.run_scoped(back, pltpu.VMEM((N, 128), f32), pltpu.VMEM((N, 128), f32), pltpu.VMEM((8, N), f32), pltpu.VMEM((2, T, W), f32))
    xatt.wait_send()
    if not aligned:
        save = [pltpu.make_async_copy(arrays[i], R[n], rs.at[L0 + 8 + i]) for i, n in enumerate(("gq", "go", "gu", "gd"))]
        for d in save:
            d.start()
        for d in save:
            d.wait()
    for t in range(3):
        dq_copy(t).wait_send()
    for k in (1, 2, 3):
        from_heads_b("dqkv", qkvb, 0, k).wait_send()
    act_done()
    for s in range(3):
        move_home_done(s, gsend.at[s], grh, S_GR, I_GR)
    for m in range(3):
        arrived_home(m, act, I_ACT)
        arrived_home(m, grh, I_GR)
    assert count[0] <= cfg["sems"], count[0]


def finish_kernel(sizes, keep, grads, act_in, *refs):
    n = 0 if sizes is None else 5
    act_out, out = refs[n], refs[n + 1]
    places = lax.broadcasted_iota(i32, (out.shape[1], keep.shape[2]), 0)
    out[0] = nn((places == keep[0]).astype(f32).astype(bf16), grads[0])
    act_out[...] = act_in[...]
    if sizes is not None:

        @pl.when(pl.program_id(0) == 0)
        def _():
            for i in range(4):
                refs[n + 2 + i][...] = refs[i][...]
            for i, width in enumerate(sizes):
                refs[n + 6 + i][...] = refs[4][i : i + 1, 0:width]


def body(patches, keep_index, shard_counts, cotangent, *shards):
    ng, ns, wq, qb, vb, wo, ob, mg, ms, wu, ub, wd, db = shards
    batches, _, patch, width = patches.shape
    tokens = keep_index.shape[2]
    dp_size, blk_size = lax.axis_size("dp"), lax.axis_size("blk")
    devices = dp_size * blk_size
    ff = wu.shape[1]
    aligned = dp_size == 8 and blk_size == 4
    dps = 8
    kr, fr = width // dps, ff // dps
    vectors = jnp.stack([ng, ns, qb, vb, ob, mg, ms, db])
    if aligned:
        own = jnp.pad(vectors, ((0, 0), (0, 128 - vectors.shape[1])))
        own_ub = jnp.pad(ub[None], ((0, 7), (0, 128 - ub.shape[0])))
        table = jnp.concatenate([own, own_ub])
        weights = (wq, wo, wu, wd)
        pieces = [w.size // 128 for w in weights] + [16]
        flat = [sum(pieces[:i]) for i in range(6)]
    else:
        axes = ("dp", "blk")
        table = lax.all_gather(vectors, axes, axis=1, tiled=True).astype(f32)
        table_ub = lax.all_gather(ub, axes, axis=0, tiled=True).astype(f32).reshape(ff // width, width)
        table = jnp.concatenate([table, table_ub, jnp.zeros((16 - 8 - ff // width, width), f32)])
        weights = tuple(lax.all_gather(w, axes, axis=0, tiled=True) for w in (wq, wo, wu, wd))
        weights = tuple(w.reshape(dps, -1, w.shape[1]) for w in weights)
        held = weights[0].reshape(dps, kr, 3, 2, 3, width // 6).transpose(0, 1, 4, 2, 3, 5).reshape(dps, kr, 3 * width)
        weights = (held, *weights[1:])
        flat = None
    cfg = dict(aligned=aligned, dps=dps, tokens=tokens, width=width, ff=ff, patch=patch, flat=flat, sems=320)
    keep = keep_index
    ins = [
        ("patches", patches[:, 0], ANY),
        ("keep", keep, VMEM),
        ("counts", shard_counts, SMEM),
        ("cotangent", cotangent[:, 0], ANY),
    ]
    ins += [(n, w, VMEM if aligned else ANY) for n, w in zip(("sq", "so", "su", "sd"), weights)]
    ins.append(("sv", table, VMEM))
    out = [
        ("act", (3, tokens, width), bf16, ANY),
        ("grh", (3, tokens, width), bf16, ANY),
        ("vg", (16, width), f32, VMEM),
    ]
    full = {"q": (dps, kr, 3 * width), "o": (dps, kr, width), "u": (dps, kr, ff), "d": (dps, fr, width)}
    for i, n in enumerate("qoud"):
        if aligned:
            out.append(("g" + n, weights[i].shape, f32, VMEM))
        else:
            out.append(("g" + n, full[n], bf16, ANY))
    if aligned:
        out.append(("vs", (16, 128), f32, VMEM))
    t3 = 3 * tokens
    scratch = [("w" + n, full[n], bf16) for n in "qoud"]
    scratch += [
        ("rows", (3, tokens, width), bf16),
        ("cot", (3, tokens, width), bf16),
        ("cnt", (3, 16, 128), bf16),
        ("cnth", (3, 16, 128), bf16),
        ("nbuf", (3, tokens, width), bf16),
        ("qkv", (3, t3, width), bf16),
        ("qkva", (3, 4 * tokens, width // 2), bf16),
        ("qkvb", (3, 4 * tokens, 256), bf16),
        ("atta", (1, 4 * tokens, width // 2), bf16),
        ("attb", (1, 4 * tokens, 256), bf16),
        ("att", (1, t3, width), bf16),
        ("fromb", (4, 3, tokens, 256), bf16),
        ("doa", (4 * tokens, width // 2), bf16),
        ("dob", (4 * tokens, 256), bf16),
        ("mid", (t3, width), f32),
        ("ysend", (3, tokens, width), bf16),
        ("vt", (16, width), f32),
        ("lse", (16, 4 * tokens), f32),
        ("bias", (2, 4 * tokens, 128), bf16),
        ("ub", (dps, fr), f32),
    ]
    if aligned:
        scratch += [
            ("zbuf", (4, flat[5], 128), bf16),
            ("zrr", (3, flat[4], 128), bf16),
            ("zrl", (3, flat[4], 128), bf16),
            ("vw", (dps, 64, 128), bf16),
            ("vx", (6, 16, width), f32),
        ]
        scratch += [("rb1" + n, (4, *full[n][1:]), bf16) for n in "qoud"]
        scratch += [("rb2" + n, (3, *full[n][1:]), bf16) for n in "qoud"]
    names = [n for n, _, _ in scratch] + ["ss", "rs"]
    shapes = [pltpu.VMEM(s, d) for _, s, d in scratch] + [pltpu.SemaphoreType.DMA((cfg["sems"],))] * 2
    flops = 6 * 3 * tokens * (4 * width * width + 2 * width * ff)
    results = pl.pallas_call(
        functools.partial(layer_kernel, cfg, [n for n, _, _ in ins], [n for n, *_ in out], names),
        out_shape=[jax.ShapeDtypeStruct(s, d) for _, s, d, _ in out],
        in_specs=[s for _, _, s in ins],
        out_specs=[s for *_, s in out],
        scratch_shapes=shapes,
        compiler_params=pltpu.CompilerParams(collective_id=0, has_side_effects=True, vmem_limit_bytes=64 * 1024 * 1024 - 512 * 1024),
        cost_estimate=pl.CostEstimate(flops=flops, bytes_accessed=50_000_000, transcendentals=0),
        name="layer",
    )(*[a for _, a, _ in ins])
    act, grh, vg, gq, go, gu, gd = results[:7]
    whole = lambda v: pl.BlockSpec(v, lambda m: (0,) * len(v))
    step = lambda *v: pl.BlockSpec((1, *v), lambda m: (m, 0, 0))
    n = width // devices
    sizes = [n] * 8 + [ff // devices] if aligned else None
    extra = [gq, go, gu, gd, results[7]] if aligned else []
    shapes = [(3, tokens, width, bf16), (3, patch, width, f32)]
    specs = [step(tokens, width), step(patch, width)]
    if aligned:
        shapes += [(*v.shape, f32) for v in extra[:4]] + [(1, v, f32) for v in sizes]
        specs += [whole(v.shape) for v in extra[:4]] + [whole((1, v)) for v in sizes]
    done = pl.pallas_call(
        functools.partial(finish_kernel, sizes),
        grid=(3,),
        in_specs=[step(1, tokens), step(tokens, width), step(tokens, width)] + [whole(v.shape) for v in extra],
        out_specs=specs,
        out_shape=[jax.ShapeDtypeStruct(v[:-1], v[-1]) for v in shapes],
        compiler_params=pltpu.CompilerParams(vmem_limit_bytes=64 * 1024 * 1024 - 512 * 1024),
        name="finish",
    )(keep, grh, act, *extra)
    act, patch_grad = done[:2]
    if aligned:
        gq, go, gu, gd = done[2:6]
        piece = [v.reshape(-1) for v in done[6:]]
    else:
        axes = ("dp", "blk")
        small = [vg[:8].reshape(8, devices, n).transpose(1, 0, 2).reshape(devices, -1), vg[8 : 8 + ff // width].reshape(devices, -1)]
        small = lax.psum_scatter(jnp.concatenate(small, axis=1), axes, scatter_dimension=0, tiled=True)[0]
        piece = [small[i * n : (i + 1) * n] for i in range(8)] + [small[8 * n :]]
        gq = gq.reshape(dps, kr, 3, 3, 2, width // 6).transpose(0, 1, 3, 4, 2, 5).reshape(dps, kr, 3 * width)
        gq, go, gu, gd = (
            lax.psum_scatter(w.reshape(-1, w.shape[-1]).astype(f32), axes, scatter_dimension=0, tiled=True) for w in (gq, go, gu, gd)
        )
    return (
        act[:, None],
        patch_grad[:, None],
        piece[V_NG],
        piece[V_NS],
        gq,
        piece[V_QB],
        piece[V_VB],
        go,
        piece[V_OB],
        piece[V_MG],
        piece[V_MS],
        gu,
        piece[V_UB],
        gd,
        piece[V_DB],
    )


def solution(mesh):
    vec, mat = P(("dp", "blk")), P(("dp", "blk"), None)
    tok = P(None, "dp", "blk", None)
    params = (vec, vec, mat, vec, vec, mat, vec, vec, vec, mat, vec, mat, vec)
    in_specs = (tok, P(None, "dp", "blk"), P(None, "dp", None), tok) + params
    out_specs = (tok, tok) + params
    return jax.shard_map(body, mesh=mesh, in_specs=in_specs, out_specs=out_specs, check_vma=False)
```
